128 devices in a mesh: dp: 2 (over core), row: 4 (over x), col: 16 (over z, y).
Axes of the slice: x: 4, y: 4, z: 4, core: 2. Of those that a mesh axis runs over, the one named last changes fastest.
Arguments:
- inputs: bfloat16 [768, 16384], P('col', ('dp', 'row')), may hold values from -6 to 6
- segments: int32 [2, 8192], P('dp'), may hold values from 0 to 4, as said below
- joint_weight: bfloat16 [768, 2304], P('col', 'row'), may hold values from -0.21875 to 0.21875
- joint_bias: float32 [1536], P('row'), may hold values from -1.8 to 1.8
- output_weight: bfloat16 [768, 768], P('row', 'col'), may hold values from -6 to 6
- output_bias: float32 [768], P('col'), may hold values from -1.8 to 1.8
- first_norm_gain: float32 [768], P('col'), may hold values from 0.5 to 1.5
- shift_first: float32 [768], P('col'), may hold values from -1.8 to 1.8
- up_weight: bfloat16 [768, 3072], P('col', 'row'), may hold values from -0.21875 to 0.21875
- up_bias: float32 [3072], P('row'), may hold values from -1.8 to 1.8
- down_weight: bfloat16 [768, 3072], P('col', 'row'), may hold values from -0.109375 to 0.109375
- down_bias: float32 [768], P('col'), may hold values from -1.8 to 1.8
- second_norm_gain: float32 [768], P('col'), may hold values from 0.5 to 1.5
- second_norm_shift: float32 [768], P('col'), may hold values from -1.8 to 1.8
- cotangent: bfloat16 [768, 16384], P('col', ('dp', 'row')), may hold values from -6 to 6
Outputs:
- layer_output: bfloat16 [768, 16384], P('col', ('dp', 'row'))
- grad_inputs: float32 [768, 16384], P('col', ('dp', 'row'))
- grad_joint_weight: float32 [768, 2304], P('col', 'row')
- grad_joint_bias: float32 [1536], P('row')
- grad_output_weight: float32 [768, 768], P('row', 'col')
- grad_output_bias: float32 [768], P('col')
- grad_gain_first: float32 [768], P('col')
- grad_shift_first: float32 [768], P('col')
- grad_up_weight: float32 [768, 3072], P('col', 'row')
- grad_up_bias: float32 [3072], P('row')
- grad_down_weight: float32 [768, 3072], P('col', 'row')
- grad_down_bias: float32 [768], P('col')
- grad_gain_second: float32 [768], P('col')
- grad_shift_second: float32 [768], P('col')
The draws below stay inside these ranges and needn't reach their ends.
Inputs may be any that keep to these rules, and one draw needn't show every extreme that they name: `segments`: in every sequence the segment numbers start at 0, rise by 0 or 1 from one token to the next, and end at 4.
All inputs are finite; a program needn't handle non-finite values.
Results may differ from the reference program's by a relative error of at most 0.019.
Values may be sent and summed in bfloat16 or wider, within the bound.
No kernel may reach another device: no remote copies, remote signals or barrier semaphores. Data moves between devices by JAX's collectives and lax.ppermute only.
A program may use at most 128 MiB of HBM per device.

```python
import math
from functools import partial
import jax
import jax.numpy as jnp
from jax import lax

D = 768
HEADS = 12
HDIM = 64
FF = 3072
SEQ = 8192
QBLK = 512
SEQS = 2
TOKENS = 16384


def draw_segments(key, part):
    key_begin, key_finish = jax.random.split(key, 2)
    begin = jax.random.randint(key_begin, (SEQS, 1), 2, QBLK)
    finish = jax.random.randint(key_finish, (SEQS, 1), SEQ - QBLK + 1, SEQ - 1)
    places = jnp.arange(SEQ, dtype=jnp.int32)[None, :]
    early = begin // 2
    late = (finish + SEQ) // 2
    starts = (places == early) | (places == begin) | (places == finish) | (places == late)
    return jnp.cumsum(starts.astype(jnp.int32), axis=1).astype(jnp.int32)


def shard_levels(stream_key, dims, cuts, smallest, largest):
    def one(axis_at, blocks):
        draws = jax.random.uniform(jax.random.fold_in(jax.random.fold_in(stream_key, 6), axis_at), (blocks,), jnp.float32, smallest / len(cuts), largest / len(cuts))
        return jnp.repeat(jnp.exp(draws), dims[axis_at] // blocks).reshape((-1,) + (1,) * (len(dims) - axis_at - 1))

    level = one(*cuts[0])
    for cut in cuts[1:]:
        level = level * one(*cut)
    return level


def normal_values(stream_key, extent, scale, reach, cuts=(), kind=jnp.bfloat16):
    loudness = shard_levels(stream_key, extent, cuts, -0.22, 0.18) if cuts else 1.0
    drawn = jax.random.normal(stream_key, extent, jnp.float32) * scale * loudness
    return jnp.minimum(jnp.maximum(drawn, -reach), reach).astype(kind)


def setup_inputs(seed: int = 0) -> dict:
    key_of = jax.random.split(jax.random.key(seed), 16)
    return {
        "inputs": normal_values(key_of[0], (D, TOKENS), 1.0, 6.0, ((0, 16), (1, 8))),
        "segments": draw_segments(jax.random.fold_in(key_of[15], 71), 0),
        "joint_weight": normal_values(key_of[2], (D, 3 * D), D ** -0.5, 0.21875, ((0, 16), (1, 4))),
        "joint_bias": normal_values(key_of[3], (2 * D,), 0.3, 1.8, ((0, 4),), jnp.float32),
        "output_weight": normal_values(key_of[4], (D, D), 1.0, 6.0, ((0, 4), (1, 16))),
        "output_bias": normal_values(key_of[5], (D,), 0.3, 1.8, ((0, 16),), jnp.float32),
        "first_norm_gain": jnp.clip(1.0 + 0.1 * jax.random.normal(key_of[6], (D,), jnp.float32), 0.5, 1.5),
        "shift_first": normal_values(key_of[7], (D,), 0.3, 1.8, ((0, 16),), jnp.float32),
        "up_weight": normal_values(key_of[8], (D, FF), D ** -0.5, 0.21875, ((0, 16), (1, 4))),
        "up_bias": normal_values(key_of[9], (FF,), 0.3, 1.8, ((0, 4),), jnp.float32),
        "down_weight": normal_values(key_of[10], (D, FF), FF ** -0.5, 0.109375, ((0, 16), (1, 4))),
        "down_bias": normal_values(key_of[11], (D,), 0.3, 1.8, ((0, 16),), jnp.float32),
        "second_norm_gain": jnp.clip(1.0 + 0.1 * jax.random.normal(key_of[12], (D,), jnp.float32), 0.5, 1.5),
        "second_norm_shift": normal_values(key_of[13], (D,), 0.3, 1.8, ((0, 16),), jnp.float32),
        "cotangent": normal_values(key_of[14], (D, TOKENS), 1.0, 6.0, ((0, 16), (1, 8))),
    }


@jax.custom_vjp
def low(v):
    return lax.optimization_barrier(v.astype(jnp.bfloat16)).astype(jnp.float32)

@jax.custom_vjp
def low_back(v):
    return v

def low_keep(v):
    return (low(v), None)

def low_pass(kept, grad):
    return (grad,)

def back_keep(v):
    return (v, None)

def back_low(kept, grad):
    return (low(grad),)
low.defvjp(low_keep, low_pass)
low_back.defvjp(back_keep, back_low)
epsilon = 1e-06
masked_score = -1e+30

def product(left_side, right_side):
    return jnp.dot(left_side, right_side, precision=lax.Precision.HIGHEST, preferred_element_type=jnp.float32)

def norm_rows(hidden, gain, shift):
    centre = lax.optimization_barrier(jnp.mean(hidden, axis=-1, keepdims=True))
    offset = hidden - centre
    spread = lax.optimization_barrier(jnp.mean(offset * offset, axis=-1, keepdims=True))
    return offset * lax.rsqrt(spread + epsilon) * gain + shift

def head_block(operands, allowed):
    query_head, key_head, value_head = operands
    factor = 1.0 / math.sqrt(HDIM)
    scores = low_back(jnp.einsum('qd,kd->qk', query_head, key_head, precision=lax.Precision.HIGHEST) * factor)
    scores = jnp.where(allowed, scores, masked_score)
    probs = jax.nn.softmax(scores, axis=-1)
    return jnp.einsum('qk,kd->qd', low(probs), value_head, precision=lax.Precision.HIGHEST)

def one_sequence(tokens, seg_row, params):
    joint_weight, joint_bias, output_weight, output_bias, first_norm_gain, shift_first, up_weight, up_bias, down_weight, down_bias, second_norm_gain, second_norm_shift = params
    bias_pairs = joint_bias.reshape(HEADS, 2, HDIM)
    bias_full = jnp.stack([bias_pairs[:, 0], jnp.zeros_like(bias_pairs[:, 0]), bias_pairs[:, 1]], axis=1).reshape(3 * D)
    proj = low(low_back(product(tokens, joint_weight) + bias_full))
    parts = proj.reshape(SEQ, HEADS, 3, HDIM)
    queries = jnp.transpose(parts[:, :, 0], (1, 0, 2))
    keys = jnp.transpose(parts[:, :, 1], (1, 0, 2))
    values = jnp.transpose(parts[:, :, 2], (1, 0, 2))
    allowed = seg_row[:, None] == seg_row[None, :]
    heads_out = lax.map(jax.checkpoint(partial(head_block, allowed=allowed)), (queries, keys, values))
    attended = low(low_back(jnp.transpose(heads_out, (1, 0, 2)).reshape(SEQ, D)))
    attn = low_back(product(attended, output_weight) + output_bias)
    first_normalized = norm_rows(tokens + attn, first_norm_gain, shift_first)
    pre_act = low_back(product(low(first_normalized), up_weight) + up_bias)
    activ = low(jax.nn.gelu(pre_act, approximate=False))
    second_branch_output = low_back(product(activ, down_weight.T) + down_bias)
    return norm_rows(first_normalized + second_branch_output, second_norm_gain, second_norm_shift)

def reference(inputs, segments, joint_weight, joint_bias, output_weight, output_bias, first_norm_gain, shift_first, up_weight, up_bias, down_weight, down_bias, second_norm_gain, second_norm_shift, cotangent):
    params = tuple((array.astype(jnp.float32) for array in (joint_weight, joint_bias, output_weight, output_bias, first_norm_gain, shift_first, up_weight, up_bias, down_weight, down_bias, second_norm_gain, second_norm_shift)))
    stacked = inputs.astype(jnp.float32).T.reshape(SEQS, SEQ, D)

    def forward(tokens_all, *weights):

        def run_one(pair):
            return one_sequence(pair[0], pair[1], weights)
        return lax.map(jax.checkpoint(run_one), (tokens_all, segments))
    encoder_result, backward = jax.vjp(forward, stacked, *params)
    grads = backward(cotangent.astype(jnp.float32).T.reshape(SEQS, SEQ, D))
    return (encoder_result.reshape(TOKENS, D).T.astype(jnp.bfloat16), grads[0].reshape(TOKENS, D).T, grads[1], grads[2], grads[3], grads[4], grads[5], grads[6], grads[7], grads[8], grads[9], grads[10], grads[11], grads[12])
```

```python
import functools
import math

import jax
import jax.numpy as jnp
from jax import lax
from jax.experimental import pallas as pl
from jax.experimental.pallas import tpu as pltpu
from jax.sharding import PartitionSpec as P

HDIM = 64
EPS = 1e-06
BLOCK_OUT = -1e30
LOG2E = 1.4426950408889634
LN2 = 0.6931471805599453
BF = jnp.bfloat16
F32 = jnp.float32

DIM = 768
NCOL = 16
NROW = 4
TOK = 128
PER_HEAD = 5
SHARE = 104
ROWS = NCOL * SHARE
KEYS = 8192
AUG = 144


def split3(v):
    hi = v.astype(BF)
    rest = v - hi.astype(F32)
    mid = rest.astype(BF)
    low = (rest - mid.astype(F32)).astype(BF)
    return hi, mid, low


def dot(a, b, ca, cb):
    return lax.dot_general(a, b, (((ca,), (cb,)), ((), ())), preferred_element_type=F32)


def gelu_parts(x):
    phi = 0.5 * (1.0 + lax.erf(x * (1.0 / math.sqrt(2.0))))
    return phi


def key_rows(seg_row):
    width = seg_row.shape[1]
    row = lax.broadcasted_iota(jnp.int32, (16, width), 0)
    hot = jnp.where(row < 5, jnp.where(row == seg_row, 1.0, 0.0), jnp.where(row < 8, 1.0, 0.0))
    return hot.astype(BF)


def forward_kernel(q_ref, kv_ref, segq_ref, segk_ref, o_ref, qa_ref, kt_ref, va_ref):
    nblk = KEYS // TOK

    def build(b, _):
        kv = kv_ref[b]
        off = pl.multiple_of(b * TOK, TOK)
        kt_ref[0:64, pl.ds(off, TOK)] = kv[0:64]
        kt_ref[64:128, pl.ds(off, TOK)] = kv[0:64]
        kt_ref[128:144, pl.ds(off, TOK)] = key_rows(segk_ref[pl.ds(b, 1), :])
        turned = kv.astype(F32).T
        lane = lax.broadcasted_iota(jnp.int32, (TOK, TOK), 1)
        va_ref[pl.ds(off, TOK), :] = jnp.where(
            lane >= 64, turned, jnp.where(lane == 0, 1.0, 0.0)
        ).astype(BF)
        return 0

    lax.fori_loop(0, nblk, build, 0)

    qblk = 416
    kblk = 1024

    def one(i, _):
        off = pl.multiple_of(i * qblk, 16)
        rows = pl.ds(off, qblk)
        scaled = q_ref[rows, :].astype(F32) * (LOG2E / 8.0)
        hi = scaled.astype(BF)
        lo = (scaled - hi.astype(F32)).astype(BF)
        seg = segq_ref[rows, :]
        lane = lax.broadcasted_iota(jnp.int32, (qblk, 16), 1)
        pen = jnp.where((lane < 5) & (lane != seg), BLOCK_OUT, 0.0)
        qa = jnp.concatenate([hi, lo, pen.astype(BF)], axis=1)

        def step(j, carry):
            top, acc = carry
            koff = pl.multiple_of(j * kblk, kblk)
            s = dot(qa, kt_ref[:, pl.ds(koff, kblk)], 1, 0)
            raised = jnp.maximum(top, jnp.max(s, axis=1, keepdims=True))
            p = jnp.exp2(s - raised).astype(BF)
            fade = jnp.exp2(top - raised)
            acc = acc * fade + dot(p, va_ref[pl.ds(koff, kblk), :], 1, 0)
            return raised, acc

        top, acc = lax.fori_loop(
            0,
            KEYS // kblk,
            step,
            (jnp.full((qblk, 1), -3e38, F32), jnp.zeros((qblk, 128), F32)),
        )
        total = acc[:, 0:1]
        o_ref[rows, :] = acc[:, 64:128] / total
        lse = top + jnp.log(total) * LOG2E
        h, m, l = split3(-lse)
        ls = jnp.where(
            lane == 5, h.astype(F32), jnp.where(lane == 6, m.astype(F32), jnp.where(lane == 7, l.astype(F32), pen))
        )
        qa_ref[rows, :] = jnp.concatenate([hi, lo, ls.astype(BF)], axis=1)
        return 0

    lax.fori_loop(0, ROWS // qblk, one, 0)


def attend(q, kv, segq, segk):
    return pl.pallas_call(
        forward_kernel,
        out_shape=(
            jax.ShapeDtypeStruct((ROWS, HDIM), F32),
            jax.ShapeDtypeStruct((ROWS, AUG), BF),
        ),
        in_specs=[pl.BlockSpec(memory_space=pltpu.VMEM)] * 4,
        out_specs=[pl.BlockSpec(memory_space=pltpu.VMEM)] * 2,
        scratch_shapes=[pltpu.VMEM((AUG, KEYS), BF), pltpu.VMEM((KEYS, 128), BF)],
        compiler_params=pltpu.CompilerParams(vmem_limit_bytes=56 * 2**20),
        cost_estimate=pl.CostEstimate(
            flops=2 * ROWS * KEYS * 512, bytes_accessed=4 * 2**20, transcendentals=ROWS * KEYS
        ),
        name="attend",
    )(q, kv, segq, segk)


def backward_kernel(qa_ref, q_ref, qt_ref, do_ref, dot_ref, o_ref, kv_ref, segk_ref, dkv_ref, dq_ref, doa_ref, acc_ref):
    step = pl.program_id(0)

    @pl.when(step == 0)
    def _():
        grad = do_ref[...].astype(F32)
        delta = jnp.sum(grad * o_ref[...], axis=1, keepdims=True)
        h, m, l = split3(-delta)
        lane = lax.broadcasted_iota(jnp.int32, (ROWS, 16), 1)
        ext = jnp.where(
            lane == 5, h.astype(F32), jnp.where(lane == 6, m.astype(F32), jnp.where(lane == 7, l.astype(F32), 0.0))
        )
        doa_ref[...] = jnp.concatenate([do_ref[...], ext.astype(BF)], axis=1)
        acc_ref[...] = jnp.zeros_like(acc_ref)

    kvt = jnp.concatenate([kv_ref[0, i] for i in range(4)], axis=1)
    extra = jnp.concatenate([key_rows(segk_ref[0, i : i + 1, :]) for i in range(4)], axis=1)
    kt = jnp.concatenate([kvt[0:64], kvt[0:64], extra], axis=0)
    vt = jnp.concatenate([kvt[64:128], extra], axis=0)
    turned = kvt.astype(F32).T.astype(BF)
    s = dot(qa_ref[...], kt, 1, 0)
    p = jnp.exp2(s)
    dp = dot(doa_ref[...], vt, 1, 0)
    ds = (p * dp).astype(BF)
    acc_ref[...] += dot(ds, turned, 1, 0)
    dk = dot(qt_ref[...], ds, 1, 0) * 0.125
    dv = dot(dot_ref[...], p.astype(BF), 1, 0)
    both = jnp.concatenate([dk, dv], axis=0).astype(BF)
    for i in range(4):
        dkv_ref[0, i] = both[:, i * TOK : (i + 1) * TOK]

    @pl.when(step == pl.num_programs(0) - 1)
    def _():
        dq_ref[...] = (acc_ref[:, 0:64] * 0.125).astype(BF)


def attend_back(qa, q, grad, o, kv, segk):
    whole = lambda shape: pl.BlockSpec(shape, lambda i: (0,) * len(shape))
    return pl.pallas_call(
        backward_kernel,
        grid=(NCOL,),
        out_shape=(
            jax.ShapeDtypeStruct((NCOL, 4, TOK, TOK), BF),
            jax.ShapeDtypeStruct((ROWS, HDIM), BF),
        ),
        in_specs=[
            whole((ROWS, AUG)),
            whole((ROWS, HDIM)),
            whole((HDIM, ROWS)),
            whole((ROWS, HDIM)),
            whole((HDIM, ROWS)),
            whole((ROWS, HDIM)),
            pl.BlockSpec((1, 4, TOK, TOK), lambda i: (i, 0, 0, 0)),
            pl.BlockSpec((1, 4, TOK), lambda i: (i, 0, 0)),
        ],
        out_specs=[
            pl.BlockSpec((1, 4, TOK, TOK), lambda i: (i, 0, 0, 0)),
            whole((ROWS, HDIM)),
        ],
        scratch_shapes=[pltpu.VMEM((ROWS, 80), BF), pltpu.VMEM((ROWS, 128), F32)],
        compiler_params=pltpu.CompilerParams(vmem_limit_bytes=56 * 2**20),
        cost_estimate=pl.CostEstimate(
            flops=2 * ROWS * KEYS * 5 * 256, bytes_accessed=8 * 2**20, transcendentals=ROWS * KEYS
        ),
        name="attend_back",
    )(qa, q, q.T, grad, grad.T, o, kv.reshape(NCOL, 4, TOK, TOK), segk.reshape(NCOL, 4, TOK))


def pack_rows(blocks):
    return jnp.concatenate([blocks[..., 0:64, :], blocks[..., 64:128, :]], axis=-1)


def unpack_rows(blocks):
    return jnp.concatenate([blocks[..., 0:64], blocks[..., 64:128]], axis=-2)


def to_workers(heads):
    padded = jnp.pad(heads, ((0, 0), (0, 32), (0, 0)))
    windows = jnp.stack([padded[:, SHARE * k : SHARE * k + 128] for k in range(PER_HEAD)], axis=1)
    keep = jnp.arange(128)[None, None, :, None] < SHARE
    windows = jnp.where(keep, windows, jnp.zeros_like(windows))
    windows = windows.reshape(15, 128, HDIM)
    return jnp.pad(pack_rows(windows), ((0, 1), (0, 0), (0, 0)))


def from_tokens(received):
    return unpack_rows(received)[:, :SHARE].reshape(ROWS, HDIM)


def to_tokens(rows):
    padded = jnp.pad(rows.reshape(NCOL, SHARE, HDIM), ((0, 0), (0, 128 - SHARE), (0, 0)))
    return pack_rows(padded)


def from_workers(received):
    rows = unpack_rows(received[:15])[:, :SHARE]
    return rows.reshape(3, PER_HEAD * SHARE, HDIM)[:, : NROW * TOK]


def exchange(blocks, axis):
    return lax.all_to_all(blocks, axis, 0, 0, tiled=True)


def swap_cores(v):
    return lax.ppermute(v, "dp", [(0, 1), (1, 0)])


def hi_lo(v):
    hi = v.astype(BF)
    return hi, (v - hi.astype(F32)).astype(BF)


def per_device(
    inputs,
    segments,
    joint_weight,
    joint_bias,
    output_weight,
    output_bias,
    first_norm_gain,
    shift_first,
    up_weight,
    up_bias,
    down_weight,
    down_bias,
    second_norm_gain,
    second_norm_shift,
    cotangent,
):
    core = lax.axis_index("dp")
    col = lax.axis_index("col")

    vectors = jnp.stack(
        [output_bias, first_norm_gain, shift_first, down_bias, second_norm_gain, second_norm_shift]
    )
    my_bias = lax.dynamic_slice_in_dim(up_bias, (core * NCOL + col) * 24, 24, 0)
    small = jnp.concatenate(
        [part.ravel() for part in split3(vectors)] + [part.ravel() for part in split3(my_bias)]
    )
    small = jnp.pad(small, (0, 4 * 384 - small.shape[0])).reshape(4, 384)
    shard = jnp.concatenate(
        [
            lax.dynamic_slice_in_dim(up_weight, core * 384, 384, 1),
            lax.dynamic_slice_in_dim(down_weight, core * 384, 384, 1),
            lax.dynamic_slice_in_dim(output_weight, core * 96, 96, 0).reshape(12, 384),
            small,
        ],
        axis=0,
    )
    everything = lax.all_gather(shard, ("dp", "row", "col"), axis=0, tiled=False)
    everything = everything.reshape(2, NROW, NCOL, 112, 384)
    up_full = jnp.transpose(everything[:, :, :, 0:48], (2, 3, 1, 0, 4)).reshape(DIM, 3072)
    down_full = jnp.transpose(everything[:, :, :, 48:96], (2, 3, 1, 0, 4)).reshape(DIM, 3072)
    out_full = jnp.transpose(
        everything[:, :, :, 96:108].reshape(2, NROW, NCOL, 96, 48), (1, 0, 3, 2, 4)
    ).reshape(DIM, DIM)
    little = everything[:, :, :, 108:112].reshape(2, NROW, NCOL, 1536).astype(F32)
    vecs = little[0, 0, :, :864].reshape(NCOL, 3, 6, 48).sum(1)
    vecs = jnp.transpose(vecs, (1, 0, 2)).reshape(6, DIM)
    out_b, gain_1, shift_1, down_b, gain_2, shift_2 = [vecs[i][None, :] for i in range(6)]
    up_b = little[:, :, :, 864:936].reshape(2, NROW, NCOL, 3, 24).sum(3)
    up_b = jnp.transpose(up_b, (1, 0, 2, 3)).reshape(1, 3072)

    def by_col(a):
        return jnp.transpose(a.reshape(48, NCOL, TOK), (1, 0, 2))

    first = jnp.concatenate(
        [by_col(inputs), by_col(cotangent), jnp.broadcast_to(joint_weight[None], (NCOL, 48, 576))],
        axis=2,
    )
    first = exchange(first, "col")
    x_t = first[:, :, 0:TOK].reshape(DIM, TOK)
    ct_t = first[:, :, TOK : 2 * TOK].reshape(DIM, TOK)
    wj = first[:, :, 2 * TOK :].reshape(DIM, 576)

    x4 = lax.all_gather(x_t, "row", axis=0, tiled=False)
    xc_t = jnp.transpose(x4, (1, 0, 2)).reshape(DIM, NROW * TOK)
    wj3 = wj.reshape(DIM, 3, 3, HDIM)
    wq = wj3[:, :, 0].reshape(DIM, 192)
    wkv = wj3[:, :, 1:].reshape(DIM, 384)
    bias3 = joint_bias.reshape(3, 2, HDIM)
    q_all = (dot(xc_t, wq, 0, 0) + bias3[:, 0].reshape(1, 192)).astype(BF)
    kv_bias = jnp.concatenate([jnp.zeros((3, HDIM), F32), bias3[:, 1]], axis=1).reshape(384, 1)
    kv_all = (dot(wkv, xc_t, 0, 0) + kv_bias).astype(BF)
    kv_heads = jnp.transpose(kv_all.reshape(3, 128, NROW, TOK), (0, 2, 1, 3)).reshape(3, 512, TOK)
    kv_out = jnp.broadcast_to(kv_heads[:, None], (3, PER_HEAD, 512, TOK)).reshape(15, 512, TOK)
    kv_out = jnp.concatenate([kv_out, kv_heads[2:3]], axis=0)
    q_out = to_workers(jnp.transpose(q_all.reshape(512, 3, HDIM), (1, 0, 2)))
    arrived = exchange(jnp.concatenate([kv_out, q_out], axis=1), "col")
    kv = arrived[:, :512].reshape(64, TOK, TOK)
    q = from_tokens(arrived[:, 512:])

    seg_k = jnp.transpose(segments.reshape(NROW, NCOL, TOK), (1, 0, 2))
    seg_rows = jnp.pad(seg_k.reshape(NCOL, 512), ((0, 0), (0, 8)))
    seg_q = lax.dynamic_slice_in_dim(seg_rows, lax.rem(col, PER_HEAD) * SHARE, SHARE, 1)
    seg_q = seg_q.reshape(ROWS, 1)
    seg_k = seg_k.reshape(64, TOK)

    o, qa = attend(q, kv, seg_q, seg_k)

    attended_r = from_workers(exchange(to_tokens(o.astype(BF)), "col"))
    attended_r = jnp.transpose(attended_r, (1, 0, 2)).reshape(NROW, TOK, 192)
    attended = exchange(attended_r, "row")
    attended = jnp.transpose(attended, (1, 0, 2)).reshape(TOK, DIM)

    tok = x_t.T.astype(F32)
    cot = ct_t.T.astype(F32)
    h1 = tok + (jnp.dot(attended, out_full, preferred_element_type=F32) + out_b)
    mean1 = jnp.mean(h1, axis=1, keepdims=True)
    off1 = h1 - mean1
    inv1 = lax.rsqrt(jnp.mean(off1 * off1, axis=1, keepdims=True) + EPS)
    xhat1 = off1 * inv1
    n1 = xhat1 * gain_1 + shift_1
    n1_low = n1.astype(BF)
    pre = jnp.dot(n1_low, up_full, preferred_element_type=F32) + up_b
    phi = gelu_parts(pre)
    activ = (pre * phi).astype(BF)
    slope = phi + pre * jnp.exp(-0.5 * pre * pre) * (1.0 / math.sqrt(2.0 * math.pi))
    h2 = n1 + (dot(activ, down_full, 1, 1) + down_b)
    mean2 = jnp.mean(h2, axis=1, keepdims=True)
    off2 = h2 - mean2
    inv2 = lax.rsqrt(jnp.mean(off2 * off2, axis=1, keepdims=True) + EPS)
    xhat2 = off2 * inv2
    final = (xhat2 * gain_2 + shift_2).astype(BF)
    dx2 = cot * gain_2
    dh2 = inv2 * (
        dx2 - jnp.mean(dx2, axis=1, keepdims=True) - xhat2 * jnp.mean(dx2 * xhat2, axis=1, keepdims=True)
    )
    d_branch = dh2.astype(BF)
    d_pre = (jnp.dot(d_branch, down_full, preferred_element_type=F32) * slope).astype(BF)
    up1 = dh2 + dot(d_pre, up_full, 1, 1)
    dx1 = up1 * gain_1
    dh1 = inv1 * (
        dx1 - jnp.mean(dx1, axis=1, keepdims=True) - xhat1 * jnp.mean(dx1 * xhat1, axis=1, keepdims=True)
    )
    d_attn = dh1.astype(BF)
    d_att = dot(d_attn, out_full, 1, 1).astype(BF)
    norm_vecs = jnp.stack(
        [
            jnp.sum(up1 * xhat1, axis=0),
            jnp.sum(up1, axis=0),
            jnp.sum(cot * xhat2, axis=0),
            jnp.sum(cot, axis=0),
        ]
    )

    d_att_r = jnp.transpose(d_att.reshape(TOK, NROW, 192), (1, 0, 2))
    d_att_r = exchange(d_att_r, "row").reshape(512, 3, HDIM)
    grad_o = from_tokens(exchange(to_workers(jnp.transpose(d_att_r, (1, 0, 2))), "col"))
    dkv, dq = attend_back(qa, q, grad_o, o, kv, seg_k)
    back = exchange(jnp.concatenate([dkv.reshape(NCOL, 512, TOK), to_tokens(dq)], axis=1), "col")
    dkv_sum = jnp.sum(back[:15, :512].reshape(3, PER_HEAD, NROW, TOK, TOK).astype(F32), axis=1)
    dkv_t = jnp.transpose(dkv_sum.astype(BF), (0, 2, 1, 3)).reshape(3, TOK, 512)
    dq_t = jnp.transpose(from_workers(back[:, 512:]), (0, 2, 1))
    dproj_t = jnp.concatenate([dq_t, dkv_t], axis=1).reshape(576, 512)

    din = jnp.dot(wj, dproj_t, preferred_element_type=F32).astype(BF)
    din = exchange(jnp.transpose(din.reshape(DIM, NROW, TOK), (1, 0, 2)), "row")
    grad_in = (jnp.sum(din.astype(F32), axis=0) + dh1.T).astype(BF)
    grad_wj = dot(xc_t, dproj_t, 1, 1)
    bias_j = jnp.sum(dproj_t.astype(F32), axis=1).reshape(3, 3, HDIM)
    bias_j = jnp.stack([bias_j[:, 0], bias_j[:, 2]], axis=1).reshape(-1)

    rows_v = jnp.concatenate([part.reshape(24, 128) for part in hi_lo(norm_vecs)], axis=0)
    share = jnp.concatenate([n1_low.T, d_branch.T, d_attn.T, rows_v], axis=0)
    share = jnp.broadcast_to(share[None], (NROW, 3 * DIM + 48, TOK))

    def by_row(a):
        return jnp.transpose(a.reshape(TOK, NROW, 6, 128), (1, 2, 0, 3)).reshape(NROW, DIM, TOK)

    sent = jnp.concatenate([share, by_row(d_pre), by_row(activ)], axis=1)
    got = exchange(sent, "row")

    def feats(a):
        return jnp.transpose(a, (1, 0, 2)).reshape(DIM, 512)

    n1_c = feats(got[:, 0:DIM])
    db_c = feats(got[:, DIM : 2 * DIM])
    da_c = feats(got[:, 2 * DIM : 3 * DIM])
    nv = got[:, 3 * DIM : 3 * DIM + 48].astype(F32).reshape(NROW, 2, 4, DIM).sum((0, 1))

    def hidden(a):
        return jnp.transpose(a.reshape(NROW, 6, TOK, 128), (0, 2, 1, 3)).reshape(512, DIM)

    dp_c = hidden(got[:, 3 * DIM + 48 : 4 * DIM + 48])
    ac_c = hidden(got[:, 4 * DIM + 48 :])
    g_up = jnp.dot(n1_c, dp_c, preferred_element_type=F32)
    g_down = jnp.dot(db_c, ac_c, preferred_element_type=F32)
    g_out = jnp.dot(da_c, attended_r.reshape(512, 192), preferred_element_type=F32)
    cols_v = jnp.stack(
        [jnp.sum(db_c.astype(F32), axis=1), jnp.sum(da_c.astype(F32), axis=1)] + [nv[i] for i in range(4)],
        axis=1,
    )
    up_sums = jnp.sum(dp_c.astype(F32), axis=0)

    def spread(v):
        return jnp.tile(v.reshape(48, -1), (NCOL, 1))

    def halves(v):
        blocks = v.reshape(NCOL, 2, 24, v.shape[1])
        mine = lax.dynamic_index_in_dim(blocks, core, 1, keepdims=False)
        other = lax.dynamic_index_in_dim(blocks, 1 - core, 1, keepdims=False)
        return (mine.astype(F32) + swap_cores(other).astype(F32)).astype(BF)

    def pair(v):
        theirs = swap_cores(v)
        return jnp.where(core == 0, jnp.concatenate([v, theirs]), jnp.concatenate([theirs, v]))

    wide = jnp.concatenate(
        [g_up.astype(BF), g_down.astype(BF), g_out.astype(BF)]
        + list(hi_lo(cols_v))
        + [spread(part) for part in hi_lo(up_sums)]
        + [jnp.zeros((DIM, 20), BF)],
        axis=1,
    )
    wide = jnp.sum(exchange(halves(wide), "col").astype(F32), axis=0)
    wide = pair(wide)
    grad_up = wide[:, 0:768]
    grad_down = wide[:, 768:1536]
    grad_out = wide[:, 1536:1728].T
    six = wide[:, 1728:1734] + wide[:, 1734:1740]
    grad_up_bias = (wide[:, 1740:1756] + wide[:, 1756:1772]).reshape(768)

    last = jnp.concatenate(
        [grad_wj.astype(BF)] + [spread(part) for part in hi_lo(bias_j)] + [jnp.zeros((DIM, 48), BF)], axis=1
    )
    last = halves(last)
    mixed = jnp.concatenate([last.reshape(NCOL, 120, 128), grad_in.reshape(NCOL, 48, TOK)], axis=1)
    mixed = exchange(mixed, "col")
    grad_inputs = jnp.transpose(mixed[:, 120:], (1, 0, 2)).reshape(48, 2048).astype(F32)
    last = jnp.sum(mixed[:, :120].astype(F32), axis=0).reshape(24, 640)
    last = pair(last)
    grad_joint = last[:, :576]
    grad_joint_bias = (last[:, 576:584] + last[:, 584:592]).reshape(384)

    out_blocks = exchange(final.T.reshape(NCOL, 48, TOK), "col")
    layer_output = jnp.transpose(out_blocks, (1, 0, 2)).reshape(48, 2048)

    return (
        layer_output,
        grad_inputs,
        grad_joint,
        grad_joint_bias,
        grad_out,
        six[:, 1],
        six[:, 2],
        six[:, 3],
        grad_up,
        grad_up_bias,
        grad_down,
        six[:, 0],
        six[:, 4],
        six[:, 5],
    )


def solution(mesh):
    grid = P("col", ("dp", "row"))
    block = P("col", "row")
    return jax.shard_map(
        per_device,
        mesh=mesh,
        in_specs=(
            grid, P("dp", None), block, P("row"), P("row", "col"), P("col"), P("col"), P("col"),
            block, P("row"), block, P("col"), P("col"), P("col"), grid,
        ),
        out_specs=(
            grid, grid, block, P("row"), P("row", "col"), P("col"), P("col"), P("col"),
            block, P("row"), block, P("col"), P("col"), P("col"),
        ),
        check_vma=False,
    )
```

```python
import math

import jax
import jax.numpy as jnp
from jax import lax
from jax.experimental import pallas as pl
from jax.experimental.pallas import tpu as pltpu
from jax.sharding import PartitionSpec as P

HDIM = 64
EPS = 1e-06
BLOCK_OUT = -1e30
LOG2E = 1.4426950408889634
BF = jnp.bfloat16
F32 = jnp.float32

DIM = 768
FF = 3072
NCOL = 16
NROW = 4
TOK = 128
PER_HEAD = 5
SHARE = 104
TAIL = SHARE - 64
ROWS = NCOL * SHARE
AUG = 144
JW = 640
HALF = 2
FWD_C = 4
BWD_C = 2
MIB = 2**20
VMEM = pl.BlockSpec(memory_space=pltpu.VMEM)
SENT = 3 * DIM + 48 + 2 * DIM
WROWS = 768


def split3(v):
    hi = v.astype(BF)
    rest = v - hi.astype(F32)
    mid = rest.astype(BF)
    low = (rest - mid.astype(F32)).astype(BF)
    return hi, mid, low


def dot(a, b, ca, cb):
    return lax.dot_general(a, b, (((ca,), (cb,)), ((), ())), preferred_element_type=F32)


def params(limit):
    return pltpu.CompilerParams(vmem_limit_bytes=limit * MIB)


def cost(us):
    return pl.CostEstimate(flops=int(us * 1e9), bytes_accessed=int(us * 2e6), transcendentals=0)


def whole(shape):
    return pl.BlockSpec(shape, lambda i: (0,) * len(shape))


def project_kernel(x_ref, w_ref, b_ref, extra_ref, first_ref, second_ref, q_ref):
    w = w_ref[...].reshape(DIM, JW)
    q_ref[...] = jnp.zeros_like(q_ref)
    for r in range(NROW):
        tokens = x_ref[r].astype(F32).T.astype(BF)
        y = dot(tokens, w, 1, 0) + b_ref[...]
        q_ref[r * TOK : (r + 1) * TOK, :] = y[:, 0:256]
        out, at = (first_ref, r) if r < HALF else (second_ref, r - HALF)
        for h in range(3):
            kv = y[:, 256 + 128 * h : 384 + 128 * h].T.astype(BF)
            for j in range(PER_HEAD * h, PER_HEAD * (h + 1) + (1 if h == 2 else 0)):
                out[j, at * TOK : (at + 1) * TOK, :] = kv
    for j in range(NCOL):
        h, k = min(j, 14) // PER_HEAD, min(j, 14) % PER_HEAD
        lanes = slice(HDIM * h, HDIM * (h + 1))
        a = q_ref[SHARE * k : SHARE * k + 64, lanes]
        b = q_ref[SHARE * k + 64 : SHARE * k + 128, lanes]
        first_ref[j, 256:320, :] = jnp.concatenate([a, b], axis=1).astype(BF)
    second_ref[:, 256:352, :] = extra_ref[...]


def project(x4, wj, bias, extra):
    return pl.pallas_call(
        project_kernel,
        out_shape=(
            jax.ShapeDtypeStruct((NCOL, 320, 128), BF),
            jax.ShapeDtypeStruct((NCOL, 352, 128), BF),
        ),
        in_specs=[VMEM] * 4,
        out_specs=[VMEM] * 2,
        scratch_shapes=[pltpu.VMEM((640, 256), F32)],
        compiler_params=params(40),
        cost_estimate=cost(3),
        name="project",
    )(x4, wj, bias, extra)


def key_rows(seg_row):
    row = lax.broadcasted_iota(jnp.int32, (16, seg_row.shape[1]), 0)
    hot = jnp.where(row < 5, jnp.where(row == seg_row, 1.0, 0.0), jnp.where(row < 8, 1.0, 0.0))
    return hot.astype(BF)


def offset_columns(value, base):
    h, m, l = split3(-value)
    lane = lax.broadcasted_iota(jnp.int32, base.shape, 1)
    return jnp.where(
        lane == 5,
        h.astype(F32),
        jnp.where(lane == 6, m.astype(F32), jnp.where(lane == 7, l.astype(F32), base)),
    )


def key_block(kv_ref, seg_ref, count):
    kvt = jnp.concatenate(
        [kv_ref[c, r * TOK : (r + 1) * TOK, :] for c in range(count) for r in range(HALF)], axis=1
    )
    extra = jnp.concatenate([key_rows(seg_ref[0, i : i + 1, :]) for i in range(count * HALF)], axis=1)
    return kvt, extra


def unpack(block_ref, store):
    for c in range(NCOL):
        block = block_ref[c].astype(F32)
        store(SHARE * c, block[:, 0:64])
        store(SHARE * c + 64, block[0:TAIL, 64:128])


def forward_step(qa_ref, kv_ref, seg_ref, acc_ref, top_ref):
    kvt, extra = key_block(kv_ref, seg_ref, FWD_C)
    kt = jnp.concatenate([kvt[0:64], kvt[0:64], extra], axis=0)
    turned = kvt.astype(F32).T
    lane = lax.broadcasted_iota(jnp.int32, turned.shape, 1)
    va = jnp.where(lane >= 64, turned, jnp.where(lane == 0, 1.0, 0.0)).astype(BF)
    s = dot(qa_ref[...], kt, 1, 0)
    parts = [s[:, i * 128 : (i + 1) * 128] for i in range(s.shape[1] // 128)]
    high = parts[0]
    for part in parts[1:]:
        high = jnp.maximum(high, part)
    top = top_ref[...]
    raised = jnp.maximum(top, jnp.broadcast_to(jnp.max(high, axis=1, keepdims=True), top.shape))
    p = jnp.concatenate([jnp.exp2(part - raised).astype(BF) for part in parts], axis=1)
    fade = jnp.exp2(top - raised)
    top_ref[...] = raised
    acc_ref[...] = acc_ref[...] * fade + dot(p, va, 1, 0)


def attend_first_kernel(q_ref, kv_ref, segq_ref, seg_ref, qa_ref, acc_ref, top_ref, q_scr):
    @pl.when(pl.program_id(0) == 0)
    def _():
        def store(at, rows):
            q_scr[at : at + rows.shape[0], :] = rows

        unpack(q_ref, store)
        scaled = q_scr[...] * (LOG2E / 8.0)
        hi = scaled.astype(BF)
        lo = (scaled - hi.astype(F32)).astype(BF)
        lane = lax.broadcasted_iota(jnp.int32, (ROWS, 16), 1)
        pen = jnp.where((lane < 5) & (lane != segq_ref[...]), BLOCK_OUT, 0.0)
        qa_ref[...] = jnp.concatenate([hi, lo, pen.astype(BF)], axis=1)
        acc_ref[...] = jnp.zeros_like(acc_ref)
        top_ref[...] = jnp.full_like(top_ref, -3e38)

    forward_step(qa_ref, kv_ref, seg_ref, acc_ref, top_ref)


def attend_second_kernel(
    qa_in, acc_in, top_in, kv_ref, seg_ref, qa_ref, o_ref, out_ref, acc_ref, top_ref
):
    @pl.when(pl.program_id(0) == 0)
    def _():
        acc_ref[...] = acc_in[...]
        top_ref[...] = top_in[...]

    forward_step(qa_in, kv_ref, seg_ref, acc_ref, top_ref)

    @pl.when(pl.program_id(0) == pl.num_programs(0) - 1)
    def _():
        acc = acc_ref[...]
        total = acc[:, 0:1]
        o = acc[:, 64:128] / total
        o_ref[...] = o
        qa_ref[:, 0:128] = qa_in[:, 0:128]
        lse = top_ref[:, 0:1] + jnp.log(total) * LOG2E
        qa_ref[:, 128:144] = offset_columns(lse, qa_in[:, 128:144].astype(F32)).astype(BF)
        for c in range(NCOL):
            out_ref[c] = pack(o_ref, SHARE * c)


def pack(ref, at, scale=None):
    a = ref[at : at + 64, 0:64]
    b = jnp.concatenate([ref[at + 64 : at + SHARE, 0:64], jnp.zeros((64 - TAIL, 64), F32)], axis=0)
    both = jnp.concatenate([a, b], axis=1)
    if scale is not None:
        both = both * scale
    return both.astype(BF)


def attend(first, second, segq, seg_first, seg_second):
    steps = NCOL // FWD_C
    kinds = (
        jax.ShapeDtypeStruct((ROWS, AUG), BF),
        jax.ShapeDtypeStruct((ROWS, 128), F32),
        jax.ShapeDtypeStruct((ROWS, 128), F32),
    )
    seg_spec = pl.BlockSpec((1, FWD_C * HALF, TOK), lambda i: (i, 0, 0))
    state = pl.pallas_call(
        attend_first_kernel,
        grid=(steps,),
        out_shape=kinds,
        in_specs=[
            pl.BlockSpec((NCOL, 64, 128), lambda i: (0, 4, 0)),
            pl.BlockSpec((FWD_C, 256, 128), lambda i: (i, 0, 0)),
            whole((ROWS, 1)),
            seg_spec,
        ],
        out_specs=[whole((ROWS, AUG)), whole((ROWS, 128)), whole((ROWS, 128))],
        scratch_shapes=[pltpu.VMEM((ROWS, HDIM), F32)],
        compiler_params=params(58),
        cost_estimate=cost(10),
        name="attend_first",
    )(first, first, segq, seg_first)
    return pl.pallas_call(
        attend_second_kernel,
        grid=(steps,),
        out_shape=(
            kinds[0],
            jax.ShapeDtypeStruct((ROWS, HDIM), F32),
            jax.ShapeDtypeStruct((NCOL, 64, 128), BF),
        ),
        in_specs=[
            whole((ROWS, AUG)),
            whole((ROWS, 128)),
            whole((ROWS, 128)),
            pl.BlockSpec((FWD_C, 256, 128), lambda i: (i, 0, 0)),
            seg_spec,
        ],
        out_specs=[whole((ROWS, AUG)), whole((ROWS, HDIM)), whole((NCOL, 64, 128))],
        scratch_shapes=[pltpu.VMEM((ROWS, 128), F32), pltpu.VMEM((ROWS, 128), F32)],
        compiler_params=params(58),
        cost_estimate=cost(10),
        name="attend_second",
    )(*state, second, seg_second)


def backward_step(qa_ref, doa_ref, turned_ref, kv_ref, seg_ref, acc_ref):
    kvt, extra = key_block(kv_ref, seg_ref, BWD_C)
    kt = jnp.concatenate([kvt[0:64], kvt[0:64], extra], axis=0)
    vt = jnp.concatenate([kvt[64:128], extra], axis=0)
    keys = kvt.astype(F32).T.astype(BF)
    p = jnp.exp2(dot(qa_ref[...], kt, 1, 0))
    dp = dot(doa_ref[...], vt, 1, 0)
    ds = (p * dp).astype(BF)
    acc_ref[...] += dot(ds, keys, 1, 0)
    dk = dot(turned_ref[0:64, :], ds, 1, 0) * 0.125
    dv = dot(turned_ref[64:128, :], p.astype(BF), 1, 0)
    return jnp.concatenate([dk, dv], axis=0).astype(BF)


def store_keys(out_ref, at, both):
    for c in range(BWD_C):
        for r in range(HALF):
            i = c * HALF + r
            out_ref[at + c, r * TOK : (r + 1) * TOK, :] = both[:, i * TOK : (i + 1) * TOK]


def back_first_kernel(
    q_ref, do_ref, qa_ref, o_ref, fin_ref, kv_ref, seg_ref, out_ref, doa_ref, turned_ref, acc_ref, pair_scr
):
    @pl.when(pl.program_id(0) == 0)
    def _():
        def store_q(at, rows):
            pair_scr[at : at + rows.shape[0], 0:64] = rows

        def store_do(at, rows):
            pair_scr[at : at + rows.shape[0], 64:128] = rows

        unpack(q_ref, store_q)
        unpack(do_ref, store_do)
        pairs = pair_scr[...]
        turned_ref[...] = pairs.T.astype(BF)
        grad = pairs[:, 64:128]
        delta = jnp.sum(grad * o_ref[...], axis=1, keepdims=True)
        ext = offset_columns(delta, jnp.zeros((ROWS, 16), F32))
        doa_ref[...] = jnp.concatenate([grad.astype(BF), ext.astype(BF)], axis=1)
        acc_ref[...] = jnp.zeros_like(acc_ref)

    both = backward_step(qa_ref, doa_ref, turned_ref, kv_ref, seg_ref, acc_ref)
    store_keys(out_ref, 0, both)
    out_ref[:, 256:304, :] = fin_ref[...]


def back_second_kernel(qa_ref, doa_ref, turned_ref, acc_in, kv_ref, seg_ref, out_ref, acc_ref):
    step = pl.program_id(0)

    @pl.when(step == 0)
    def _():
        acc_ref[...] = acc_in[...]

    both = backward_step(qa_ref, doa_ref, turned_ref, kv_ref, seg_ref, acc_ref)
    store_keys(out_ref, step * BWD_C, both)

    @pl.when(step == pl.num_programs(0) - 1)
    def _():
        for c in range(NCOL):
            out_ref[c, 256:320, :] = pack(acc_ref, SHARE * c, 0.125)


SEG_BACK = pl.BlockSpec((1, BWD_C * HALF, TOK), lambda i: (i, 0, 0))
KEYS_BACK = pl.BlockSpec((BWD_C, 256, 128), lambda i: (i, 0, 0))
BACK_STEPS = NCOL // BWD_C


def attend_back_first(first, grad, qa, o, fin, seg_first):
    return pl.pallas_call(
        back_first_kernel,
        grid=(BACK_STEPS,),
        out_shape=(
            jax.ShapeDtypeStruct((NCOL, 304, 128), BF),
            jax.ShapeDtypeStruct((ROWS, 80), BF),
            jax.ShapeDtypeStruct((128, ROWS), BF),
            jax.ShapeDtypeStruct((ROWS, 128), F32),
        ),
        in_specs=[
            pl.BlockSpec((NCOL, 64, 128), lambda i: (0, 4, 0)),
            whole((NCOL, 64, 128)),
            whole((ROWS, AUG)),
            whole((ROWS, HDIM)),
            pl.BlockSpec((BWD_C, 48, 128), lambda i: (i, 0, 0)),
            KEYS_BACK,
            SEG_BACK,
        ],
        out_specs=[
            pl.BlockSpec((BWD_C, 304, 128), lambda i: (i, 0, 0)),
            whole((ROWS, 80)),
            whole((128, ROWS)),
            whole((ROWS, 128)),
        ],
        scratch_shapes=[pltpu.VMEM((ROWS, 128), F32)],
        compiler_params=params(58),
        cost_estimate=cost(18),
        name="attend_back_first",
    )(first, grad, qa, o, fin, first, seg_first)


def attend_back_second(qa, doa, turned, acc, second, seg_second):
    return pl.pallas_call(
        back_second_kernel,
        grid=(BACK_STEPS,),
        out_shape=jax.ShapeDtypeStruct((NCOL, 320, 128), BF),
        in_specs=[
            whole((ROWS, AUG)),
            whole((ROWS, 80)),
            whole((128, ROWS)),
            whole((ROWS, 128)),
            KEYS_BACK,
            SEG_BACK,
        ],
        out_specs=whole((NCOL, 320, 128)),
        scratch_shapes=[pltpu.VMEM((ROWS, 128), F32)],
        compiler_params=params(58),
        cost_estimate=cost(18),
        name="attend_back_second",
    )(qa, doa, turned, acc, second, seg_second)


def gather_rows(block_ref, scr, rows=slice(0, 64)):
    for j in range(15):
        h, k = j // PER_HEAD, j % PER_HEAD
        block = block_ref[j, rows, :].astype(F32)
        lanes = slice(HDIM * h, HDIM * (h + 1))
        scr[SHARE * k : SHARE * k + 64, lanes] = block[:, 0:64]
        scr[SHARE * k + 64 : SHARE * (k + 1), lanes] = block[0:TAIL, 64:128]


def to_row_kernel(got_ref, bias_ref, out_ref, scr):
    gather_rows(got_ref, scr)
    for r in range(NROW):
        out_ref[r, 0:TOK, :] = scr[r * TOK : (r + 1) * TOK, :].astype(BF)
        out_ref[r, TOK : TOK + 16, :] = bias_ref[...]


def to_row(got, bias_rows):
    return pl.pallas_call(
        to_row_kernel,
        out_shape=jax.ShapeDtypeStruct((NROW, TOK + 16, 192), BF),
        in_specs=[VMEM] * 2,
        out_specs=VMEM,
        scratch_shapes=[pltpu.VMEM((528, 192), F32)],
        cost_estimate=cost(1),
        compiler_params=params(16),
        name="to_row",
    )(got, bias_rows)


def to_col_kernel(got_ref, out_ref, scr):
    scr[512:640, :] = jnp.zeros((128, 192), F32)
    for r in range(NROW):
        scr[r * TOK : (r + 1) * TOK, :] = got_ref[r].astype(F32)
    for j in range(15):
        h, k = j // PER_HEAD, j % PER_HEAD
        lanes = slice(HDIM * h, HDIM * (h + 1))
        a = scr[SHARE * k : SHARE * k + 64, lanes]
        b = scr[SHARE * k + 64 : SHARE * k + 128, lanes]
        out_ref[j] = jnp.concatenate([a, b], axis=1).astype(BF)
    out_ref[15] = jnp.zeros((64, 128), BF)


def to_col(got):
    return pl.pallas_call(
        to_col_kernel,
        out_shape=jax.ShapeDtypeStruct((NCOL, 64, 128), BF),
        in_specs=[VMEM],
        out_specs=VMEM,
        scratch_shapes=[pltpu.VMEM((640, 192), F32)],
        cost_estimate=cost(1),
        compiler_params=params(16),
        name="to_col",
    )(got)


def feature_mean(v):
    return jnp.sum(v, axis=1, keepdims=True) * (1.0 / DIM)


def tokenwise_kernel(
    att_ref, x_ref, extra_ref, all_ref,
    sent_ref, datt_ref, fin_ref, dh1_ref,
    up_ref, down_ref, out_ref, slope_ref, act_ref, sems,
):
    copies = []
    for g in range(3):
        for k in range(2):
            for r in range(NROW):
                copies.append(
                    pltpu.make_async_copy(
                        all_ref.at[k, r, :, 96:112, g * 128 : (g + 1) * 128],
                        out_ref.at[k * NROW + r, :, 16 * g : 16 * (g + 1), :],
                        sems.at[0],
                    )
                )
    n_out = len(copies)
    for r in range(NROW):
        for k in range(2):
            lanes = slice(r * DIM + k * 384, r * DIM + (k + 1) * 384)
            copies.append(
                pltpu.make_async_copy(all_ref.at[k, r, :, 0:48, :], up_ref.at[:, :, lanes], sems.at[1 + r])
            )
    for r in range(NROW):
        for k in range(2):
            lanes = slice(r * DIM + k * 384, r * DIM + (k + 1) * 384)
            copies.append(
                pltpu.make_async_copy(all_ref.at[k, r, :, 48:96, :], down_ref.at[:, :, lanes], sems.at[5 + r])
            )
    for copy in copies:
        copy.start()

    def wait(group):
        chosen = copies[:n_out] if group == 0 else copies[n_out + 2 * (group - 1) : n_out + 2 * group]
        for copy in chosen:
            copy.wait()

    tok = x_ref[...].reshape(DIM, TOK).astype(F32).T
    cot = extra_ref[:, 256:304, :].reshape(DIM, TOK).astype(F32).T
    vecs = extra_ref[:, 304:352, :].reshape(DIM, TOK).astype(F32).T
    out_b, gain_1, shift_1, down_b, gain_2, shift_2 = [
        vecs[i : i + 1] + vecs[6 + i : 7 + i] + vecs[12 + i : 13 + i] for i in range(6)
    ]
    gap = jnp.zeros((TOK, 32), BF)

    wait(0)
    attn = jnp.zeros((TOK, DIM), F32)
    for r in range(NROW):
        rows = att_ref[r, 0:TOK, :]
        for k in range(2):
            piece = jnp.concatenate([rows[:, 96 * k : 96 * (k + 1)], gap], axis=1)
            attn = attn + dot(piece, out_ref[k * NROW + r].reshape(DIM, 128), 1, 1)
    h1 = tok + (attn + out_b)
    off = h1 - feature_mean(h1)
    inv1 = lax.rsqrt(feature_mean(off * off) + EPS)
    xhat1 = off * inv1
    n1 = xhat1 * gain_1 + shift_1
    n1_low = n1.astype(BF)

    branch = jnp.zeros((TOK, DIM), F32)
    for r in range(NROW):
        wait(1 + r)
        cols = slice(r * DIM, (r + 1) * DIM)
        parts = att_ref[r, TOK : TOK + 12, :].astype(F32)
        parts = parts[0:4] + parts[4:8] + parts[8:12]
        up_b = jnp.concatenate([parts[i : i + 1] for i in range(4)], axis=1)
        pre = dot(n1_low, up_ref[:, :, cols].reshape(DIM, DIM), 1, 0) + up_b
        phi = 0.5 * (1.0 + lax.erf(pre * (1.0 / math.sqrt(2.0))))
        act = (pre * phi).astype(BF)
        slope_ref[:, cols] = phi + pre * jnp.exp(-0.5 * pre * pre) * (1.0 / math.sqrt(2.0 * math.pi))
        for i in range(6):
            at = 3 * DIM + 48 + DIM + i * TOK
            sent_ref[r, at : at + TOK, :] = act[:, i * TOK : (i + 1) * TOK]
        wait(5 + r)
        branch = branch + dot(act, down_ref[:, :, cols].reshape(DIM, DIM), 1, 1)
    h2 = n1 + (branch + down_b)
    off = h2 - feature_mean(h2)
    inv2 = lax.rsqrt(feature_mean(off * off) + EPS)
    xhat2 = off * inv2
    fin_ref[...] = (xhat2 * gain_2 + shift_2).T.astype(BF).reshape(NCOL, 48, TOK)
    dx = cot * gain_2
    dh2 = inv2 * (dx - feature_mean(dx) - xhat2 * feature_mean(dx * xhat2))
    d_branch = dh2.astype(BF)

    back = jnp.zeros((TOK, DIM), F32)
    for r in range(NROW):
        cols = slice(r * DIM, (r + 1) * DIM)
        d_act = dot(d_branch, down_ref[:, :, cols].reshape(DIM, DIM), 1, 0)
        d_pre = (d_act * slope_ref[:, cols]).astype(BF)
        for i in range(6):
            at = 3 * DIM + 48 + i * TOK
            sent_ref[r, at : at + TOK, :] = d_pre[:, i * TOK : (i + 1) * TOK]
        back = back + dot(d_pre, up_ref[:, :, cols].reshape(DIM, DIM), 1, 1)
    up1 = dh2 + back
    dx = up1 * gain_1
    dh1 = inv1 * (dx - feature_mean(dx) - xhat1 * feature_mean(dx * xhat1))
    d_attn = dh1.astype(BF)
    for r in range(NROW):
        pieces = [dot(d_attn, out_ref[k * NROW + r].reshape(DIM, 128), 1, 0)[:, 0:96] for k in range(2)]
        datt_ref[r] = jnp.concatenate(pieces, axis=1).astype(BF)
    turned = dh1.T
    dh1_ref[...] = turned
    shared = [n1.T.astype(BF), dh2.T.astype(BF), turned.astype(BF)]
    sums = [
        jnp.sum(v, axis=0, keepdims=True) for v in (up1 * xhat1, up1, cot * xhat2, cot)
    ]
    rows = []
    for part in range(2):
        for v in sums:
            hi = v.astype(BF).astype(F32)
            piece = hi if part == 0 else v - hi
            rows += [piece[:, i * 128 : (i + 1) * 128] for i in range(6)]
    shared.append(jnp.concatenate(rows, axis=0).astype(BF))
    at = 0
    for v in shared:
        for r in range(NROW):
            sent_ref[r, at : at + v.shape[0], :] = v
        at += v.shape[0]


def tokenwise(att, x_t, extra, everything):
    return pl.pallas_call(
        tokenwise_kernel,
        out_shape=(
            jax.ShapeDtypeStruct((NROW, SENT, TOK), BF),
            jax.ShapeDtypeStruct((NROW, TOK, 192), BF),
            jax.ShapeDtypeStruct((NCOL, 48, TOK), BF),
            jax.ShapeDtypeStruct((DIM, TOK), F32),
        ),
        in_specs=[VMEM] * 3 + [pl.BlockSpec(memory_space=pl.ANY)],
        out_specs=[VMEM] * 4,
        scratch_shapes=[
            pltpu.VMEM((NCOL, 48, FF), BF),
            pltpu.VMEM((NCOL, 48, FF), BF),
            pltpu.VMEM((2 * NROW, NCOL, 48, 128), BF),
            pltpu.VMEM((TOK, FF), F32),
            pltpu.VMEM((TOK, FF), BF),
            pltpu.SemaphoreType.DMA((9,)),
        ],
        compiler_params=params(48),
        cost_estimate=cost(15),
        name="tokenwise",
    )(att, x_t, extra, everything)


def place(core, mine_ref, other_ref, blocks, half_rows):
    for at, block in blocks:
        low = at < half_rows
        local = at if low else at - half_rows
        rows = slice(local, local + block.shape[1])
        keep = core == (0 if low else 1)

        @pl.when(keep)
        def _():
            mine_ref[:, rows, :] = block

        @pl.when(jnp.logical_not(keep))
        def _():
            other_ref[:, rows, :] = block


def weight_grads_kernel(core_ref, got_ref, att_ref, mine_ref, other_ref):
    core = core_ref[0]

    def feats(at):
        return jnp.concatenate([got_ref[r, at : at + DIM, :] for r in range(NROW)], axis=1)

    def hidden(at):
        return jnp.concatenate(
            [
                jnp.concatenate([got_ref[r, at + i * TOK : at + (i + 1) * TOK, :] for i in range(6)], axis=1)
                for r in range(NROW)
            ],
            axis=0,
        )

    def chunks(g, count):
        return [g[:, i * 128 : (i + 1) * 128].astype(BF).reshape(NCOL, 48, 128) for i in range(count)]

    ones = jnp.ones((16, NROW * TOK), BF)
    d_pre = hidden(3 * DIM + 48)
    d_branch = feats(DIM)
    d_attn = feats(2 * DIM)
    att = jnp.concatenate([att_ref[r, 0:TOK, :] for r in range(NROW)], axis=0)
    att = jnp.concatenate([att, jnp.zeros((NROW * TOK, 64), BF)], axis=1)
    pieces = chunks(dot(feats(0), d_pre, 1, 0), 6)
    pieces += chunks(dot(d_branch, hidden(4 * DIM + 48), 1, 0), 6)
    pieces += chunks(dot(d_attn, att, 1, 0), 2)
    sums = [dot(ones, d_branch, 1, 1)[0:1], dot(ones, d_attn, 1, 1)[0:1], dot(ones, d_pre, 1, 0)[0:1]]
    norm = got_ref[0, 3 * DIM : 3 * DIM + 48, :].astype(F32)
    for r in range(1, NROW):
        norm = norm + got_ref[r, 3 * DIM : 3 * DIM + 48, :].astype(F32)
    rows = [norm[0:24] + norm[24:48]]
    for v in sums:
        rows += [v[:, i * 128 : (i + 1) * 128] for i in range(6)]
    rows.append(jnp.zeros((6, 128), F32))
    rows = jnp.concatenate(rows, axis=0)
    hi = rows.astype(BF)
    lo = (rows - hi.astype(F32)).astype(BF)
    misc = jnp.concatenate([hi, lo], axis=0)
    blocks = [(48 * i, piece) for i, piece in enumerate(pieces)]
    blocks.append((672, jnp.broadcast_to(misc[None], (NCOL, 96, 128))))
    place(core, mine_ref, other_ref, blocks, WROWS // 2)


def weight_grads(core, got, att):
    kind = jax.ShapeDtypeStruct((NCOL, WROWS // 2, 128), BF)
    return pl.pallas_call(
        weight_grads_kernel,
        out_shape=(kind, kind),
        in_specs=[pl.BlockSpec(memory_space=pltpu.SMEM)] + [VMEM] * 2,
        out_specs=[VMEM] * 2,
        compiler_params=params(48),
        cost_estimate=cost(5),
        name="weight_grads",
    )(core, got, att)


def project_back_kernel(
    core_ref, first_ref, second_ref, w_ref, x_ref, din_ref, mine_ref, other_ref, scr
):
    core = core_ref[0]
    scr[...] = jnp.zeros_like(scr)
    gather_rows(second_ref, scr, slice(256, 320))
    dq = scr[0:512, :].T.astype(BF)
    w = w_ref[...].reshape(DIM, JW)
    grad = jnp.zeros((DIM, JW), F32)
    total = jnp.zeros((16, JW), F32)
    ones = jnp.ones((16, TOK), BF)
    for r in range(NROW):
        source, at = (first_ref, r) if r < HALF else (second_ref, r - HALF)
        parts = [dq[:, r * TOK : (r + 1) * TOK]]
        for h in range(3):
            acc = source[PER_HEAD * h, at * TOK : (at + 1) * TOK, :].astype(F32)
            for k in range(1, PER_HEAD):
                acc = acc + source[PER_HEAD * h + k, at * TOK : (at + 1) * TOK, :].astype(F32)
            parts.append(acc.astype(BF))
        d_proj = jnp.concatenate(parts, axis=0)
        din_ref[r] = dot(w, d_proj, 1, 0).astype(BF)
        grad = grad + dot(x_ref[r], d_proj, 1, 1)
        total = total + dot(ones, d_proj, 1, 1)
    rows = [total[0:1, i * 128 : (i + 1) * 128] for i in range(5)] + [jnp.zeros((3, 128), F32)]
    rows = jnp.concatenate(rows, axis=0)
    hi = rows.astype(BF)
    lo = (rows - hi.astype(F32)).astype(BF)
    misc = jnp.broadcast_to(jnp.concatenate([hi, lo], axis=0)[None], (NCOL, 16, 128))
    low = grad.astype(BF)
    pieces = [low[:, i * 128 : (i + 1) * 128].reshape(NCOL, 48, 128) for i in range(5)]
    blocks = [(0, pieces[0]), (48, pieces[1]), (96, pieces[2][:, 0:32]), (128, pieces[2][:, 32:48])]
    blocks += [(144, pieces[3]), (192, pieces[4]), (240, misc)]
    place(core, mine_ref, other_ref, blocks, 128)


def project_back(core, first, second, wj, x4):
    kind = jax.ShapeDtypeStruct((NCOL, 128, 128), BF)
    return pl.pallas_call(
        project_back_kernel,
        out_shape=(jax.ShapeDtypeStruct((NROW, DIM, TOK), BF), kind, kind),
        in_specs=[pl.BlockSpec(memory_space=pltpu.SMEM)] + [VMEM] * 4,
        out_specs=[VMEM] * 3,
        scratch_shapes=[pltpu.VMEM((528, 256), F32)],
        compiler_params=params(48),
        cost_estimate=cost(5),
        name="project_back",
    )(core, first, second, wj, x4)


def last_kernel(mine_ref, theirs_ref, din_ref, dh1_ref, out_ref):
    out_ref[:, 0:128, :] = (mine_ref[...].astype(F32) + theirs_ref[...].astype(F32)).astype(BF)
    total = dh1_ref[...]
    for r in range(NROW):
        total = total + din_ref[r].astype(F32)
    out_ref[:, 128:176, :] = total.astype(BF).reshape(NCOL, 48, TOK)


def last_payload(mine, theirs, din, dh1):
    return pl.pallas_call(
        last_kernel,
        out_shape=jax.ShapeDtypeStruct((NCOL, 176, 128), BF),
        in_specs=[VMEM] * 4,
        out_specs=VMEM,
        compiler_params=params(24),
        cost_estimate=cost(1),
        name="last_payload",
    )(mine, theirs, din, dh1)


def exchange(blocks, axis):
    return lax.all_to_all(blocks, axis, 0, 0, tiled=True)


def swap_cores(v):
    return lax.ppermute(v, "dp", [(0, 1), (1, 0)])


def pair(core, v):
    theirs = swap_cores(v)
    return jnp.where(core == 0, jnp.concatenate([v, theirs]), jnp.concatenate([theirs, v]))


def per_device(
    inputs,
    segments,
    joint_weight,
    joint_bias,
    output_weight,
    output_bias,
    first_norm_gain,
    shift_first,
    up_weight,
    up_bias,
    down_weight,
    down_bias,
    second_norm_gain,
    second_norm_shift,
    cotangent,
):
    core = lax.axis_index("dp")
    col = lax.axis_index("col")
    core_word = core.reshape(1).astype(jnp.int32)

    def by_col(a):
        return jnp.transpose(a.reshape(48, NCOL, TOK), (1, 0, 2))

    x_t = exchange(by_col(inputs), "col")
    jw = joint_weight.reshape(48, 3, 3, HDIM)
    jw = jnp.concatenate(
        [jw[:, :, 0].reshape(48, 192), jnp.zeros((48, 64), BF), jw[:, :, 1:].reshape(48, 384)], axis=1
    )
    x_t, jw = lax.optimization_barrier((x_t, jw))
    wj = exchange(jnp.broadcast_to(jw[None], (NCOL, 48, JW)), "col")
    x4 = lax.all_gather(x_t.reshape(DIM, TOK), "row", axis=0, tiled=False)

    turned = lax.dynamic_slice_in_dim(output_weight, core * 96, 96, 0).T
    turned = jnp.pad(turned, ((0, 0), (0, 32))).reshape(3, 16, 128)
    turned = jnp.transpose(turned, (1, 0, 2)).reshape(16, 384)
    shard = jnp.concatenate(
        [
            lax.dynamic_slice_in_dim(up_weight, core * 384, 384, 1),
            lax.dynamic_slice_in_dim(down_weight, core * 384, 384, 1),
            turned,
        ],
        axis=0,
    )
    everything = lax.all_gather(shard, ("dp", "row", "col"), axis=0, tiled=False)
    everything = everything.reshape(2, NROW, NCOL, 112, 384)

    vectors = jnp.stack(
        [output_bias, first_norm_gain, shift_first, down_bias, second_norm_gain, second_norm_shift], axis=1
    )
    vectors = jnp.pad(jnp.concatenate(split3(vectors), axis=1), ((0, 0), (0, 110)))
    extra = jnp.concatenate(
        [by_col(cotangent), jnp.broadcast_to(vectors[None], (NCOL, 48, 128))], axis=1
    )
    bias3 = joint_bias.reshape(3, 2, HDIM)
    bias = jnp.concatenate(
        [
            bias3[:, 0].reshape(192),
            jnp.zeros((64,), F32),
            jnp.concatenate([jnp.zeros((3, HDIM), F32), bias3[:, 1]], axis=1).reshape(384),
        ]
    ).reshape(1, JW)
    bias_rows = jnp.pad(jnp.concatenate([v.reshape(4, 192) for v in split3(up_bias)]), ((0, 4), (0, 0)))
    seg_k = jnp.transpose(segments.reshape(NROW, NCOL, TOK), (1, 0, 2))
    seg_rows = jnp.pad(seg_k.reshape(NCOL, 512), ((0, 0), (0, 8)))
    seg_q = lax.dynamic_slice_in_dim(seg_rows, lax.rem(col, PER_HEAD) * SHARE, SHARE, 1)
    seg_q = seg_q.reshape(ROWS, 1)
    seg_a = seg_k[:, :HALF]
    seg_b = seg_k[:, HALF:]

    first, second = project(x4, wj, bias, extra)
    first = exchange(first, "col")
    second = exchange(second, "col")
    by_step = lambda s, n: s.reshape(NCOL // n, n * HALF, TOK)
    qa, o, o_blocks = attend(first, second, seg_q, by_step(seg_a, FWD_C), by_step(seg_b, FWD_C))

    att_r = to_row(exchange(o_blocks, "col"), bias_rows)
    att = exchange(att_r, "row")
    sent, d_att, fin, dh1 = tokenwise(att, x_t, second, everything)

    grad_o = exchange(to_col(exchange(d_att, "row")), "col")
    got = exchange(sent, "row")
    back_a, doa, turned_qd, acc = attend_back_first(first, grad_o, qa, o, fin, by_step(seg_a, BWD_C))
    back_a = exchange(back_a, "col")
    mine, other = weight_grads(core_word, got, att_r)
    theirs = swap_cores(other)
    acc, mine = lax.optimization_barrier((acc, mine))
    back_b = attend_back_second(qa, doa, turned_qd, acc, second, by_step(seg_b, BWD_C))
    back_b, theirs = lax.optimization_barrier((back_b, theirs))
    back_b = exchange(back_b, "col")
    wide = (mine.astype(F32) + theirs.astype(F32)).astype(BF)
    wide = exchange(wide, "col")

    din, mine_j, other_j = project_back(core_word, back_a, back_b, wj, x4)
    theirs_j = swap_cores(other_j)
    din = exchange(din, "row")
    mixed = exchange(last_payload(mine_j, theirs_j, din, dh1), "col")

    layer_output = jnp.transpose(back_a[:, 256:304], (1, 0, 2)).reshape(48, 2048)
    wide = pair(core, jnp.sum(wide.astype(F32), axis=0))
    as_cols = lambda v, n: jnp.transpose(v.reshape(n, 48, 128), (1, 0, 2)).reshape(48, n * 128)
    grad_up = as_cols(wide[0:288], 6)
    grad_down = as_cols(wide[288:576], 6)
    grad_out = as_cols(wide[576:672], 2)[:, :192].T
    vecs = (wide[672:720] + wide[720:768])[:42].reshape(7, DIM)
    own = lax.dynamic_slice_in_dim(vecs[:6], col * 48, 48, 1)
    grad_up_bias = vecs[6]

    grad_inputs = jnp.transpose(mixed[:, 128:].astype(F32), (1, 0, 2)).reshape(48, 2048)
    last = pair(core, jnp.sum(mixed[:, :128].astype(F32), axis=0))
    gj = as_cols(last[0:240], 5)
    gj_q = gj[:, :192].reshape(48, 3, 1, HDIM)
    gj_kv = gj[:, 256:].reshape(48, 3, 2, HDIM)
    grad_joint = jnp.concatenate([gj_q, gj_kv], axis=2).reshape(48, 576)
    bj = (last[240:245] + last[248:253]).reshape(JW)
    bj = jnp.concatenate([bj[:192].reshape(3, 1, HDIM), bj[256:].reshape(3, 2, HDIM)[:, 1:]], axis=1)
    grad_joint_bias = bj.reshape(384)

    return (
        layer_output,
        grad_inputs,
        grad_joint,
        grad_joint_bias,
        grad_out,
        own[5],
        own[0],
        own[1],
        grad_up,
        grad_up_bias,
        grad_down,
        own[4],
        own[2],
        own[3],
    )


def solution(mesh):
    grid = P("col", ("dp", "row"))
    block = P("col", "row")
    return jax.shard_map(
        per_device,
        mesh=mesh,
        in_specs=(
            grid, P("dp", None), block, P("row"), P("row", "col"), P("col"), P("col"), P("col"),
            block, P("row"), block, P("col"), P("col"), P("col"), grid,
        ),
        out_specs=(
            grid, grid, block, P("row"), P("row", "col"), P("col"), P("col"), P("col"),
            block, P("row"), block, P("col"), P("col"), P("col"),
        ),
        check_vma=False,
    )
```

```python
import math

import jax
import jax.numpy as jnp
from jax import lax
from jax.experimental import pallas as pl
from jax.experimental.pallas import tpu as pltpu
from jax.sharding import PartitionSpec as P

HDIM = 64
EPS = 1e-06
BLOCK_OUT = -1e30
LOG2E = 1.4426950408889634
BF = jnp.bfloat16
F32 = jnp.float32

DIM = 768
FF = 3072
NCOL = 16
NROW = 4
TOK = 128
PER_HEAD = 5
SHARE = 104
TAIL = SHARE - 64
ROWS = NCOL * SHARE
AUG = 144
JW = 640
HALF = 2
FWD_C = 2
BWD_C = 2
Q_AT = NROW * TOK
C_AT = Q_AT + 64
BLOCK = C_AT + 48
MIB = 2**20
COL = ("z", "y")
VMEM = pl.BlockSpec(memory_space=pltpu.VMEM)
SMEM = pl.BlockSpec(memory_space=pltpu.SMEM)
SENT = 3 * DIM + 48 + 2 * DIM
WROWS = 768


def split3(v):
    hi = v.astype(BF)
    rest = v - hi.astype(F32)
    mid = rest.astype(BF)
    low = (rest - mid.astype(F32)).astype(BF)
    return hi, mid, low


def dot(a, b, ca, cb):
    return lax.dot_general(a, b, (((ca,), (cb,)), ((), ())), preferred_element_type=F32)


def params(limit):
    return pltpu.CompilerParams(vmem_limit_bytes=limit * MIB)


def cost(us):
    return pl.CostEstimate(flops=int(us * 1e9), bytes_accessed=int(us * 2e6), transcendentals=0)


Q_BLOCK = pl.BlockSpec((NCOL, 64, 128), lambda i: (0, Q_AT // 64, 0))


def whole(shape):
    return pl.BlockSpec(shape, lambda i: (0,) * len(shape))


def project_kernel(x_ref, w_ref, b_ref, cot_ref, out_ref, q_ref):
    w = w_ref[...].reshape(DIM, JW)
    q_ref[...] = jnp.zeros_like(q_ref)
    for r in range(NROW):
        tokens = x_ref[r].astype(F32).T.astype(BF)
        y = dot(tokens, w, 1, 0) + b_ref[...]
        q_ref[r * TOK : (r + 1) * TOK, :] = y[:, 0:256]
        for h in range(3):
            kv = y[:, 256 + 128 * h : 384 + 128 * h].T.astype(BF)
            for j in range(PER_HEAD * h, PER_HEAD * (h + 1) + (1 if h == 2 else 0)):
                out_ref[j, r * TOK : (r + 1) * TOK, :] = kv
    for j in range(NCOL):
        h, k = min(j, 14) // PER_HEAD, min(j, 14) % PER_HEAD
        lanes = slice(HDIM * h, HDIM * (h + 1))
        a = q_ref[SHARE * k : SHARE * k + 64, lanes]
        b = q_ref[SHARE * k + 64 : SHARE * k + 128, lanes]
        out_ref[j, Q_AT:C_AT, :] = jnp.concatenate([a, b], axis=1).astype(BF)
    out_ref[:, C_AT:BLOCK, :] = cot_ref[...]


def project(x4, wj, bias, cot):
    return pl.pallas_call(
        project_kernel,
        out_shape=jax.ShapeDtypeStruct((NCOL, BLOCK, 128), BF),
        in_specs=[VMEM] * 4,
        out_specs=VMEM,
        scratch_shapes=[pltpu.VMEM((640, 256), F32)],
        compiler_params=params(40),
        cost_estimate=cost(3),
        name="project",
    )(x4, wj, bias, cot)


def key_rows(seg_row):
    row = lax.broadcasted_iota(jnp.int32, (16, seg_row.shape[1]), 0)
    hot = jnp.where(row < 5, jnp.where(row == seg_row, 1.0, 0.0), jnp.where(row < 8, 1.0, 0.0))
    return hot.astype(BF)


def offset_columns(value, base):
    h, m, l = split3(-value)
    lane = lax.broadcasted_iota(jnp.int32, base.shape, 1)
    return jnp.where(
        lane == 5,
        h.astype(F32),
        jnp.where(lane == 6, m.astype(F32), jnp.where(lane == 7, l.astype(F32), base)),
    )


def key_block(kv_refs, seg_ref):
    tiles = [
        ref[c, at : at + TOK, :]
        for c in range(kv_refs[0].shape[0])
        for ref in kv_refs
        for at in range(0, ref.shape[1], TOK)
    ]
    extra = [key_rows(seg_ref[0, i : i + 1, :]) for i in range(len(tiles))]
    return jnp.concatenate(tiles, axis=1), jnp.concatenate(extra, axis=1)


def unpack(block_ref, store):
    for c in range(NCOL):
        block = block_ref[c].astype(F32)
        store(SHARE * c, block[:, 0:64])
        store(SHARE * c + 64, block[0:TAIL, 64:128])


def forward_step(qa_ref, kv_ref, seg_ref, acc_ref, top_ref):
    kvt, extra = key_block([kv_ref], seg_ref)
    kt = jnp.concatenate([kvt[0:64], kvt[0:64], extra], axis=0)
    turned = kvt.astype(F32).T
    lane = lax.broadcasted_iota(jnp.int32, turned.shape, 1)
    va = jnp.where(lane >= 64, turned, jnp.where(lane == 0, 1.0, 0.0)).astype(BF)
    s = dot(qa_ref[...], kt, 1, 0)
    parts = [s[:, i * 128 : (i + 1) * 128] for i in range(s.shape[1] // 128)]
    high = parts[0]
    for part in parts[1:]:
        high = jnp.maximum(high, part)
    top = top_ref[...]
    raised = jnp.maximum(top, jnp.broadcast_to(jnp.max(high, axis=1, keepdims=True), top.shape))
    p = jnp.concatenate([jnp.exp2(part - raised).astype(BF) for part in parts], axis=1)
    fade = jnp.exp2(top - raised)
    top_ref[...] = raised
    acc_ref[...] = acc_ref[...] * fade + dot(p, va, 1, 0)


def attend_kernel(
    q_ref, kv_ref, segq_ref, seg_ref, qa_ref, o_ref, out_ref, q_scr, acc_ref, top_ref
):
    @pl.when(pl.program_id(0) == 0)
    def _():
        def store(at, rows):
            q_scr[at : at + rows.shape[0], :] = rows

        unpack(q_ref, store)
        scaled = q_scr[...] * (LOG2E / 8.0)
        hi = scaled.astype(BF)
        lo = (scaled - hi.astype(F32)).astype(BF)
        lane = lax.broadcasted_iota(jnp.int32, (ROWS, 16), 1)
        pen = jnp.where((lane < 5) & (lane != segq_ref[...]), BLOCK_OUT, 0.0)
        qa_ref[...] = jnp.concatenate([hi, lo, pen.astype(BF)], axis=1)
        acc_ref[...] = jnp.zeros_like(acc_ref)
        top_ref[...] = jnp.full_like(top_ref, -3e38)

    forward_step(qa_ref, kv_ref, seg_ref, acc_ref, top_ref)

    @pl.when(pl.program_id(0) == pl.num_programs(0) - 1)
    def _():
        acc = acc_ref[...]
        total = acc[:, 0:1]
        o_ref[...] = acc[:, 64:128] / total
        lse = top_ref[:, 0:1] + jnp.log(total) * LOG2E
        qa_ref[:, 128:144] = offset_columns(lse, qa_ref[:, 128:144].astype(F32)).astype(BF)
        for c in range(NCOL):
            out_ref[c] = pack(o_ref, SHARE * c)


def pack(ref, at, scale=None):
    a = ref[at : at + 64, 0:64]
    b = jnp.concatenate([ref[at + 64 : at + SHARE, 0:64], jnp.zeros((64 - TAIL, 64), F32)], axis=0)
    both = jnp.concatenate([a, b], axis=1)
    if scale is not None:
        both = both * scale
    return both.astype(BF)


def attend(arrived, segq, seg_k):
    seg = seg_k.reshape(NCOL // FWD_C, FWD_C * NROW, TOK)
    return pl.pallas_call(
        attend_kernel,
        grid=(NCOL // FWD_C,),
        out_shape=(
            jax.ShapeDtypeStruct((ROWS, AUG), BF),
            jax.ShapeDtypeStruct((ROWS, HDIM), F32),
            jax.ShapeDtypeStruct((NCOL, 64, 128), BF),
        ),
        in_specs=[
            Q_BLOCK,
            pl.BlockSpec((FWD_C, Q_AT, 128), lambda i: (i, 0, 0)),
            whole((ROWS, 1)),
            pl.BlockSpec((1, FWD_C * NROW, TOK), lambda i: (i, 0, 0)),
        ],
        out_specs=[whole((ROWS, AUG)), whole((ROWS, HDIM)), whole((NCOL, 64, 128))],
        scratch_shapes=[
            pltpu.VMEM((ROWS, HDIM), F32),
            pltpu.VMEM((ROWS, 128), F32),
            pltpu.VMEM((ROWS, 128), F32),
        ],
        compiler_params=params(60),
        cost_estimate=cost(20),
        name="attend",
    )(arrived, arrived, segq, seg)


def backward_step(qa_ref, doa_ref, turned_ref, kv_refs, seg_ref, acc_ref):
    kvt, extra = key_block(kv_refs, seg_ref)
    kt = jnp.concatenate([kvt[0:64], kvt[0:64], extra], axis=0)
    vt = jnp.concatenate([kvt[64:128], extra], axis=0)
    keys = kvt.astype(F32).T.astype(BF)
    p = jnp.exp2(dot(qa_ref[...], kt, 1, 0))
    dp = dot(doa_ref[...], vt, 1, 0)
    ds = (p * dp).astype(BF)
    acc_ref[...] += dot(ds, keys, 1, 0)
    dk = dot(turned_ref[0:64, :], ds, 1, 0) * 0.125
    dv = dot(turned_ref[64:128, :], p.astype(BF), 1, 0)
    return jnp.concatenate([dk, dv], axis=0).astype(BF)


def store_keys(out_ref, at, both):
    for c in range(BWD_C):
        for r in range(HALF):
            i = c * HALF + r
            out_ref[at + c, r * TOK : (r + 1) * TOK, :] = both[:, i * TOK : (i + 1) * TOK]


def back_first_kernel(
    q_ref, do_ref, qa_ref, o_ref, fin_ref, kv_ref, seg_ref, out_ref, doa_ref, turned_ref, acc_ref, pair_scr
):
    @pl.when(pl.program_id(0) == 0)
    def _():
        def store_q(at, rows):
            pair_scr[at : at + rows.shape[0], 0:64] = rows

        def store_do(at, rows):
            pair_scr[at : at + rows.shape[0], 64:128] = rows

        unpack(q_ref, store_q)
        unpack(do_ref, store_do)
        pairs = pair_scr[...]
        turned_ref[...] = pairs.T.astype(BF)
        grad = pairs[:, 64:128]
        delta = jnp.sum(grad * o_ref[...], axis=1, keepdims=True)
        ext = offset_columns(delta, jnp.zeros((ROWS, 16), F32))
        doa_ref[...] = jnp.concatenate([grad.astype(BF), ext.astype(BF)], axis=1)
        acc_ref[...] = jnp.zeros_like(acc_ref)

    both = backward_step(qa_ref, doa_ref, turned_ref, [kv_ref], seg_ref, acc_ref)
    store_keys(out_ref, 0, both)
    out_ref[:, 256:304, :] = fin_ref[...]


def back_second_kernel(
    qa_ref, doa_ref, turned_ref, acc_in, kv_ref, seg_ref, out_ref, acc_ref
):
    step = pl.program_id(0)

    @pl.when(step == 0)
    def _():
        acc_ref[...] = acc_in[...]

    both = backward_step(qa_ref, doa_ref, turned_ref, [kv_ref], seg_ref, acc_ref)
    store_keys(out_ref, step * BWD_C, both)

    @pl.when(step == pl.num_programs(0) - 1)
    def _():
        for c in range(NCOL):
            out_ref[c, 256:320, :] = pack(acc_ref, SHARE * c, 0.125)


SEG_BACK = pl.BlockSpec((1, BWD_C * HALF, TOK), lambda i: (i, 0, 0))
BACK_STEPS = NCOL // BWD_C


def attend_back_first(arrived, grad, qa, o, fin, seg_k):
    seg = seg_k[:, :HALF].reshape(BACK_STEPS, BWD_C * HALF, TOK)
    return pl.pallas_call(
        back_first_kernel,
        grid=(BACK_STEPS,),
        out_shape=(
            jax.ShapeDtypeStruct((NCOL, 304, 128), BF),
            jax.ShapeDtypeStruct((ROWS, 80), BF),
            jax.ShapeDtypeStruct((128, ROWS), BF),
            jax.ShapeDtypeStruct((ROWS, 128), F32),
        ),
        in_specs=[
            Q_BLOCK,
            whole((NCOL, 64, 128)),
            whole((ROWS, AUG)),
            whole((ROWS, HDIM)),
            pl.BlockSpec((BWD_C, 48, 128), lambda i: (i, 0, 0)),
            pl.BlockSpec((BWD_C, HALF * TOK, 128), lambda i: (i, 0, 0)),
            SEG_BACK,
        ],
        out_specs=[
            pl.BlockSpec((BWD_C, 304, 128), lambda i: (i, 0, 0)),
            whole((ROWS, 80)),
            whole((128, ROWS)),
            whole((ROWS, 128)),
        ],
        scratch_shapes=[pltpu.VMEM((ROWS, 128), F32)],
        compiler_params=params(58),
        cost_estimate=cost(18),
        name="attend_back_first",
    )(arrived, grad, qa, o, fin, arrived, seg)


def attend_back_second(qa, doa, turned, acc, arrived, seg_k):
    seg = seg_k[:, HALF:].reshape(BACK_STEPS, BWD_C * HALF, TOK)
    return pl.pallas_call(
        back_second_kernel,
        grid=(BACK_STEPS,),
        out_shape=jax.ShapeDtypeStruct((NCOL, 320, 128), BF),
        in_specs=[
            whole((ROWS, AUG)),
            whole((ROWS, 80)),
            whole((128, ROWS)),
            whole((ROWS, 128)),
            pl.BlockSpec((BWD_C, HALF * TOK, 128), lambda i: (i, 1, 0)),
            SEG_BACK,
        ],
        out_specs=whole((NCOL, 320, 128)),
        scratch_shapes=[pltpu.VMEM((ROWS, 128), F32)],
        compiler_params=params(58),
        cost_estimate=cost(18),
        name="attend_back_second",
    )(qa, doa, turned, acc, arrived, seg)


def gather_rows(block_ref, scr, rows=slice(0, 64)):
    for j in range(15):
        h, k = j // PER_HEAD, j % PER_HEAD
        block = block_ref[j, rows, :].astype(F32)
        lanes = slice(HDIM * h, HDIM * (h + 1))
        scr[SHARE * k : SHARE * k + 64, lanes] = block[:, 0:64]
        scr[SHARE * k + 64 : SHARE * (k + 1), lanes] = block[0:TAIL, 64:128]


def to_row_kernel(got_ref, bias_ref, out_ref, scr):
    gather_rows(got_ref, scr)
    for r in range(NROW):
        out_ref[r, 0:TOK, :] = scr[r * TOK : (r + 1) * TOK, :].astype(BF)
        out_ref[r, TOK : TOK + 16, :] = bias_ref[...]


def to_row(got, bias_rows):
    return pl.pallas_call(
        to_row_kernel,
        out_shape=jax.ShapeDtypeStruct((NROW, TOK + 16, 192), BF),
        in_specs=[VMEM] * 2,
        out_specs=VMEM,
        scratch_shapes=[pltpu.VMEM((528, 192), F32)],
        cost_estimate=cost(1),
        compiler_params=params(16),
        name="to_row",
    )(got, bias_rows)


def to_col_kernel(got_ref, out_ref, scr):
    scr[512:640, :] = jnp.zeros((128, 192), F32)
    for r in range(NROW):
        scr[r * TOK : (r + 1) * TOK, :] = got_ref[r].astype(F32)
    for j in range(15):
        h, k = j // PER_HEAD, j % PER_HEAD
        lanes = slice(HDIM * h, HDIM * (h + 1))
        a = scr[SHARE * k : SHARE * k + 64, lanes]
        b = scr[SHARE * k + 64 : SHARE * k + 128, lanes]
        out_ref[j] = jnp.concatenate([a, b], axis=1).astype(BF)
    out_ref[15] = jnp.zeros((64, 128), BF)


def to_col(got):
    return pl.pallas_call(
        to_col_kernel,
        out_shape=jax.ShapeDtypeStruct((NCOL, 64, 128), BF),
        in_specs=[VMEM],
        out_specs=VMEM,
        scratch_shapes=[pltpu.VMEM((640, 192), F32)],
        cost_estimate=cost(1),
        compiler_params=params(16),
        name="to_col",
    )(got)


def feature_mean(v):
    return jnp.sum(v, axis=1, keepdims=True) * (1.0 / DIM)


def tokenwise_kernel(
    row_ref, att_ref, x_ref, cot_ref, vec_ref, all_ref,
    sent_ref, datt_ref, fin_ref, dh1_ref,
    up_ref, down_ref, out_ref, slope_ref, sems,
):
    row = row_ref[0]
    copies = []
    for g in range(3):
        for k in range(2):
            for r in range(NROW):
                copies.append(
                    pltpu.make_async_copy(
                        all_ref.at[k, r, :, 96:112, g * 128 : (g + 1) * 128],
                        out_ref.at[k * NROW + r, :, 16 * g : 16 * (g + 1), :],
                        sems.at[0],
                    )
                )
    n_out = len(copies)
    for r in range(NROW):
        for k in range(2):
            lanes = slice(r * DIM + k * 384, r * DIM + (k + 1) * 384)
            copies.append(
                pltpu.make_async_copy(all_ref.at[k, r, :, 0:48, :], up_ref.at[:, :, lanes], sems.at[1 + r])
            )
    for r in range(NROW):
        for k in range(2):
            lanes = slice(r * DIM + k * 384, r * DIM + (k + 1) * 384)
            copies.append(
                pltpu.make_async_copy(all_ref.at[k, r, :, 48:96, :], down_ref.at[:, :, lanes], sems.at[5 + r])
            )
    for copy in copies:
        copy.start()

    def wait(group):
        chosen = copies[:n_out] if group == 0 else copies[n_out + 2 * (group - 1) : n_out + 2 * group]
        for copy in chosen:
            copy.wait()

    tok = x_ref[...].reshape(DIM, TOK).astype(F32).T
    cot = cot_ref[...].reshape(DIM, TOK).astype(F32).T
    vecs = vec_ref[...].reshape(DIM, TOK).astype(F32).T[64:128]
    out_b, gain_1, shift_1, down_b, gain_2, shift_2 = [
        vecs[i : i + 1] + vecs[6 + i : 7 + i] + vecs[12 + i : 13 + i] for i in range(6)
    ]
    gap = jnp.zeros((TOK, 32), BF)

    wait(0)
    attn = jnp.zeros((TOK, DIM), F32)
    for r in range(NROW):
        rows = att_ref[r, 0:TOK, :]
        for k in range(2):
            piece = jnp.concatenate([rows[:, 96 * k : 96 * (k + 1)], gap], axis=1)
            attn = attn + dot(piece, out_ref[k * NROW + r].reshape(DIM, 128), 1, 1)
    h1 = tok + (attn + out_b)
    off = h1 - feature_mean(h1)
    inv1 = lax.rsqrt(feature_mean(off * off) + EPS)
    xhat1 = off * inv1
    n1 = xhat1 * gain_1 + shift_1
    n1_low = n1.astype(BF)

    branch = jnp.zeros((TOK, DIM), F32)
    for r in range(NROW):
        wait(1 + r)
        cols = slice(r * DIM, (r + 1) * DIM)
        parts = att_ref[r, TOK : TOK + 12, :].astype(F32)
        parts = parts[0:4] + parts[4:8] + parts[8:12]
        up_b = jnp.concatenate([parts[i : i + 1] for i in range(4)], axis=1)
        pre = dot(n1_low, up_ref[:, :, cols].reshape(DIM, DIM), 1, 0) + up_b
        phi = 0.5 * (1.0 + lax.erf(pre * (1.0 / math.sqrt(2.0))))
        act = (pre * phi).astype(BF)
        slope_ref[:, cols] = phi + pre * jnp.exp(-0.5 * pre * pre) * (1.0 / math.sqrt(2.0 * math.pi))
        for i in range(6):
            at = 3 * DIM + 48 + DIM + i * TOK
            sent_ref[lax.rem(r + NROW - row, NROW), at : at + TOK, :] = act[:, i * TOK : (i + 1) * TOK]
        wait(5 + r)
        branch = branch + dot(act, down_ref[:, :, cols].reshape(DIM, DIM), 1, 1)
    h2 = n1 + (branch + down_b)
    off = h2 - feature_mean(h2)
    inv2 = lax.rsqrt(feature_mean(off * off) + EPS)
    xhat2 = off * inv2
    fin_ref[...] = (xhat2 * gain_2 + shift_2).T.astype(BF).reshape(NCOL, 48, TOK)
    dx = cot * gain_2
    dh2 = inv2 * (dx - feature_mean(dx) - xhat2 * feature_mean(dx * xhat2))
    d_branch = dh2.astype(BF)

    back = jnp.zeros((TOK, DIM), F32)
    for r in range(NROW):
        cols = slice(r * DIM, (r + 1) * DIM)
        d_act = dot(d_branch, down_ref[:, :, cols].reshape(DIM, DIM), 1, 0)
        d_pre = (d_act * slope_ref[:, cols]).astype(BF)
        for i in range(6):
            at = 3 * DIM + 48 + i * TOK
            sent_ref[lax.rem(r + NROW - row, NROW), at : at + TOK, :] = d_pre[:, i * TOK : (i + 1) * TOK]
        back = back + dot(d_pre, up_ref[:, :, cols].reshape(DIM, DIM), 1, 1)
    up1 = dh2 + back
    dx = up1 * gain_1
    dh1 = inv1 * (dx - feature_mean(dx) - xhat1 * feature_mean(dx * xhat1))
    d_attn = dh1.astype(BF)
    for r in range(NROW):
        pieces = [dot(d_attn, out_ref[k * NROW + r].reshape(DIM, 128), 1, 0)[:, 0:96] for k in range(2)]
        datt_ref[r] = jnp.concatenate(pieces, axis=1).astype(BF)
    turned = dh1.T
    dh1_ref[...] = turned
    shared = [n1.T.astype(BF), dh2.T.astype(BF), turned.astype(BF)]
    sums = [
        jnp.sum(v, axis=0, keepdims=True) for v in (up1 * xhat1, up1, cot * xhat2, cot)
    ]
    rows = []
    for part in range(2):
        for v in sums:
            hi = v.astype(BF).astype(F32)
            piece = hi if part == 0 else v - hi
            rows += [piece[:, i * 128 : (i + 1) * 128] for i in range(6)]
    shared.append(jnp.concatenate(rows, axis=0).astype(BF))
    at = 0
    for v in shared:
        for r in range(NROW):
            sent_ref[r, at : at + v.shape[0], :] = v
        at += v.shape[0]


def tokenwise(row, att, x_t, arrived, wj, everything):
    return pl.pallas_call(
        tokenwise_kernel,
        out_shape=(
            jax.ShapeDtypeStruct((NROW, SENT, TOK), BF),
            jax.ShapeDtypeStruct((NROW, TOK, 192), BF),
            jax.ShapeDtypeStruct((NCOL, 48, TOK), BF),
            jax.ShapeDtypeStruct((DIM, TOK), F32),
        ),
        grid=(1,),
        in_specs=[
            SMEM,
            whole((NROW, TOK + 16, 192)),
            whole((NCOL, 48, TOK)),
            pl.BlockSpec((NCOL, 48, TOK), lambda i: (0, C_AT // 48, 0)),
            pl.BlockSpec((NCOL, 48, TOK), lambda i: (0, 0, 1)),
            pl.BlockSpec(memory_space=pl.ANY),
        ],
        out_specs=[
            whole((NROW, SENT, TOK)),
            whole((NROW, TOK, 192)),
            whole((NCOL, 48, TOK)),
            whole((DIM, TOK)),
        ],
        scratch_shapes=[
            pltpu.VMEM((NCOL, 48, FF), BF),
            pltpu.VMEM((NCOL, 48, FF), BF),
            pltpu.VMEM((2 * NROW, NCOL, 48, 128), BF),
            pltpu.VMEM((TOK, FF), F32),
            pltpu.SemaphoreType.DMA((9,)),
        ],
        compiler_params=params(48),
        cost_estimate=cost(15),
        name="tokenwise",
    )(row, att, x_t, arrived, wj, everything)


def place(core, mine_ref, other_ref, blocks, half_rows):
    for at, block in blocks:
        low = at < half_rows
        local = at if low else at - half_rows
        rows = slice(local, local + block.shape[1])
        keep = core == (0 if low else 1)

        @pl.when(keep)
        def _():
            mine_ref[:, rows, :] = block

        @pl.when(jnp.logical_not(keep))
        def _():
            other_ref[:, rows, :] = block


def weight_grads_kernel(
    core_ref, row_ref, own_ref, got_1, got_2, got_3, att_ref, mine_ref, other_ref
):
    core, row = core_ref[0], row_ref[0]
    got_ref = [own_ref.at[0], got_1, got_2, got_3]
    source = [lax.rem(row + NROW - d, NROW) for d in range(NROW)]

    def feats(at):
        return jnp.concatenate([got_ref[r][at : at + DIM, :] for r in range(NROW)], axis=1)

    def hidden(at):
        return jnp.concatenate(
            [
                jnp.concatenate([got_ref[r][at + i * TOK : at + (i + 1) * TOK, :] for i in range(6)], axis=1)
                for r in range(NROW)
            ],
            axis=0,
        )

    def chunks(g, count):
        return [g[:, i * 128 : (i + 1) * 128].astype(BF).reshape(NCOL, 48, 128) for i in range(count)]

    ones = jnp.ones((16, NROW * TOK), BF)
    d_pre = hidden(3 * DIM + 48)
    d_branch = feats(DIM)
    d_attn = feats(2 * DIM)
    att = jnp.concatenate([att_ref[source[r], 0:TOK, :] for r in range(NROW)], axis=0)
    att = jnp.concatenate([att, jnp.zeros((NROW * TOK, 64), BF)], axis=1)
    pieces = chunks(dot(feats(0), d_pre, 1, 0), 6)
    pieces += chunks(dot(d_branch, hidden(4 * DIM + 48), 1, 0), 6)
    pieces += chunks(dot(d_attn, att, 1, 0), 2)
    sums = [dot(ones, d_branch, 1, 1)[0:1], dot(ones, d_attn, 1, 1)[0:1], dot(ones, d_pre, 1, 0)[0:1]]
    norm = got_ref[0][3 * DIM : 3 * DIM + 48, :].astype(F32)
    for r in range(1, NROW):
        norm = norm + got_ref[r][3 * DIM : 3 * DIM + 48, :].astype(F32)
    rows = [norm[0:24] + norm[24:48]]
    for v in sums:
        rows += [v[:, i * 128 : (i + 1) * 128] for i in range(6)]
    rows.append(jnp.zeros((6, 128), F32))
    rows = jnp.concatenate(rows, axis=0)
    hi = rows.astype(BF)
    lo = (rows - hi.astype(F32)).astype(BF)
    misc = jnp.concatenate([hi, lo], axis=0)
    blocks = [(48 * i, piece) for i, piece in enumerate(pieces)]
    blocks.append((672, jnp.broadcast_to(misc[None], (NCOL, 96, 128))))
    place(core, mine_ref, other_ref, blocks, WROWS // 2)


def weight_grads(core, row, sent, got, att):
    kind = jax.ShapeDtypeStruct((NCOL, WROWS // 2, 128), BF)
    return pl.pallas_call(
        weight_grads_kernel,
        out_shape=(kind, kind),
        grid=(1,),
        in_specs=[SMEM, SMEM, pl.BlockSpec((1, SENT, TOK), lambda i: (0, 0, 0))]
        + [whole((SENT, TOK))] * 3
        + [whole((NROW, TOK + 16, 192))],
        out_specs=[whole(kind.shape)] * 2,
        compiler_params=params(56),
        cost_estimate=cost(1),
        name="weight_grads",
    )(core, row, sent, *got, att)


def project_back_kernel(
    core_ref, first_ref, second_ref, w_ref, x_ref, din_ref, mine_ref, other_ref, scr
):
    core = core_ref[0]
    scr[...] = jnp.zeros_like(scr)
    gather_rows(second_ref, scr, slice(256, 320))
    dq = scr[0:512, :].T.astype(BF)
    w = w_ref[...].reshape(DIM, JW)
    grad = jnp.zeros((DIM, JW), F32)
    total = jnp.zeros((16, JW), F32)
    ones = jnp.ones((16, TOK), BF)
    for r in range(NROW):
        source, at = (first_ref, r) if r < HALF else (second_ref, r - HALF)
        parts = [dq[:, r * TOK : (r + 1) * TOK]]
        for h in range(3):
            acc = source[PER_HEAD * h, at * TOK : (at + 1) * TOK, :].astype(F32)
            for k in range(1, PER_HEAD):
                acc = acc + source[PER_HEAD * h + k, at * TOK : (at + 1) * TOK, :].astype(F32)
            parts.append(acc.astype(BF))
        d_proj = jnp.concatenate(parts, axis=0)
        din_ref[r] = dot(w, d_proj, 1, 0).astype(BF)
        grad = grad + dot(x_ref[r], d_proj, 1, 1)
        total = total + dot(ones, d_proj, 1, 1)
    rows = [total[0:1, i * 128 : (i + 1) * 128] for i in range(5)] + [jnp.zeros((3, 128), F32)]
    rows = jnp.concatenate(rows, axis=0)
    hi = rows.astype(BF)
    lo = (rows - hi.astype(F32)).astype(BF)
    misc = jnp.broadcast_to(jnp.concatenate([hi, lo], axis=0)[None], (NCOL, 16, 128))
    low = grad.astype(BF)
    pieces = [low[:, i * 128 : (i + 1) * 128].reshape(NCOL, 48, 128) for i in range(5)]
    blocks = [(0, pieces[0]), (48, pieces[1]), (96, pieces[2][:, 0:32]), (128, pieces[2][:, 32:48])]
    blocks += [(144, pieces[3]), (192, pieces[4]), (240, misc)]
    place(core, mine_ref, other_ref, blocks, 128)


def project_back(core, first, second, wj, x4):
    kind = jax.ShapeDtypeStruct((NCOL, 128, 128), BF)
    return pl.pallas_call(
        project_back_kernel,
        out_shape=(jax.ShapeDtypeStruct((NROW, DIM, TOK), BF), kind, kind),
        in_specs=[SMEM] + [VMEM] * 4,
        out_specs=[VMEM] * 3,
        scratch_shapes=[pltpu.VMEM((528, 256), F32)],
        compiler_params=params(48),
        cost_estimate=cost(5),
        name="project_back",
    )(core, first, second, wj, x4)


def last_kernel(mine_ref, theirs_ref, din_ref, dh1_ref, out_ref):
    out_ref[:, 0:128, :] = (mine_ref[...].astype(F32) + theirs_ref[...].astype(F32)).astype(BF)
    total = dh1_ref[...]
    for r in range(NROW):
        total = total + din_ref[r].astype(F32)
    out_ref[:, 128:176, :] = total.astype(BF).reshape(NCOL, 48, TOK)


def last_payload(mine, theirs, din, dh1):
    return pl.pallas_call(
        last_kernel,
        out_shape=jax.ShapeDtypeStruct((NCOL, 176, 128), BF),
        in_specs=[VMEM] * 4,
        out_specs=VMEM,
        compiler_params=params(24),
        cost_estimate=cost(1),
        name="last_payload",
    )(mine, theirs, din, dh1)


def exchange(blocks, axis):
    return lax.all_to_all(blocks, axis, 0, 0, tiled=True)


def around(v, axis, shift):
    return lax.ppermute(v, axis, [(i, (i + shift) % 4) for i in range(4)])


def swap_cores(v):
    return lax.ppermute(v, "dp", [(0, 1), (1, 0)])


def per_device(
    inputs,
    segments,
    joint_weight,
    joint_bias,
    output_weight,
    output_bias,
    first_norm_gain,
    shift_first,
    up_weight,
    up_bias,
    down_weight,
    down_bias,
    second_norm_gain,
    second_norm_shift,
    cotangent,
):
    core = lax.axis_index("dp")
    col = lax.axis_index(COL)
    row = lax.axis_index("row")
    my_y = lax.axis_index("y")
    core_word = core.reshape(1).astype(jnp.int32)
    row_word = row.reshape(1).astype(jnp.int32)

    def by_col(a):
        return jnp.transpose(a.reshape(48, NCOL, TOK), (1, 0, 2))

    blocks = by_col(inputs)
    blocks, up_weight, down_weight, output_weight = lax.optimization_barrier(
        (blocks, up_weight, down_weight, output_weight)
    )
    x_t = exchange(blocks, COL)
    vectors = jnp.stack(
        [output_bias, first_norm_gain, shift_first, down_bias, second_norm_gain, second_norm_shift], axis=1
    )
    vectors = jnp.pad(jnp.concatenate(split3(vectors), axis=1), ((0, 0), (0, 46)))
    jw = joint_weight.reshape(48, 3, 3, HDIM)
    jw = jnp.concatenate([jw[:, :, 0].reshape(48, 192), vectors, jw[:, :, 1:].reshape(48, 384)], axis=1)
    jw = jnp.broadcast_to(jw[None], (NCOL, 48, JW))
    x_t, jw = lax.optimization_barrier((x_t, jw))
    wj = exchange(jw, COL)
    x4 = lax.all_gather(x_t.reshape(DIM, TOK), "row", axis=0, tiled=False)

    turned = lax.dynamic_slice_in_dim(output_weight, core * 96, 96, 0).T
    turned = jnp.pad(turned, ((0, 0), (0, 32))).reshape(3, 16, 128)
    turned = jnp.transpose(turned, (1, 0, 2)).reshape(16, 384)
    shard = jnp.concatenate(
        [
            lax.dynamic_slice_in_dim(up_weight, core * 384, 384, 1),
            lax.dynamic_slice_in_dim(down_weight, core * 384, 384, 1),
            turned,
        ],
        axis=0,
    )
    everything = lax.all_gather(shard, ("dp", "row", "z", "y"), axis=0, tiled=False)
    everything = everything.reshape(2, NROW, NCOL, 112, 384)

    bias3 = joint_bias.reshape(3, 2, HDIM)
    bias = jnp.concatenate(
        [
            bias3[:, 0].reshape(192),
            jnp.zeros((64,), F32),
            jnp.concatenate([jnp.zeros((3, HDIM), F32), bias3[:, 1]], axis=1).reshape(384),
        ]
    ).reshape(1, JW)
    bias_rows = jnp.pad(jnp.concatenate([v.reshape(4, 192) for v in split3(up_bias)]), ((0, 4), (0, 0)))
    seg_k = jnp.transpose(segments.reshape(NROW, NCOL, TOK), (1, 0, 2))
    seg_rows = jnp.pad(seg_k.reshape(NCOL, 512), ((0, 0), (0, 8)))
    seg_q = lax.dynamic_slice_in_dim(seg_rows, lax.rem(col, PER_HEAD) * SHARE, SHARE, 1)
    seg_q = seg_q.reshape(ROWS, 1)

    arrived = exchange(project(x4, wj, bias, by_col(cotangent)), COL)
    qa, o, o_blocks = attend(arrived, seg_q, seg_k)

    att_r = to_row(exchange(o_blocks, COL), bias_rows)
    att = exchange(att_r, "row")
    sent, d_att, fin, dh1 = tokenwise(row_word, att, x_t, arrived, wj, everything)

    d_blocks = to_col(exchange(d_att, "row"))
    d_blocks, sent = lax.optimization_barrier((d_blocks, sent))
    grad_o = exchange(d_blocks, COL)
    got = [around(sent[d], "row", d) for d in range(1, NROW)]
    back_a, doa, turned_qd, acc = attend_back_first(arrived, grad_o, qa, o, fin, seg_k)
    back_b = attend_back_second(qa, doa, turned_qd, acc, arrived, seg_k)
    back_a = exchange(back_a, COL)
    late = lax.optimization_barrier((back_b, got, sent))
    got, sent = late[1:]
    mine, other = weight_grads(core_word, row_word, sent, got, att_r)
    theirs = swap_cores(other)
    back_b, back_a = lax.optimization_barrier((back_b, back_a))
    back_b = exchange(back_b, COL)
    wide = (mine.astype(F32) + theirs.astype(F32)).astype(BF).reshape(4, 4, WROWS // 2, 128)
    wide, back_b = lax.optimization_barrier((wide, back_b))
    wide = lax.psum_scatter(wide, "z", scatter_dimension=0, tiled=False)

    din, mine_j, other_j = project_back(core_word, back_a, back_b, wj, x4)
    theirs_j = swap_cores(other_j)
    din = exchange(din, "row")
    mixed = last_payload(mine_j, theirs_j, din, dh1)
    mixed, wide = lax.optimization_barrier((mixed, wide))
    mixed = exchange(mixed, COL)
    wide = lax.dynamic_index_in_dim(wide, my_y, 0, keepdims=False).astype(F32) + sum(
        around(lax.dynamic_index_in_dim(wide, lax.rem(my_y + d, 4), 0, keepdims=False), "y", d).astype(F32)
        for d in range(1, 4)
    )

    layer_output = jnp.transpose(back_a[:, 256:304], (1, 0, 2)).reshape(48, 2048)
    mixed, wide = lax.optimization_barrier((mixed, wide))
    mine = jnp.concatenate([wide, jnp.sum(mixed[:, :128].astype(F32), axis=0)], axis=0)
    theirs = swap_cores(mine)
    low = jnp.where(core == 0, mine, theirs)
    high = jnp.where(core == 0, theirs, mine)
    wide = jnp.concatenate([low[:384], high[:384]], axis=0)
    last = jnp.concatenate([low[384:], high[384:]], axis=0)
    as_cols = lambda v, n: jnp.transpose(v.reshape(n, 48, 128), (1, 0, 2)).reshape(48, n * 128)
    grad_up = as_cols(wide[0:288], 6)
    grad_down = as_cols(wide[288:576], 6)
    grad_out = as_cols(wide[576:672], 2)[:, :192].T
    vecs = (wide[672:720] + wide[720:768])[:42].reshape(7, DIM)
    own = lax.dynamic_slice_in_dim(vecs[:6], col * 48, 48, 1)
    grad_up_bias = vecs[6]
    grad_inputs = jnp.transpose(mixed[:, 128:].astype(F32), (1, 0, 2)).reshape(48, 2048)
    gj = as_cols(last[0:240], 5)
    gj_q = gj[:, :192].reshape(48, 3, 1, HDIM)
    gj_kv = gj[:, 256:].reshape(48, 3, 2, HDIM)
    grad_joint = jnp.concatenate([gj_q, gj_kv], axis=2).reshape(48, 576)
    bj = (last[240:245] + last[248:253]).reshape(JW)
    bj = jnp.concatenate([bj[:192].reshape(3, 1, HDIM), bj[256:].reshape(3, 2, HDIM)[:, 1:]], axis=1)
    grad_joint_bias = bj.reshape(384)

    return (
        layer_output,
        grad_inputs,
        grad_joint,
        grad_joint_bias,
        grad_out,
        own[5],
        own[0],
        own[1],
        grad_up,
        grad_up_bias,
        grad_down,
        own[4],
        own[2],
        own[3],
    )


def solution(mesh):
    sizes = (mesh.shape["dp"], mesh.shape["row"], 4, 4)
    fine = jax.sharding.Mesh(mesh.devices.reshape(sizes), ("dp", "row", "z", "y"))
    grid = P(COL, ("dp", "row"))
    block = P(COL, "row")
    return jax.shard_map(
        per_device,
        mesh=fine,
        in_specs=(
            grid, P("dp", None), block, P("row"), P("row", COL), P(COL), P(COL), P(COL),
            block, P("row"), block, P(COL), P(COL), P(COL), grid,
        ),
        out_specs=(
            grid, grid, block, P("row"), P("row", COL), P(COL), P(COL), P(COL),
            block, P("row"), block, P(COL), P(COL), P(COL),
        ),
        check_vma=False,
    )
```

```python
import math

import jax
import jax.numpy as jnp
from jax import lax
from jax.experimental import pallas as pl
from jax.experimental.pallas import tpu as pltpu
from jax.sharding import PartitionSpec as P

HDIM = 64
EPS = 1e-06
BLOCK_OUT = -1e30
LOG2E = 1.4426950408889634
BF = jnp.bfloat16
F32 = jnp.float32

DIM = 768
FF = 3072
NCOL = 16
NROW = 4
TOK = 128
PER_HEAD = 5
SHARE = 104
TAIL = SHARE - 64
ROWS = NCOL * SHARE
AUG = 144
JW = 640
HALF = 2
FWD_C = 2
BWD_C = 2
Q_AT = NROW * TOK
C_AT = Q_AT + 64
BLOCK = C_AT + 48
MIB = 2**20
COL = ("z", "y")
VMEM = pl.BlockSpec(memory_space=pltpu.VMEM)
SMEM = pl.BlockSpec(memory_space=pltpu.SMEM)
SENT = 3 * DIM + 48 + 2 * DIM
WROWS = 768


def split3(v):
    hi = v.astype(BF)
    rest = v - hi.astype(F32)
    mid = rest.astype(BF)
    low = (rest - mid.astype(F32)).astype(BF)
    return hi, mid, low


def dot(a, b, ca, cb):
    return lax.dot_general(a, b, (((ca,), (cb,)), ((), ())), preferred_element_type=F32)


LIMITS = {
    "project": 16,
    "attend": 32,
    "attend_back_first": 63,
    "attend_back_second": 63,
    "to_row": 8,
    "to_col": 8,
    "tokenwise": 63,
    "weight_grads": 63,
    "project_back": 20,
    "last_payload": 12,
    "finish": 12,
    "joint_gradient": 8,
}


def params(name):
    return pltpu.CompilerParams(vmem_limit_bytes=LIMITS[name] * MIB)


def cost(us):
    return pl.CostEstimate(flops=int(us * 1e9), bytes_accessed=int(us * 2e6), transcendentals=0)


Q_BLOCK = pl.BlockSpec((NCOL, 64, 128), lambda i: (0, Q_AT // 64, 0))


def whole(shape):
    return pl.BlockSpec(shape, lambda i: (0,) * len(shape))


def project_kernel(x_ref, w_ref, b_ref, cot_ref, out_ref, q_ref):
    w = w_ref[...].reshape(DIM, JW)
    q_ref[...] = jnp.zeros_like(q_ref)
    for r in range(NROW):
        tokens = x_ref[r].astype(F32).T.astype(BF)
        y = dot(tokens, w, 1, 0) + b_ref[...]
        q_ref[r * TOK : (r + 1) * TOK, :] = y[:, 0:256]
        for h in range(3):
            kv = y[:, 256 + 128 * h : 384 + 128 * h].T.astype(BF)
            for j in range(PER_HEAD * h, PER_HEAD * (h + 1) + (1 if h == 2 else 0)):
                out_ref[j, r * TOK : (r + 1) * TOK, :] = kv
    for j in range(NCOL):
        h, k = min(j, 14) // PER_HEAD, min(j, 14) % PER_HEAD
        lanes = slice(HDIM * h, HDIM * (h + 1))
        a = q_ref[SHARE * k : SHARE * k + 64, lanes]
        b = q_ref[SHARE * k + 64 : SHARE * k + 128, lanes]
        out_ref[j, Q_AT:C_AT, :] = jnp.concatenate([a, b], axis=1).astype(BF)
    out_ref[:, C_AT:BLOCK, :] = cot_ref[...]


def project(x4, wj, bias, cot):
    return pl.pallas_call(
        project_kernel,
        out_shape=pltpu.HBM((NCOL, BLOCK, 128), BF),
        in_specs=[VMEM] * 4,
        out_specs=VMEM,
        scratch_shapes=[pltpu.VMEM((640, 256), F32)],
        compiler_params=params("project"),
        cost_estimate=cost(3),
        name="project",
    )(x4, wj, bias, cot)


def key_rows(seg_row):
    row = lax.broadcasted_iota(jnp.int32, (16, seg_row.shape[1]), 0)
    hot = jnp.where(row < 5, jnp.where(row == seg_row, 1.0, 0.0), jnp.where(row < 8, 1.0, 0.0))
    return hot.astype(BF)


def offset_columns(value, base):
    h, m, l = split3(-value)
    lane = lax.broadcasted_iota(jnp.int32, base.shape, 1)
    return jnp.where(
        lane == 5,
        h.astype(F32),
        jnp.where(lane == 6, m.astype(F32), jnp.where(lane == 7, l.astype(F32), base)),
    )


def key_block(kv_refs, seg_ref):
    tiles = [
        ref[c, at : at + TOK, :]
        for c in range(kv_refs[0].shape[0])
        for ref in kv_refs
        for at in range(0, ref.shape[1], TOK)
    ]
    extra = [key_rows(seg_ref[0, i : i + 1, :]) for i in range(len(tiles))]
    return jnp.concatenate(tiles, axis=1), jnp.concatenate(extra, axis=1)


def unpack(block_ref, store):
    for c in range(NCOL):
        block = block_ref[c].astype(F32)
        store(SHARE * c, block[:, 0:64])
        store(SHARE * c + 64, block[0:TAIL, 64:128])


def forward_step(qa_ref, kv_ref, seg_ref, acc_ref, top_ref):
    kvt, extra = key_block([kv_ref], seg_ref)
    kt = jnp.concatenate([kvt[0:64], kvt[0:64], extra], axis=0)
    turned = kvt.astype(F32).T
    lane = lax.broadcasted_iota(jnp.int32, turned.shape, 1)
    va = jnp.where(lane >= 64, turned, jnp.where(lane == 0, 1.0, 0.0)).astype(BF)
    s = dot(qa_ref[...], kt, 1, 0)
    parts = [s[:, i * 128 : (i + 1) * 128] for i in range(s.shape[1] // 128)]
    high = parts[0]
    for part in parts[1:]:
        high = jnp.maximum(high, part)
    top = top_ref[...]
    raised = jnp.maximum(top, jnp.broadcast_to(jnp.max(high, axis=1, keepdims=True), top.shape))
    p = jnp.concatenate([jnp.exp2(part - raised).astype(BF) for part in parts], axis=1)
    fade = jnp.exp2(top - raised)
    top_ref[...] = raised
    acc_ref[...] = acc_ref[...] * fade + dot(p, va, 1, 0)


def attend_kernel(
    q_ref, kv_ref, segq_ref, seg_ref, qa_ref, o_ref, out_ref, q_scr, acc_ref, top_ref
):
    @pl.when(pl.program_id(0) == 0)
    def _():
        def store(at, rows):
            q_scr[at : at + rows.shape[0], :] = rows

        unpack(q_ref, store)
        scaled = q_scr[...] * (LOG2E / 8.0)
        hi = scaled.astype(BF)
        lo = (scaled - hi.astype(F32)).astype(BF)
        lane = lax.broadcasted_iota(jnp.int32, (ROWS, 16), 1)
        pen = jnp.where((lane < 5) & (lane != segq_ref[...]), BLOCK_OUT, 0.0)
        qa_ref[...] = jnp.concatenate([hi, lo, pen.astype(BF)], axis=1)
        acc_ref[...] = jnp.zeros_like(acc_ref)
        top_ref[...] = jnp.full_like(top_ref, -3e38)

    forward_step(qa_ref, kv_ref, seg_ref, acc_ref, top_ref)

    @pl.when(pl.program_id(0) == pl.num_programs(0) - 1)
    def _():
        acc = acc_ref[...]
        total = acc[:, 0:1]
        o_ref[...] = acc[:, 64:128] / total
        lse = top_ref[:, 0:1] + jnp.log(total) * LOG2E
        qa_ref[:, 128:144] = offset_columns(lse, qa_ref[:, 128:144].astype(F32)).astype(BF)
        for c in range(NCOL):
            out_ref[c] = pack(o_ref, SHARE * c)


def pack(ref, at, scale=None):
    a = ref[at : at + 64, 0:64]
    b = jnp.concatenate([ref[at + 64 : at + SHARE, 0:64], jnp.zeros((64 - TAIL, 64), F32)], axis=0)
    both = jnp.concatenate([a, b], axis=1)
    if scale is not None:
        both = both * scale
    return both.astype(BF)


def attend(arrived, segq, seg_k):
    seg = seg_k.reshape(NCOL // FWD_C, FWD_C * NROW, TOK)
    return pl.pallas_call(
        attend_kernel,
        grid=(NCOL // FWD_C,),
        out_shape=(
            pltpu.HBM((ROWS, AUG), BF),
            pltpu.HBM((ROWS, HDIM), F32),
            pltpu.HBM((NCOL, 64, 128), BF),
        ),
        in_specs=[
            Q_BLOCK,
            pl.BlockSpec((FWD_C, Q_AT, 128), lambda i: (i, 0, 0)),
            whole((ROWS, 1)),
            pl.BlockSpec((1, FWD_C * NROW, TOK), lambda i: (i, 0, 0)),
        ],
        out_specs=[whole((ROWS, AUG)), whole((ROWS, HDIM)), whole((NCOL, 64, 128))],
        scratch_shapes=[
            pltpu.VMEM((ROWS, HDIM), F32),
            pltpu.VMEM((ROWS, 128), F32),
            pltpu.VMEM((ROWS, 128), F32),
        ],
        compiler_params=params("attend"),
        cost_estimate=cost(20),
        name="attend",
    )(arrived, arrived, segq, seg)


def backward_step(qa_ref, doa_ref, turned_ref, kv_refs, seg_ref, acc_ref):
    kvt, extra = key_block(kv_refs, seg_ref)
    kt = jnp.concatenate([kvt[0:64], kvt[0:64], extra], axis=0)
    vt = jnp.concatenate([kvt[64:128], extra], axis=0)
    keys = kvt.astype(F32).T.astype(BF)
    p = jnp.exp2(dot(qa_ref[...], kt, 1, 0))
    dp = dot(doa_ref[...], vt, 1, 0)
    ds = (p * dp).astype(BF)
    acc_ref[...] += dot(ds, keys, 1, 0)
    dk = dot(turned_ref[0:64, :], ds, 1, 0) * 0.125
    dv = dot(turned_ref[64:128, :], p.astype(BF), 1, 0)
    return jnp.concatenate([dk, dv], axis=0).astype(BF)


def store_keys(out_ref, at, both):
    for c in range(BWD_C):
        for r in range(HALF):
            i = c * HALF + r
            out_ref[at + c, r * TOK : (r + 1) * TOK, :] = both[:, i * TOK : (i + 1) * TOK]


def back_first_kernel(
    q_ref, do_ref, qa_ref, o_ref, fin_ref, kv_ref, seg_ref, out_ref, doa_ref, turned_ref, acc_ref, pair_scr
):
    @pl.when(pl.program_id(0) == 0)
    def _():
        def store_q(at, rows):
            pair_scr[at : at + rows.shape[0], 0:64] = rows

        def store_do(at, rows):
            pair_scr[at : at + rows.shape[0], 64:128] = rows

        unpack(q_ref, store_q)
        unpack(do_ref, store_do)
        pairs = pair_scr[...]
        turned_ref[...] = pairs.T.astype(BF)
        grad = pairs[:, 64:128]
        delta = jnp.sum(grad * o_ref[...], axis=1, keepdims=True)
        ext = offset_columns(delta, jnp.zeros((ROWS, 16), F32))
        doa_ref[...] = jnp.concatenate([grad.astype(BF), ext.astype(BF)], axis=1)
        acc_ref[...] = jnp.zeros_like(acc_ref)

    both = backward_step(qa_ref, doa_ref, turned_ref, [kv_ref], seg_ref, acc_ref)
    store_keys(out_ref, 0, both)
    out_ref[:, 256:304, :] = fin_ref[...]


def back_second_kernel(
    qa_ref, doa_ref, turned_ref, acc_in, kv_ref, seg_ref, out_ref, acc_ref
):
    step = pl.program_id(0)

    @pl.when(step == 0)
    def _():
        acc_ref[...] = acc_in[...]

    both = backward_step(qa_ref, doa_ref, turned_ref, [kv_ref], seg_ref, acc_ref)
    store_keys(out_ref, step * BWD_C, both)

    @pl.when(step == pl.num_programs(0) - 1)
    def _():
        for c in range(NCOL):
            out_ref[c, 256:320, :] = pack(acc_ref, SHARE * c, 0.125)


SEG_BACK = pl.BlockSpec((1, BWD_C * HALF, TOK), lambda i: (i, 0, 0))
BACK_STEPS = NCOL // BWD_C


def attend_back_first(arrived, grad, qa, o, fin, seg_k):
    seg = seg_k[:, :HALF].reshape(BACK_STEPS, BWD_C * HALF, TOK)
    return pl.pallas_call(
        back_first_kernel,
        grid=(BACK_STEPS,),
        out_shape=(
            pltpu.HBM((NCOL, 304, 128), BF),
            pltpu.HBM((ROWS, 80), BF),
            pltpu.HBM((128, ROWS), BF),
            pltpu.HBM((ROWS, 128), F32),
        ),
        in_specs=[
            Q_BLOCK,
            whole((NCOL, 64, 128)),
            whole((ROWS, AUG)),
            whole((ROWS, HDIM)),
            pl.BlockSpec((BWD_C, 48, 128), lambda i: (i, 0, 0)),
            pl.BlockSpec((BWD_C, HALF * TOK, 128), lambda i: (i, 0, 0)),
            SEG_BACK,
        ],
        out_specs=[
            pl.BlockSpec((BWD_C, 304, 128), lambda i: (i, 0, 0)),
            whole((ROWS, 80)),
            whole((128, ROWS)),
            whole((ROWS, 128)),
        ],
        scratch_shapes=[pltpu.VMEM((ROWS, 128), F32)],
        compiler_params=params("attend_back_first"),
        cost_estimate=cost(18),
        name="attend_back_first",
    )(arrived, grad, qa, o, fin, arrived, seg)


def attend_back_second(qa, doa, turned, acc, arrived, seg_k):
    seg = seg_k[:, HALF:].reshape(BACK_STEPS, BWD_C * HALF, TOK)
    return pl.pallas_call(
        back_second_kernel,
        grid=(BACK_STEPS,),
        out_shape=pltpu.HBM((NCOL, 320, 128), BF),
        in_specs=[
            whole((ROWS, AUG)),
            whole((ROWS, 80)),
            whole((128, ROWS)),
            whole((ROWS, 128)),
            pl.BlockSpec((BWD_C, HALF * TOK, 128), lambda i: (i, 1, 0)),
            SEG_BACK,
        ],
        out_specs=whole((NCOL, 320, 128)),
        scratch_shapes=[pltpu.VMEM((ROWS, 128), F32)],
        compiler_params=params("attend_back_second"),
        cost_estimate=cost(18),
        name="attend_back_second",
    )(qa, doa, turned, acc, arrived, seg)


def gather_rows(block_ref, scr, rows=slice(0, 64)):
    for j in range(15):
        h, k = j // PER_HEAD, j % PER_HEAD
        block = block_ref[j, rows, :].astype(F32)
        lanes = slice(HDIM * h, HDIM * (h + 1))
        scr[SHARE * k : SHARE * k + 64, lanes] = block[:, 0:64]
        scr[SHARE * k + 64 : SHARE * (k + 1), lanes] = block[0:TAIL, 64:128]


def heads_of(block):
    return jnp.concatenate(
        [
            jnp.concatenate([block[64 * h : 64 * (h + 1), 64 * k : 64 * (k + 1)] for h in range(3)], axis=1)
            for k in range(2)
        ],
        axis=0,
    )


def to_row_kernel(got_ref, bias_ref, out_ref, scr):
    gather_rows(got_ref, scr)
    for r in range(NROW):
        for h in range(3):
            lanes = slice(HDIM * h, HDIM * (h + 1))
            a = scr[r * TOK : r * TOK + 64, lanes]
            b = scr[r * TOK + 64 : (r + 1) * TOK, lanes]
            out_ref[r, 64 * h : 64 * (h + 1), :] = jnp.concatenate([a, b], axis=1).astype(BF)
        out_ref[r, 192:224, :] = bias_ref[...]


def to_row(got, bias_rows):
    return pl.pallas_call(
        to_row_kernel,
        out_shape=pltpu.HBM((NROW, 224, TOK), BF),
        in_specs=[VMEM] * 2,
        out_specs=VMEM,
        scratch_shapes=[pltpu.VMEM((528, 192), F32)],
        cost_estimate=cost(1),
        compiler_params=params("to_row"),
        name="to_row",
    )(got, bias_rows)


def to_col_kernel(got_ref, out_ref, scr):
    scr[512:640, :] = jnp.zeros((128, 192), F32)
    for r in range(NROW):
        scr[r * TOK : (r + 1) * TOK, :] = heads_of(got_ref[r].astype(F32))
    for j in range(15):
        h, k = j // PER_HEAD, j % PER_HEAD
        lanes = slice(HDIM * h, HDIM * (h + 1))
        a = scr[SHARE * k : SHARE * k + 64, lanes]
        b = scr[SHARE * k + 64 : SHARE * k + 128, lanes]
        out_ref[j] = jnp.concatenate([a, b], axis=1).astype(BF)
    out_ref[15] = jnp.zeros((64, 128), BF)


def to_col(got):
    return pl.pallas_call(
        to_col_kernel,
        out_shape=pltpu.HBM((NCOL, 64, 128), BF),
        in_specs=[VMEM],
        out_specs=VMEM,
        scratch_shapes=[pltpu.VMEM((640, 192), F32)],
        cost_estimate=cost(1),
        compiler_params=params("to_col"),
        name="to_col",
    )(got)


def feature_mean(v):
    return jnp.sum(v, axis=1, keepdims=True) * (1.0 / DIM)


def tokenwise_kernel(
    row_ref, att_ref, x_ref, cot_ref, vec_ref, all_ref,
    sent_ref, datt_ref, fin_ref, dh1_ref,
    up_ref, down_ref, out_ref, slope_ref, sems,
):
    row = row_ref[0]
    copies = []
    for g in range(3):
        for k in range(2):
            for r in range(NROW):
                copies.append(
                    pltpu.make_async_copy(
                        all_ref.at[k, r, :, 96:112, g * 128 : (g + 1) * 128],
                        out_ref.at[k * NROW + r, :, 16 * g : 16 * (g + 1), :],
                        sems.at[0],
                    )
                )
    n_out = len(copies)
    for r in range(NROW):
        for k in range(2):
            lanes = slice(r * DIM + k * 384, r * DIM + (k + 1) * 384)
            copies.append(
                pltpu.make_async_copy(all_ref.at[k, r, :, 0:48, :], up_ref.at[:, :, lanes], sems.at[1 + r])
            )
    for r in range(NROW):
        for k in range(2):
            lanes = slice(r * DIM + k * 384, r * DIM + (k + 1) * 384)
            copies.append(
                pltpu.make_async_copy(all_ref.at[k, r, :, 48:96, :], down_ref.at[:, :, lanes], sems.at[5 + r])
            )
    for copy in copies:
        copy.start()

    def wait(group):
        chosen = copies[:n_out] if group == 0 else copies[n_out + 2 * (group - 1) : n_out + 2 * group]
        for copy in chosen:
            copy.wait()

    tok = x_ref[...].reshape(DIM, TOK).astype(F32).T
    cot = cot_ref[...].reshape(DIM, TOK).astype(F32).T
    vecs = vec_ref[...].reshape(DIM, TOK).astype(F32).T[64:128]
    out_b, gain_1, shift_1, down_b, gain_2, shift_2 = [
        vecs[i : i + 1] + vecs[6 + i : 7 + i] + vecs[12 + i : 13 + i] for i in range(6)
    ]
    gap = jnp.zeros((TOK, 32), BF)

    wait(0)
    attn = jnp.zeros((TOK, DIM), F32)
    for r in range(NROW):
        rows = heads_of(att_ref[r, 0:192, :].astype(F32)).astype(BF)
        for k in range(2):
            piece = jnp.concatenate([rows[:, 96 * k : 96 * (k + 1)], gap], axis=1)
            attn = attn + dot(piece, out_ref[k * NROW + r].reshape(DIM, 128), 1, 1)
    h1 = tok + (attn + out_b)
    off = h1 - feature_mean(h1)
    inv1 = lax.rsqrt(feature_mean(off * off) + EPS)
    xhat1 = off * inv1
    n1 = xhat1 * gain_1 + shift_1
    n1_low = n1.astype(BF)

    branch = jnp.zeros((TOK, DIM), F32)
    for r in range(NROW):
        wait(1 + r)
        cols = slice(r * DIM, (r + 1) * DIM)
        parts = att_ref[r, 192:224, :].astype(F32)
        parts = parts[0:6] + parts[6:12] + parts[12:18]
        up_b = jnp.concatenate([parts[i : i + 1] for i in range(6)], axis=1)
        pre = dot(n1_low, up_ref[:, :, cols].reshape(DIM, DIM), 1, 0) + up_b
        phi = 0.5 * (1.0 + lax.erf(pre * (1.0 / math.sqrt(2.0))))
        act = (pre * phi).astype(BF)
        slope_ref[:, cols] = phi + pre * jnp.exp(-0.5 * pre * pre) * (1.0 / math.sqrt(2.0 * math.pi))
        for i in range(6):
            at = 3 * DIM + 48 + DIM + i * TOK
            sent_ref[lax.rem(r + NROW - row, NROW), at : at + TOK, :] = act[:, i * TOK : (i + 1) * TOK]
        wait(5 + r)
        branch = branch + dot(act, down_ref[:, :, cols].reshape(DIM, DIM), 1, 1)
    h2 = n1 + (branch + down_b)
    off = h2 - feature_mean(h2)
    inv2 = lax.rsqrt(feature_mean(off * off) + EPS)
    xhat2 = off * inv2
    fin_ref[...] = (xhat2 * gain_2 + shift_2).T.astype(BF).reshape(NCOL, 48, TOK)
    dx = cot * gain_2
    dh2 = inv2 * (dx - feature_mean(dx) - xhat2 * feature_mean(dx * xhat2))
    d_branch = dh2.astype(BF)

    back = jnp.zeros((TOK, DIM), F32)
    for r in range(NROW):
        cols = slice(r * DIM, (r + 1) * DIM)
        d_act = dot(d_branch, down_ref[:, :, cols].reshape(DIM, DIM), 1, 0)
        d_pre = (d_act * slope_ref[:, cols]).astype(BF)
        for i in range(6):
            at = 3 * DIM + 48 + i * TOK
            sent_ref[lax.rem(r + NROW - row, NROW), at : at + TOK, :] = d_pre[:, i * TOK : (i + 1) * TOK]
        back = back + dot(d_pre, up_ref[:, :, cols].reshape(DIM, DIM), 1, 1)
    up1 = dh2 + back
    dx = up1 * gain_1
    dh1 = inv1 * (dx - feature_mean(dx) - xhat1 * feature_mean(dx * xhat1))
    d_attn = dh1.astype(BF)
    for r in range(NROW):
        pieces = [dot(d_attn, out_ref[k * NROW + r].reshape(DIM, 128), 1, 0)[:, 0:96] for k in range(2)]
        piece = jnp.concatenate(pieces, axis=1)
        for h in range(3):
            lanes = slice(HDIM * h, HDIM * (h + 1))
            both = jnp.concatenate([piece[0:64, lanes], piece[64:128, lanes]], axis=1)
            datt_ref[r, 64 * h : 64 * (h + 1), :] = both.astype(BF)
    turned = dh1.T
    dh1_ref[...] = turned
    shared = [n1.T.astype(BF), dh2.T.astype(BF), turned.astype(BF)]
    sums = [
        jnp.sum(v, axis=0, keepdims=True) for v in (up1 * xhat1, up1, cot * xhat2, cot)
    ]
    rows = []
    for part in range(2):
        for v in sums:
            hi = v.astype(BF).astype(F32)
            piece = hi if part == 0 else v - hi
            rows += [piece[:, i * 128 : (i + 1) * 128] for i in range(6)]
    shared.append(jnp.concatenate(rows, axis=0).astype(BF))
    at = 0
    for v in shared:
        for r in range(NROW):
            sent_ref[r, at : at + v.shape[0], :] = v
        at += v.shape[0]


def tokenwise(row, att, x_t, arrived, wj, everything):
    return pl.pallas_call(
        tokenwise_kernel,
        out_shape=(
            pltpu.HBM((NROW, SENT, TOK), BF),
            pltpu.HBM((NROW, 192, TOK), BF),
            pltpu.HBM((NCOL, 48, TOK), BF),
            pltpu.HBM((DIM, TOK), F32),
        ),
        grid=(1,),
        in_specs=[
            SMEM,
            whole((NROW, 224, TOK)),
            whole((NCOL, 48, TOK)),
            pl.BlockSpec((NCOL, 48, TOK), lambda i: (0, C_AT // 48, 0)),
            pl.BlockSpec((NCOL, 48, TOK), lambda i: (0, 0, 1)),
            pl.BlockSpec(memory_space=pl.ANY),
        ],
        out_specs=[
            whole((NROW, SENT, TOK)),
            whole((NROW, 192, TOK)),
            whole((NCOL, 48, TOK)),
            whole((DIM, TOK)),
        ],
        scratch_shapes=[
            pltpu.VMEM((NCOL, 48, FF), BF),
            pltpu.VMEM((NCOL, 48, FF), BF),
            pltpu.VMEM((2 * NROW, NCOL, 48, 128), BF),
            pltpu.VMEM((TOK, FF), F32),
            pltpu.SemaphoreType.DMA((9,)),
        ],
        compiler_params=params("tokenwise"),
        cost_estimate=cost(15),
        name="tokenwise",
    )(row, att, x_t, arrived, wj, everything)


def place(core, mine_ref, other_ref, blocks, half_rows):
    for at, block in blocks:
        low = at < half_rows
        local = at if low else at - half_rows
        rows = slice(local, local + block.shape[1])
        keep = core == (0 if low else 1)

        @pl.when(keep)
        def _():
            mine_ref[:, rows, :] = block

        @pl.when(jnp.logical_not(keep))
        def _():
            other_ref[:, rows, :] = block


def weight_grads_kernel(
    core_ref, row_ref, own_ref, got_1, got_2, got_3, att_ref, mine_ref, other_ref
):
    core, row = core_ref[0], row_ref[0]
    got_ref = [own_ref.at[0], got_1, got_2, got_3]
    source = [lax.rem(row + NROW - d, NROW) for d in range(NROW)]

    def feats(at):
        return jnp.concatenate([got_ref[r][at : at + DIM, :] for r in range(NROW)], axis=1)

    def hidden(at):
        return jnp.concatenate(
            [
                jnp.concatenate([got_ref[r][at + i * TOK : at + (i + 1) * TOK, :] for i in range(6)], axis=1)
                for r in range(NROW)
            ],
            axis=0,
        )

    def chunks(g, count):
        return [g[:, i * 128 : (i + 1) * 128].astype(BF).reshape(NCOL, 48, 128) for i in range(count)]

    ones = jnp.ones((16, NROW * TOK), BF)
    d_pre = hidden(3 * DIM + 48)
    d_branch = feats(DIM)
    d_attn = feats(2 * DIM)
    att = jnp.concatenate([heads_of(att_ref[source[r], 0:192, :].astype(F32)).astype(BF) for r in range(NROW)], axis=0)
    att = jnp.concatenate([att, jnp.zeros((NROW * TOK, 64), BF)], axis=1)
    pieces = chunks(dot(feats(0), d_pre, 1, 0), 6)
    pieces += chunks(dot(d_branch, hidden(4 * DIM + 48), 1, 0), 6)
    pieces += chunks(dot(d_attn, att, 1, 0), 2)
    sums = [dot(ones, d_branch, 1, 1)[0:1], dot(ones, d_attn, 1, 1)[0:1], dot(ones, d_pre, 1, 0)[0:1]]
    norm = got_ref[0][3 * DIM : 3 * DIM + 48, :].astype(F32)
    for r in range(1, NROW):
        norm = norm + got_ref[r][3 * DIM : 3 * DIM + 48, :].astype(F32)
    rows = [norm[0:24] + norm[24:48]]
    for v in sums:
        rows += [v[:, i * 128 : (i + 1) * 128] for i in range(6)]
    rows.append(jnp.zeros((6, 128), F32))
    rows = jnp.concatenate(rows, axis=0)
    hi = rows.astype(BF)
    lo = (rows - hi.astype(F32)).astype(BF)
    misc = jnp.concatenate([hi, lo], axis=0)
    blocks = [(48 * i, piece) for i, piece in enumerate(pieces)]
    blocks.append((672, jnp.broadcast_to(misc[None], (NCOL, 96, 128))))
    place(core, mine_ref, other_ref, blocks, WROWS // 2)


def weight_grads(core, row, sent, got, att):
    kind = pltpu.HBM((NCOL, WROWS // 2, 128), BF)
    return pl.pallas_call(
        weight_grads_kernel,
        out_shape=(kind, kind),
        grid=(1,),
        in_specs=[SMEM, SMEM, pl.BlockSpec((1, SENT, TOK), lambda i: (0, 0, 0))]
        + [whole((SENT, TOK))] * 3
        + [whole((NROW, 224, TOK))],
        out_specs=[whole(kind.shape)] * 2,
        compiler_params=params("weight_grads"),
        cost_estimate=cost(1),
        name="weight_grads",
    )(core, row, sent, *got, att)


def project_back_kernel(
    core_ref, first_ref, second_ref, w_ref, x_ref, din_ref, mine_ref, other_ref, layer_ref, scr
):
    core = core_ref[0]
    layer_ref[...] = jnp.concatenate([first_ref[c, 256:304, :] for c in range(NCOL)], axis=1)
    scr[...] = jnp.zeros_like(scr)
    gather_rows(second_ref, scr, slice(256, 320))
    dq = scr[0:512, :].T.astype(BF)
    w = w_ref[...].reshape(DIM, JW)
    grad = jnp.zeros((DIM, JW), F32)
    total = jnp.zeros((16, JW), F32)
    ones = jnp.ones((16, TOK), BF)
    for r in range(NROW):
        source, at = (first_ref, r) if r < HALF else (second_ref, r - HALF)
        parts = [dq[:, r * TOK : (r + 1) * TOK]]
        for h in range(3):
            acc = source[PER_HEAD * h, at * TOK : (at + 1) * TOK, :].astype(F32)
            for k in range(1, PER_HEAD):
                acc = acc + source[PER_HEAD * h + k, at * TOK : (at + 1) * TOK, :].astype(F32)
            parts.append(acc.astype(BF))
        d_proj = jnp.concatenate(parts, axis=0)
        din_ref[r] = dot(w, d_proj, 1, 0).astype(BF)
        grad = grad + dot(x_ref[r], d_proj, 1, 1)
        total = total + dot(ones, d_proj, 1, 1)
    rows = [total[0:1, i * 128 : (i + 1) * 128] for i in range(5)] + [jnp.zeros((3, 128), F32)]
    rows = jnp.concatenate(rows, axis=0)
    hi = rows.astype(BF)
    lo = (rows - hi.astype(F32)).astype(BF)
    misc = jnp.broadcast_to(jnp.concatenate([hi, lo], axis=0)[None], (NCOL, 16, 128))
    low = grad.astype(BF)
    pieces = [low[:, i * 128 : (i + 1) * 128].reshape(NCOL, 48, 128) for i in range(5)]
    blocks = [(0, pieces[0]), (48, pieces[1]), (96, pieces[2][:, 0:32]), (128, pieces[2][:, 32:48])]
    blocks += [(144, pieces[3]), (192, pieces[4]), (240, misc)]
    place(core, mine_ref, other_ref, blocks, 128)


def project_back(core, first, second, wj, x4):
    kind = pltpu.HBM((NCOL, 128, 128), BF)
    return pl.pallas_call(
        project_back_kernel,
        out_shape=(
            pltpu.HBM((NROW, DIM, TOK), BF),
            kind,
            kind,
            pltpu.HBM((48, NCOL * TOK), BF),
        ),
        in_specs=[SMEM] + [VMEM] * 4,
        out_specs=[VMEM] * 4,
        scratch_shapes=[pltpu.VMEM((528, 256), F32)],
        compiler_params=params("project_back"),
        cost_estimate=cost(5),
        name="project_back",
    )(core, first, second, wj, x4)


def last_kernel(mine_ref, theirs_ref, din_ref, dh1_ref, out_ref):
    out_ref[:, 0:128, :] = (mine_ref[...].astype(F32) + theirs_ref[...].astype(F32)).astype(BF)
    total = dh1_ref[...]
    for r in range(NROW):
        total = total + din_ref[r].astype(F32)
    out_ref[:, 128:176, :] = total.astype(BF).reshape(NCOL, 48, TOK)


def last_payload(mine, theirs, din, dh1):
    return pl.pallas_call(
        last_kernel,
        out_shape=pltpu.HBM((NCOL, 176, 128), BF),
        in_specs=[VMEM] * 4,
        out_specs=VMEM,
        compiler_params=params("last_payload"),
        cost_estimate=cost(1),
        name="last_payload",
    )(mine, theirs, din, dh1)


def join(core_ref, mine, theirs):
    first = core_ref[0] == 0
    a, b = mine[...], theirs[...]
    return jnp.concatenate([jnp.where(first, a, b), jnp.where(first, b, a)], axis=0)


def finish_kernel(
    core_ref, col_ref, wide_ref, other_ref, out_ref, up_ref, up_bias_ref, down_ref, *own_refs
):
    wide = join(core_ref, wide_ref, other_ref)
    for i in range(6):
        lanes = slice(i * 128, (i + 1) * 128)
        up_ref[:, lanes] = wide[48 * i : 48 * (i + 1)]
        down_ref[:, lanes] = wide[288 + 48 * i : 288 + 48 * (i + 1)]
    out_ref[...] = jnp.concatenate([wide[576:624], wide[624:672, 0:64]], axis=1)
    vecs = wide[672:720] + wide[720:768]
    up_bias_ref[...] = vecs[36:42]
    rows = [
        jnp.concatenate([vecs[6 * v + i : 6 * v + i + 1] for i in range(6)], axis=1) for v in range(6)
    ]
    rows = jnp.concatenate(rows + [jnp.zeros((2, DIM), F32)], axis=0)
    feature = lax.broadcasted_iota(jnp.int32, (DIM, 48), 0)
    lane = lax.broadcasted_iota(jnp.int32, (DIM, 48), 1)
    pick = jnp.where(feature == col_ref[0] * 48 + lane, 1.0, 0.0).astype(BF)
    own = sum(dot(part, pick, 1, 0) for part in split3(rows))
    for v, ref in enumerate(own_refs):
        ref[...] = own[v : v + 1]


def finish(core, col, wide, other):
    shapes = [(48, 192), (48, DIM), (6, 128), (48, DIM)] + [(1, 48)] * 6
    return pl.pallas_call(
        finish_kernel,
        out_shape=[pltpu.HBM(shape, F32) for shape in shapes],
        in_specs=[SMEM] * 2 + [VMEM] * 2,
        out_specs=[VMEM] * len(shapes),
        compiler_params=params("finish"),
        cost_estimate=cost(1),
        name="finish",
    )(core, col, wide, other)


def joint_kernel(core_ref, last_ref, other_ref, joint_ref, joint_bias_ref):
    last = join(core_ref, last_ref, other_ref)
    chunks = [last[48 * i : 48 * (i + 1)] for i in range(5)]
    heads = [chunks[0][:, 0:64], chunks[0][:, 64:128], chunks[1][:, 0:64]]
    joint_ref[...] = jnp.concatenate([v for h in range(3) for v in (heads[h], chunks[2 + h])], axis=1)
    sums = last[240:248] + last[248:256]
    heads = [sums[0:1, 0:64], sums[0:1, 64:128], sums[1:2, 0:64]]
    joint_bias_ref[...] = jnp.concatenate(
        [jnp.concatenate([heads[h], sums[2 + h : 3 + h, 64:128]], axis=1) for h in range(3)], axis=0
    )


def joint_gradient(core, last, other):
    return pl.pallas_call(
        joint_kernel,
        out_shape=[pltpu.HBM(shape, F32) for shape in ((48, 576), (3, 128))],
        in_specs=[SMEM] + [VMEM] * 2,
        out_specs=[VMEM] * 2,
        compiler_params=params("joint_gradient"),
        cost_estimate=cost(1),
        name="joint_gradient",
    )(core, last, other)


def exchange(blocks, axis):
    return lax.all_to_all(blocks, axis, 0, 0, tiled=True)


def around(v, axis, shift):
    return lax.ppermute(v, axis, [(i, (i + shift) % 4) for i in range(4)])


def swap_cores(v):
    return lax.ppermute(v, "dp", [(0, 1), (1, 0)])


def per_device(
    inputs,
    segments,
    joint_weight,
    joint_bias,
    output_weight,
    output_bias,
    first_norm_gain,
    shift_first,
    up_weight,
    up_bias,
    down_weight,
    down_bias,
    second_norm_gain,
    second_norm_shift,
    cotangent,
):
    core = lax.axis_index("dp")
    col = lax.axis_index(COL)
    row = lax.axis_index("row")
    my_z, my_y = lax.axis_index("z"), lax.axis_index("y")
    core_word = core.reshape(1).astype(jnp.int32)
    row_word = row.reshape(1).astype(jnp.int32)

    def by_col(a):
        return jnp.transpose(a.reshape(48, NCOL, TOK), (1, 0, 2))

    blocks = by_col(inputs)
    blocks, up_weight, down_weight, output_weight = lax.optimization_barrier(
        (blocks, up_weight, down_weight, output_weight)
    )
    x_t = exchange(blocks, COL)
    vectors = jnp.stack(
        [output_bias, first_norm_gain, shift_first, down_bias, second_norm_gain, second_norm_shift], axis=1
    )
    vectors = jnp.pad(jnp.concatenate(split3(vectors), axis=1), ((0, 0), (0, 46)))
    jw = joint_weight.reshape(48, 3, 3, HDIM)
    jw = jnp.concatenate([jw[:, :, 0].reshape(48, 192), vectors, jw[:, :, 1:].reshape(48, 384)], axis=1)
    jw = jnp.broadcast_to(jw[None], (NCOL, 48, JW))
    x_t, jw = lax.optimization_barrier((x_t, jw))
    wj = exchange(jw, COL)
    x4 = lax.all_gather(x_t.reshape(DIM, TOK), "row", axis=0, tiled=False)

    turned = lax.dynamic_slice_in_dim(output_weight, core * 96, 96, 0).T
    turned = jnp.pad(turned, ((0, 0), (0, 32))).reshape(3, 16, 128)
    turned = jnp.transpose(turned, (1, 0, 2)).reshape(16, 384)
    shard = jnp.concatenate(
        [
            lax.dynamic_slice_in_dim(up_weight, core * 384, 384, 1),
            lax.dynamic_slice_in_dim(down_weight, core * 384, 384, 1),
            turned,
        ],
        axis=0,
    )
    everything = lax.all_gather(shard, ("dp", "row", "z", "y"), axis=0, tiled=False)
    everything = everything.reshape(2, NROW, NCOL, 112, 384)

    bias3 = joint_bias.reshape(3, 2, HDIM)
    bias = jnp.concatenate(
        [
            bias3[:, 0].reshape(192),
            jnp.zeros((64,), F32),
            jnp.concatenate([jnp.zeros((3, HDIM), F32), bias3[:, 1]], axis=1).reshape(384),
        ]
    ).reshape(1, JW)
    bias_rows = jnp.pad(jnp.concatenate([v.reshape(6, 128) for v in split3(up_bias)]), ((0, 14), (0, 0)))
    seg_k = jnp.transpose(segments.reshape(NROW, NCOL, TOK), (1, 0, 2))
    seg_rows = jnp.pad(seg_k.reshape(NCOL, 512), ((0, 0), (0, 8)))
    seg_q = lax.dynamic_slice_in_dim(seg_rows, lax.rem(col, PER_HEAD) * SHARE, SHARE, 1)
    seg_q = seg_q.reshape(ROWS, 1)

    arrived = exchange(project(x4, wj, bias, by_col(cotangent)), COL)
    qa, o, o_blocks = attend(arrived, seg_q, seg_k)

    att_r = to_row(exchange(o_blocks, COL), bias_rows)
    att = exchange(att_r, "row")
    sent, d_att, fin, dh1 = tokenwise(row_word, att, x_t, arrived, wj, everything)

    d_blocks = to_col(exchange(d_att, "row"))
    d_blocks, sent = lax.optimization_barrier((d_blocks, sent))
    grad_o = exchange(d_blocks, COL)
    got = [around(sent[d], "row", d) for d in range(1, NROW)]
    back_a, doa, turned_qd, acc = attend_back_first(arrived, grad_o, qa, o, fin, seg_k)
    back_b = attend_back_second(qa, doa, turned_qd, acc, arrived, seg_k)
    back_a = exchange(back_a, COL)
    back_b, got, sent, back_a = lax.optimization_barrier((back_b, got, sent, back_a))
    mine, other = weight_grads(core_word, row_word, sent, got, att_r)
    theirs = swap_cores(other)
    back_b, back_a = lax.optimization_barrier((back_b, back_a))
    back_b = exchange(back_b, COL)
    wide = (mine.astype(F32) + theirs.astype(F32)).astype(BF).reshape(4, 4, WROWS // 2, 128)
    near = [lax.dynamic_index_in_dim(wide, lax.rem(my_z + d, 4), 0, keepdims=False) for d in range(4)]
    near = [near[0]] + [around(near[d], "z", d) for d in range(1, 4)]
    wide = near[0].astype(F32) + near[1].astype(F32) + near[2].astype(F32) + near[3].astype(F32)
    wide = wide.astype(BF)

    din, mine_j, other_j, layer_output = project_back(core_word, back_a, back_b, wj, x4)
    theirs_j = swap_cores(other_j)
    din = exchange(din, "row")
    near = [lax.dynamic_index_in_dim(wide, lax.rem(my_y + d, 4), 0, keepdims=False) for d in range(4)]
    din, near = lax.optimization_barrier((din, near))
    near = [near[0]] + [around(near[d], "y", d) for d in range(1, 4)]
    mixed = exchange(last_payload(mine_j, theirs_j, din, dh1), COL)
    wide = near[0].astype(F32) + near[1].astype(F32) + near[2].astype(F32) + near[3].astype(F32)
    grad_out, grad_up, grad_up_bias, grad_down, *own = finish(
        core_word, col.reshape(1).astype(jnp.int32), wide, swap_cores(wide)
    )
    last = jnp.sum(mixed[:, :128].astype(F32), axis=0)
    grad_inputs = jnp.transpose(mixed[:, 128:].astype(F32), (1, 0, 2)).reshape(48, 2048)
    grad_joint, grad_joint_bias = joint_gradient(core_word, last, swap_cores(last))
    own = [v.reshape(48) for v in own]

    return (
        layer_output,
        grad_inputs,
        grad_joint,
        grad_joint_bias.reshape(384),
        grad_out.T,
        own[5],
        own[0],
        own[1],
        grad_up,
        grad_up_bias.reshape(768),
        grad_down,
        own[4],
        own[2],
        own[3],
    )


def solution(mesh):
    sizes = (mesh.shape["dp"], mesh.shape["row"], 4, 4)
    fine = jax.sharding.Mesh(mesh.devices.reshape(sizes), ("dp", "row", "z", "y"))
    grid = P(COL, ("dp", "row"))
    block = P(COL, "row")
    return jax.shard_map(
        per_device,
        mesh=fine,
        in_specs=(
            grid, P("dp", None), block, P("row"), P("row", COL), P(COL), P(COL), P(COL),
            block, P("row"), block, P(COL), P(COL), P(COL), grid,
        ),
        out_specs=(
            grid, grid, block, P("row"), P("row", COL), P(COL), P(COL), P(COL),
            block, P("row"), block, P(COL), P(COL), P(COL),
        ),
        check_vma=False,
    )
```

```python
import math

import jax
import jax.numpy as jnp
from jax import lax
from jax.experimental import pallas as pl
from jax.experimental.pallas import tpu as pltpu
from jax.sharding import PartitionSpec as P

HDIM = 64
EPS = 1e-06
BLOCK_OUT = -1e30
LOG2E = 1.4426950408889634
BF = jnp.bfloat16
F32 = jnp.float32

DIM = 768
FF = 3072
NCOL = 16
NROW = 4
TOK = 128
PER_HEAD = 5
SHARE = 26
SLOTS = NROW * NCOL
ROWS = SLOTS * SHARE
AUG = 144
JW = 640
HALF = 2
FWD_C = 2
BWD_C = 4
Q_AT = NROW * TOK
C_AT = Q_AT + 64
BLOCK = C_AT + 48
MIB = 2**20
COL = ("z", "y")
ALL = ("row", "z", "y")
VMEM = pl.BlockSpec(memory_space=pltpu.VMEM)
SMEM = pl.BlockSpec(memory_space=pltpu.SMEM)
A_AT = 5 * DIM + 48
SENT = A_AT + 192
WROWS = 768


def split3(v):
    hi = v.astype(BF)
    rest = v - hi.astype(F32)
    mid = rest.astype(BF)
    low = (rest - mid.astype(F32)).astype(BF)
    return hi, mid, low


def dot(a, b, ca, cb):
    return lax.dot_general(a, b, (((ca,), (cb,)), ((), ())), preferred_element_type=F32)


LIMITS = {
    "project": 16,
    "attend": 32,
    "attend_back_first": 63,
    "attend_back_second": 63,
    "tokenwise": 63,
    "weight_grads": 63,
    "project_back": 20,
    "last_payload": 12,
    "finish": 12,
    "joint_gradient": 8,
}


def params(name):
    return pltpu.CompilerParams(vmem_limit_bytes=LIMITS[name] * MIB)


def cost(us):
    return pl.CostEstimate(flops=int(us * 1e9), bytes_accessed=int(us * 2e6), transcendentals=0)


Q_BLOCK = pl.BlockSpec((NCOL, 64, 128), lambda i: (0, Q_AT // 64, 0))


def whole(shape):
    return pl.BlockSpec(shape, lambda i: (0,) * len(shape))


def pack(ref, at, lane, scale=None):
    lanes = slice(lane, lane + HDIM)
    rest = jnp.concatenate([ref[at + 16 : at + SHARE, lanes], jnp.zeros((6, HDIM), F32)], axis=0)
    both = jnp.concatenate([ref[at : at + 16, lanes], rest], axis=1)
    return (both if scale is None else both * scale).astype(BF)


def unpack(block, ref, at, lane, rows=SHARE):
    block = block.astype(F32)
    lanes = slice(lane, lane + HDIM)
    ref[at : at + 16, lanes] = block[:, 0:64]
    ref[at + 16 : at + rows, lanes] = block[0 : rows - 16, 64:128]


def project_kernel(x_ref, w_ref, b_ref, cot_ref, out_ref, q_ref):
    w = w_ref[...].reshape(DIM, JW)
    q_ref[...] = jnp.zeros_like(q_ref)
    for r in range(NROW):
        tokens = x_ref[r].astype(F32).T.astype(BF)
        y = dot(tokens, w, 1, 0) + b_ref[...]
        q_ref[r * TOK : (r + 1) * TOK, :] = y[:, 0:256]
        for h in range(3):
            kv = y[:, 256 + 128 * h : 384 + 128 * h].T.astype(BF)
            for j in range(PER_HEAD * h, PER_HEAD * (h + 1) + (1 if h == 2 else 0)):
                out_ref[j, r * TOK : (r + 1) * TOK, :] = kv
    for j in range(NCOL):
        h, k = min(j, 14) // PER_HEAD, min(j, 14) % PER_HEAD
        for r in range(NROW):
            at = r * TOK + SHARE * k
            out_ref[j, Q_AT + 16 * r : Q_AT + 16 * (r + 1), :] = pack(q_ref, at, HDIM * h)
    out_ref[:, C_AT:BLOCK, :] = cot_ref[...]


def project(x4, wj, bias, cot):
    return pl.pallas_call(
        project_kernel,
        out_shape=pltpu.HBM((NCOL, BLOCK, 128), BF),
        in_specs=[VMEM] * 4,
        out_specs=VMEM,
        scratch_shapes=[pltpu.VMEM((640, 256), F32)],
        compiler_params=params("project"),
        cost_estimate=cost(3),
        name="project",
    )(x4, wj, bias, cot)


def key_rows(seg_row):
    row = lax.broadcasted_iota(jnp.int32, (16, seg_row.shape[1]), 0)
    hot = jnp.where(row < 5, jnp.where(row == seg_row, 1.0, 0.0), jnp.where(row < 8, 1.0, 0.0))
    return hot.astype(BF)


def offset_columns(value, base):
    h, m, l = split3(-value)
    lane = lax.broadcasted_iota(jnp.int32, base.shape, 1)
    return jnp.where(
        lane == 5,
        h.astype(F32),
        jnp.where(lane == 6, m.astype(F32), jnp.where(lane == 7, l.astype(F32), base)),
    )


def key_block(kv_ref, seg_ref, begin):
    pairs = [(c, r) for c in range(kv_ref.shape[0]) for r in range(kv_ref.shape[1] // TOK)]
    tiles = [kv_ref[c, r * TOK : (r + 1) * TOK, :] for c, r in pairs]
    at = pl.program_id(0) * kv_ref.shape[0]
    extra = [key_rows(seg_ref[pl.ds((begin + r) * NCOL + at + c, 1), :]) for c, r in pairs]
    return jnp.concatenate(tiles, axis=1), jnp.concatenate(extra, axis=1)


def forward_step(qa_ref, kv_ref, seg_ref, acc_ref, top_ref):
    kvt, extra = key_block(kv_ref, seg_ref, 0)
    kt = jnp.concatenate([kvt[0:64], kvt[0:64], extra], axis=0)
    turned = kvt.astype(F32).T
    lane = lax.broadcasted_iota(jnp.int32, turned.shape, 1)
    va = jnp.where(lane >= 64, turned, jnp.where(lane == 0, 1.0, 0.0)).astype(BF)
    s = dot(qa_ref[...], kt, 1, 0)
    parts = [s[:, i * 128 : (i + 1) * 128] for i in range(s.shape[1] // 128)]
    high = parts[0]
    for part in parts[1:]:
        high = jnp.maximum(high, part)
    top = top_ref[...]
    raised = jnp.maximum(top, jnp.broadcast_to(jnp.max(high, axis=1, keepdims=True), top.shape))
    p = jnp.concatenate([jnp.exp2(part - raised).astype(BF) for part in parts], axis=1)
    fade = jnp.exp2(top - raised)
    top_ref[...] = raised
    acc_ref[...] = acc_ref[...] * fade + dot(p, va, 1, 0)


def attend_kernel(
    shift_ref, q_ref, kv_ref, seg_ref, qa_ref, o_ref, out_ref, q_scr, pen_scr, acc_ref, top_ref
):
    @pl.when(pl.program_id(0) == 0)
    def _():
        columns = pltpu.roll(seg_ref[...].astype(F32), shift_ref[0], 1).T
        lane = lax.broadcasted_iota(jnp.int32, (SHARE, 16), 1)
        seg = lane.astype(F32)
        for r in range(NROW):
            for c in range(NCOL):
                slot = r * NCOL + c
                unpack(q_ref[c, 16 * r : 16 * (r + 1), :], q_scr, SHARE * slot, 0)
                pen_scr[SHARE * slot : SHARE * (slot + 1), :] = jnp.where(
                    (lane < 5) & (seg != columns[0:SHARE, slot : slot + 1]), BLOCK_OUT, 0.0
                )
        scaled = q_scr[...] * (LOG2E / 8.0)
        hi = scaled.astype(BF)
        lo = (scaled - hi.astype(F32)).astype(BF)
        pen = pen_scr[...]
        qa_ref[...] = jnp.concatenate([hi, lo, pen.astype(BF)], axis=1)
        acc_ref[...] = jnp.zeros_like(acc_ref)
        top_ref[...] = jnp.full_like(top_ref, -3e38)

    forward_step(qa_ref, kv_ref, seg_ref, acc_ref, top_ref)

    @pl.when(pl.program_id(0) == pl.num_programs(0) - 1)
    def _():
        acc = acc_ref[...]
        total = acc[:, 0:1]
        o_ref[...] = acc[:, 64:128] / total
        lse = top_ref[:, 0:1] + jnp.log(total) * LOG2E
        qa_ref[:, 128:144] = offset_columns(lse, qa_ref[:, 128:144].astype(F32)).astype(BF)
        for slot in range(SLOTS):
            out_ref[slot] = pack(o_ref, SHARE * slot, 0)


def attend(shift, arrived, seg):
    return pl.pallas_call(
        attend_kernel,
        grid=(NCOL // FWD_C,),
        out_shape=(
            pltpu.HBM((ROWS, AUG), BF),
            pltpu.HBM((ROWS, HDIM), F32),
            pltpu.HBM((SLOTS, 16, 128), BF),
        ),
        in_specs=[
            SMEM,
            Q_BLOCK,
            pl.BlockSpec((FWD_C, Q_AT, 128), lambda i: (i, 0, 0)),
            whole((SLOTS, TOK)),
        ],
        out_specs=[whole((ROWS, AUG)), whole((ROWS, HDIM)), whole((SLOTS, 16, 128))],
        scratch_shapes=[
            pltpu.VMEM((ROWS, HDIM), F32),
            pltpu.VMEM((ROWS, 16), F32),
            pltpu.VMEM((ROWS, 128), F32),
            pltpu.VMEM((ROWS, 128), F32),
        ],
        compiler_params=params("attend"),
        cost_estimate=cost(20),
        name="attend",
    )(shift, arrived, arrived, seg)


def backward_step(qa_ref, doa_ref, turned_ref, kv_ref, seg_ref, begin, acc_ref):
    kvt, extra = key_block(kv_ref, seg_ref, begin)
    kt = jnp.concatenate([kvt[0:64], kvt[0:64], extra], axis=0)
    vt = jnp.concatenate([kvt[64:128], extra], axis=0)
    keys = kvt.astype(F32).T.astype(BF)
    p = jnp.exp2(dot(qa_ref[...], kt, 1, 0))
    dp = dot(doa_ref[...], vt, 1, 0)
    ds = (p * dp).astype(BF)
    acc_ref[...] += dot(ds, keys, 1, 0)
    dk = dot(turned_ref[0:64, :], ds, 1, 0) * 0.125
    dv = dot(turned_ref[64:128, :], p.astype(BF), 1, 0)
    return jnp.concatenate([dk, dv], axis=0).astype(BF)


def store_keys(out_ref, at, both):
    for c in range(BWD_C):
        for r in range(HALF):
            i = c * HALF + r
            out_ref[at + c, r * TOK : (r + 1) * TOK, :] = both[:, i * TOK : (i + 1) * TOK]


def back_first_kernel(
    q_ref, do_ref, qa_ref, o_ref, fin_ref, kv_ref, seg_ref, out_ref, doa_ref, turned_ref, acc_ref, pair_scr
):
    @pl.when(pl.program_id(0) == 0)
    def _():
        for r in range(NROW):
            for c in range(NCOL):
                slot = r * NCOL + c
                unpack(q_ref[c, 16 * r : 16 * (r + 1), :], pair_scr, SHARE * slot, 0)
                unpack(do_ref[slot], pair_scr, SHARE * slot, HDIM)
        pairs = pair_scr[...]
        turned_ref[...] = pairs.T.astype(BF)
        grad = pairs[:, 64:128]
        delta = jnp.sum(grad * o_ref[...], axis=1, keepdims=True)
        ext = offset_columns(delta, jnp.zeros((ROWS, 16), F32))
        doa_ref[...] = jnp.concatenate([grad.astype(BF), ext.astype(BF)], axis=1)
        acc_ref[...] = jnp.zeros_like(acc_ref)

    both = backward_step(qa_ref, doa_ref, turned_ref, kv_ref, seg_ref, 0, acc_ref)
    store_keys(out_ref, 0, both)
    out_ref[:, 256:304, :] = fin_ref[...]


def back_second_kernel(
    qa_ref, doa_ref, turned_ref, acc_in, kv_ref, seg_ref, out_ref, acc_ref
):
    step = pl.program_id(0)

    @pl.when(step == 0)
    def _():
        acc_ref[...] = acc_in[...]

    both = backward_step(qa_ref, doa_ref, turned_ref, kv_ref, seg_ref, HALF, acc_ref)
    store_keys(out_ref, step * BWD_C, both)

    @pl.when(step == pl.num_programs(0) - 1)
    def _():
        for r in range(NROW):
            for c in range(NCOL):
                block = pack(acc_ref, SHARE * (r * NCOL + c), 0, 0.125)
                out_ref[c, 256 + 16 * r : 272 + 16 * r, :] = block


SEG_BACK = whole((SLOTS, TOK))
BACK_STEPS = NCOL // BWD_C


def attend_back_first(arrived, grad, qa, o, fin, seg):
    return pl.pallas_call(
        back_first_kernel,
        grid=(BACK_STEPS,),
        out_shape=(
            pltpu.HBM((NCOL, 304, 128), BF),
            pltpu.HBM((ROWS, 80), BF),
            pltpu.HBM((128, ROWS), BF),
            pltpu.HBM((ROWS, 128), F32),
        ),
        in_specs=[
            Q_BLOCK,
            whole((SLOTS, 16, 128)),
            whole((ROWS, AUG)),
            whole((ROWS, HDIM)),
            pl.BlockSpec((BWD_C, 48, 128), lambda i: (i, 0, 0)),
            pl.BlockSpec((BWD_C, HALF * TOK, 128), lambda i: (i, 0, 0)),
            SEG_BACK,
        ],
        out_specs=[
            pl.BlockSpec((BWD_C, 304, 128), lambda i: (i, 0, 0)),
            whole((ROWS, 80)),
            whole((128, ROWS)),
            whole((ROWS, 128)),
        ],
        scratch_shapes=[pltpu.VMEM((ROWS, 128), F32)],
        compiler_params=params("attend_back_first"),
        cost_estimate=cost(18),
        name="attend_back_first",
    )(arrived, grad, qa, o, fin, arrived, seg)


def attend_back_second(qa, doa, turned, acc, arrived, seg):
    return pl.pallas_call(
        back_second_kernel,
        grid=(BACK_STEPS,),
        out_shape=pltpu.HBM((NCOL, 320, 128), BF),
        in_specs=[
            whole((ROWS, AUG)),
            whole((ROWS, 80)),
            whole((128, ROWS)),
            whole((ROWS, 128)),
            pl.BlockSpec((BWD_C, HALF * TOK, 128), lambda i: (i, 1, 0)),
            SEG_BACK,
        ],
        out_specs=whole((NCOL, 320, 128)),
        scratch_shapes=[pltpu.VMEM((ROWS, 128), F32)],
        compiler_params=params("attend_back_second"),
        cost_estimate=cost(18),
        name="attend_back_second",
    )(qa, doa, turned, acc, arrived, seg)


def heads_of(block):
    return jnp.concatenate(
        [
            jnp.concatenate([block[64 * h : 64 * (h + 1), 64 * k : 64 * (k + 1)] for h in range(3)], axis=1)
            for k in range(2)
        ],
        axis=0,
    )


def room(k):
    return min(SHARE, TOK - SHARE * k)


def feature_mean(v):
    return jnp.sum(v, axis=1, keepdims=True) * (1.0 / DIM)


def tokenwise_kernel(
    row_ref, att_ref, x_ref, cot_ref, vec_ref, upb_ref, all_ref,
    sent_ref, datt_ref, fin_ref, dh1_ref,
    up_ref, down_ref, out_ref, slope_ref, att_scr, back_scr, sems,
):
    row = row_ref[0]
    copies = []
    for g in range(3):
        for k in range(2):
            for r in range(NROW):
                copies.append(
                    pltpu.make_async_copy(
                        all_ref.at[k, r, :, 96:112, g * 128 : (g + 1) * 128],
                        out_ref.at[k * NROW + r, :, 16 * g : 16 * (g + 1), :],
                        sems.at[0],
                    )
                )
    n_out = len(copies)
    for r in range(NROW):
        for k in range(2):
            lanes = slice(r * DIM + k * 384, r * DIM + (k + 1) * 384)
            copies.append(
                pltpu.make_async_copy(all_ref.at[k, r, :, 0:48, :], up_ref.at[:, :, lanes], sems.at[1 + r])
            )
    for r in range(NROW):
        for k in range(2):
            lanes = slice(r * DIM + k * 384, r * DIM + (k + 1) * 384)
            copies.append(
                pltpu.make_async_copy(all_ref.at[k, r, :, 48:96, :], down_ref.at[:, :, lanes], sems.at[5 + r])
            )
    for copy in copies:
        copy.start()

    def wait(group):
        chosen = copies[:n_out] if group == 0 else copies[n_out + 2 * (group - 1) : n_out + 2 * group]
        for copy in chosen:
            copy.wait()

    tok = x_ref[...].reshape(DIM, TOK).astype(F32).T
    cot = cot_ref[...].reshape(DIM, TOK).astype(F32).T
    vecs = vec_ref[...].reshape(DIM, TOK).astype(F32).T[64:128]
    out_b, gain_1, shift_1, down_b, gain_2, shift_2 = [
        vecs[i : i + 1] + vecs[6 + i : 7 + i] + vecs[12 + i : 13 + i] for i in range(6)
    ]
    gap = jnp.zeros((TOK, 32), BF)

    for r in range(NROW):
        for j in range(15):
            h, k = j // PER_HEAD, j % PER_HEAD
            unpack(att_ref[r * NCOL + j], att_scr, SHARE * k, 192 * r + HDIM * h, room(k))
    for r in range(NROW):
        target = lax.rem(r + NROW - row, NROW)
        for h in range(3):
            lanes = slice(192 * r + HDIM * h, 192 * r + HDIM * (h + 1))
            both = jnp.concatenate([att_scr[0:64, lanes], att_scr[64:128, lanes]], axis=1)
            sent_ref[target, A_AT + 64 * h : A_AT + 64 * (h + 1), :] = both.astype(BF)
    wait(0)
    attn = jnp.zeros((TOK, DIM), F32)
    for r in range(NROW):
        for k in range(2):
            lanes = slice(192 * r + 96 * k, 192 * r + 96 * (k + 1))
            piece = jnp.concatenate([att_scr[:, lanes].astype(BF), gap], axis=1)
            attn = attn + dot(piece, out_ref[k * NROW + r].reshape(DIM, 128), 1, 1)
    h1 = tok + (attn + out_b)
    off = h1 - feature_mean(h1)
    inv1 = lax.rsqrt(feature_mean(off * off) + EPS)
    xhat1 = off * inv1
    n1 = xhat1 * gain_1 + shift_1
    n1_low = n1.astype(BF)

    branch = jnp.zeros((TOK, DIM), F32)
    for r in range(NROW):
        wait(1 + r)
        cols = slice(r * DIM, (r + 1) * DIM)
        pre = dot(n1_low, up_ref[:, :, cols].reshape(DIM, DIM), 1, 0) + upb_ref[r : r + 1, :]
        phi = 0.5 * (1.0 + lax.erf(pre * (1.0 / math.sqrt(2.0))))
        act = (pre * phi).astype(BF)
        slope_ref[:, cols] = phi + pre * jnp.exp(-0.5 * pre * pre) * (1.0 / math.sqrt(2.0 * math.pi))
        for i in range(6):
            at = 3 * DIM + 48 + DIM + i * TOK
            sent_ref[lax.rem(r + NROW - row, NROW), at : at + TOK, :] = act[:, i * TOK : (i + 1) * TOK]
        wait(5 + r)
        branch = branch + dot(act, down_ref[:, :, cols].reshape(DIM, DIM), 1, 1)
    h2 = n1 + (branch + down_b)
    off = h2 - feature_mean(h2)
    inv2 = lax.rsqrt(feature_mean(off * off) + EPS)
    xhat2 = off * inv2
    fin_ref[...] = (xhat2 * gain_2 + shift_2).T.astype(BF).reshape(NCOL, 48, TOK)
    dx = cot * gain_2
    dh2 = inv2 * (dx - feature_mean(dx) - xhat2 * feature_mean(dx * xhat2))
    d_branch = dh2.astype(BF)

    back = jnp.zeros((TOK, DIM), F32)
    for r in range(NROW):
        cols = slice(r * DIM, (r + 1) * DIM)
        d_act = dot(d_branch, down_ref[:, :, cols].reshape(DIM, DIM), 1, 0)
        d_pre = (d_act * slope_ref[:, cols]).astype(BF)
        for i in range(6):
            at = 3 * DIM + 48 + i * TOK
            sent_ref[lax.rem(r + NROW - row, NROW), at : at + TOK, :] = d_pre[:, i * TOK : (i + 1) * TOK]
        back = back + dot(d_pre, up_ref[:, :, cols].reshape(DIM, DIM), 1, 1)
    up1 = dh2 + back
    dx = up1 * gain_1
    dh1 = inv1 * (dx - feature_mean(dx) - xhat1 * feature_mean(dx * xhat1))
    d_attn = dh1.astype(BF)
    back_scr[TOK : TOK + 8, :] = jnp.zeros((8, 192), F32)
    for r in range(NROW):
        pieces = [dot(d_attn, out_ref[k * NROW + r].reshape(DIM, 128), 1, 0)[:, 0:96] for k in range(2)]
        back_scr[0:TOK, :] = jnp.concatenate(pieces, axis=1)
        for j in range(15):
            h, k = j // PER_HEAD, j % PER_HEAD
            datt_ref[r * NCOL + j] = pack(back_scr, SHARE * k, HDIM * h)
        datt_ref[r * NCOL + 15] = jnp.zeros((16, 128), BF)
    turned = dh1.T
    dh1_ref[...] = turned
    shared = [n1.T.astype(BF), dh2.T.astype(BF), turned.astype(BF)]
    sums = [
        jnp.sum(v, axis=0, keepdims=True) for v in (up1 * xhat1, up1, cot * xhat2, cot)
    ]
    rows = []
    for part in range(2):
        for v in sums:
            hi = v.astype(BF).astype(F32)
            piece = hi if part == 0 else v - hi
            rows += [piece[:, i * 128 : (i + 1) * 128] for i in range(6)]
    shared.append(jnp.concatenate(rows, axis=0).astype(BF))
    at = 0
    for v in shared:
        for r in range(NROW):
            sent_ref[r, at : at + v.shape[0], :] = v
        at += v.shape[0]


def tokenwise(row, att, x_t, arrived, wj, up_bias, everything):
    return pl.pallas_call(
        tokenwise_kernel,
        out_shape=(
            pltpu.HBM((NROW, SENT, TOK), BF),
            pltpu.HBM((SLOTS, 16, 128), BF),
            pltpu.HBM((NCOL, 48, TOK), BF),
            pltpu.HBM((DIM, TOK), F32),
        ),
        grid=(1,),
        in_specs=[
            SMEM,
            whole((SLOTS, 16, 128)),
            whole((NCOL, 48, TOK)),
            pl.BlockSpec((NCOL, 48, TOK), lambda i: (0, C_AT // 48, 0)),
            pl.BlockSpec((NCOL, 48, TOK), lambda i: (0, 0, 1)),
            whole((NROW, DIM)),
            pl.BlockSpec(memory_space=pl.ANY),
        ],
        out_specs=[
            whole((NROW, SENT, TOK)),
            whole((SLOTS, 16, 128)),
            whole((NCOL, 48, TOK)),
            whole((DIM, TOK)),
        ],
        scratch_shapes=[
            pltpu.VMEM((NCOL, 48, FF), BF),
            pltpu.VMEM((NCOL, 48, FF), BF),
            pltpu.VMEM((2 * NROW, NCOL, 48, 128), BF),
            pltpu.VMEM((TOK, FF), F32),
            pltpu.VMEM((TOK, DIM), F32),
            pltpu.VMEM((TOK + 8, 192), F32),
            pltpu.SemaphoreType.DMA((9,)),
        ],
        compiler_params=params("tokenwise"),
        cost_estimate=cost(15),
        name="tokenwise",
    )(row, att, x_t, arrived, wj, up_bias, everything)


def place(core, mine_ref, other_ref, blocks, half_rows):
    for at, block in blocks:
        low = at < half_rows
        local = at if low else at - half_rows
        rows = slice(local, local + block.shape[1])
        keep = core == (0 if low else 1)

        @pl.when(keep)
        def _():
            mine_ref[:, rows, :] = block

        @pl.when(jnp.logical_not(keep))
        def _():
            other_ref[:, rows, :] = block


def weight_grads_kernel(
    core_ref, own_ref, got_1, got_2, got_3, mine_ref, other_ref
):
    core = core_ref[0]
    got_ref = [own_ref.at[0], got_1, got_2, got_3]

    def feats(at):
        return jnp.concatenate([got_ref[r][at : at + DIM, :] for r in range(NROW)], axis=1)

    def hidden(at):
        return jnp.concatenate(
            [
                jnp.concatenate([got_ref[r][at + i * TOK : at + (i + 1) * TOK, :] for i in range(6)], axis=1)
                for r in range(NROW)
            ],
            axis=0,
        )

    def chunks(g, count):
        return [g[:, i * 128 : (i + 1) * 128].astype(BF).reshape(NCOL, 48, 128) for i in range(count)]

    ones = jnp.ones((16, NROW * TOK), BF)
    d_pre = hidden(3 * DIM + 48)
    d_branch = feats(DIM)
    d_attn = feats(2 * DIM)
    att = jnp.concatenate([heads_of(got_ref[r][A_AT:SENT, :].astype(F32)).astype(BF) for r in range(NROW)], axis=0)
    att = jnp.concatenate([att, jnp.zeros((NROW * TOK, 64), BF)], axis=1)
    pieces = chunks(dot(feats(0), d_pre, 1, 0), 6)
    pieces += chunks(dot(d_branch, hidden(4 * DIM + 48), 1, 0), 6)
    pieces += chunks(dot(d_attn, att, 1, 0), 2)
    sums = [dot(ones, d_branch, 1, 1)[0:1], dot(ones, d_attn, 1, 1)[0:1], dot(ones, d_pre, 1, 0)[0:1]]
    norm = got_ref[0][3 * DIM : 3 * DIM + 48, :].astype(F32)
    for r in range(1, NROW):
        norm = norm + got_ref[r][3 * DIM : 3 * DIM + 48, :].astype(F32)
    rows = [norm[0:24] + norm[24:48]]
    for v in sums:
        rows += [v[:, i * 128 : (i + 1) * 128] for i in range(6)]
    rows.append(jnp.zeros((6, 128), F32))
    rows = jnp.concatenate(rows, axis=0)
    hi = rows.astype(BF)
    lo = (rows - hi.astype(F32)).astype(BF)
    misc = jnp.concatenate([hi, lo], axis=0)
    blocks = [(48 * i, piece) for i, piece in enumerate(pieces)]
    blocks.append((672, jnp.broadcast_to(misc[None], (NCOL, 96, 128))))
    place(core, mine_ref, other_ref, blocks, WROWS // 2)


def weight_grads(core, sent, got):
    kind = pltpu.HBM((NCOL, WROWS // 2, 128), BF)
    return pl.pallas_call(
        weight_grads_kernel,
        out_shape=(kind, kind),
        grid=(1,),
        in_specs=[SMEM, pl.BlockSpec((1, SENT, TOK), lambda i: (0, 0, 0))] + [whole((SENT, TOK))] * 3,
        out_specs=[whole(kind.shape)] * 2,
        compiler_params=params("weight_grads"),
        cost_estimate=cost(1),
        name="weight_grads",
    )(core, sent, *got)


def project_back_kernel(
    core_ref, first_ref, second_ref, w_ref, x_ref, din_ref, mine_ref, other_ref, layer_ref, scr
):
    core = core_ref[0]
    layer_ref[...] = jnp.concatenate([first_ref[c, 256:304, :] for c in range(NCOL)], axis=1)
    scr[...] = jnp.zeros_like(scr)
    for j in range(15):
        h, k = j // PER_HEAD, j % PER_HEAD
        for r in range(NROW):
            block = second_ref[j, 256 + 16 * r : 272 + 16 * r, :]
            unpack(block, scr, r * TOK + SHARE * k, HDIM * h, room(k))
    dq = scr[...].T.astype(BF)
    w = w_ref[...].reshape(DIM, JW)
    grad = jnp.zeros((DIM, JW), F32)
    total = jnp.zeros((16, JW), F32)
    ones = jnp.ones((16, TOK), BF)
    for r in range(NROW):
        source, at = (first_ref, r) if r < HALF else (second_ref, r - HALF)
        parts = [dq[:, r * TOK : (r + 1) * TOK]]
        for h in range(3):
            acc = source[PER_HEAD * h, at * TOK : (at + 1) * TOK, :].astype(F32)
            for k in range(1, PER_HEAD):
                acc = acc + source[PER_HEAD * h + k, at * TOK : (at + 1) * TOK, :].astype(F32)
            parts.append(acc.astype(BF))
        d_proj = jnp.concatenate(parts, axis=0)
        din_ref[r] = dot(w, d_proj, 1, 0).astype(BF)
        grad = grad + dot(x_ref[r], d_proj, 1, 1)
        total = total + dot(ones, d_proj, 1, 1)
    rows = [total[0:1, i * 128 : (i + 1) * 128] for i in range(5)] + [jnp.zeros((3, 128), F32)]
    rows = jnp.concatenate(rows, axis=0)
    hi = rows.astype(BF)
    lo = (rows - hi.astype(F32)).astype(BF)
    misc = jnp.broadcast_to(jnp.concatenate([hi, lo], axis=0)[None], (NCOL, 16, 128))
    low = grad.astype(BF)
    pieces = [low[:, i * 128 : (i + 1) * 128].reshape(NCOL, 48, 128) for i in range(5)]
    blocks = [(0, pieces[0]), (48, pieces[1]), (96, pieces[2][:, 0:32]), (128, pieces[2][:, 32:48])]
    blocks += [(144, pieces[3]), (192, pieces[4]), (240, misc)]
    place(core, mine_ref, other_ref, blocks, 128)


def project_back(core, first, second, wj, x4):
    kind = pltpu.HBM((NCOL, 128, 128), BF)
    return pl.pallas_call(
        project_back_kernel,
        out_shape=(
            pltpu.HBM((NROW, DIM, TOK), BF),
            kind,
            kind,
            pltpu.HBM((48, NCOL * TOK), BF),
        ),
        in_specs=[SMEM] + [VMEM] * 4,
        out_specs=[VMEM] * 4,
        scratch_shapes=[pltpu.VMEM((512, 256), F32)],
        compiler_params=params("project_back"),
        cost_estimate=cost(5),
        name="project_back",
    )(core, first, second, wj, x4)


def last_kernel(mine_ref, theirs_ref, din_ref, dh1_ref, out_ref):
    out_ref[:, 0:128, :] = (mine_ref[...].astype(F32) + theirs_ref[...].astype(F32)).astype(BF)
    total = dh1_ref[...]
    for r in range(NROW):
        total = total + din_ref[r].astype(F32)
    out_ref[:, 128:176, :] = total.astype(BF).reshape(NCOL, 48, TOK)


def last_payload(mine, theirs, din, dh1):
    return pl.pallas_call(
        last_kernel,
        out_shape=pltpu.HBM((NCOL, 176, 128), BF),
        in_specs=[VMEM] * 4,
        out_specs=VMEM,
        compiler_params=params("last_payload"),
        cost_estimate=cost(1),
        name="last_payload",
    )(mine, theirs, din, dh1)


def join(core_ref, mine, theirs):
    first = core_ref[0] == 0
    a, b = mine[...], theirs[...]
    return jnp.concatenate([jnp.where(first, a, b), jnp.where(first, b, a)], axis=0)


def finish_kernel(
    core_ref, col_ref, wide_ref, other_ref, out_ref, up_ref, up_bias_ref, down_ref, *own_refs
):
    wide = join(core_ref, wide_ref, other_ref)
    for i in range(6):
        lanes = slice(i * 128, (i + 1) * 128)
        up_ref[:, lanes] = wide[48 * i : 48 * (i + 1)]
        down_ref[:, lanes] = wide[288 + 48 * i : 288 + 48 * (i + 1)]
    out_ref[...] = jnp.concatenate([wide[576:624], wide[624:672, 0:64]], axis=1)
    vecs = wide[672:720] + wide[720:768]
    up_bias_ref[...] = vecs[36:42]
    rows = [
        jnp.concatenate([vecs[6 * v + i : 6 * v + i + 1] for i in range(6)], axis=1) for v in range(6)
    ]
    rows = jnp.concatenate(rows + [jnp.zeros((2, DIM), F32)], axis=0)
    feature = lax.broadcasted_iota(jnp.int32, (DIM, 48), 0)
    lane = lax.broadcasted_iota(jnp.int32, (DIM, 48), 1)
    pick = jnp.where(feature == col_ref[0] * 48 + lane, 1.0, 0.0).astype(BF)
    own = sum(dot(part, pick, 1, 0) for part in split3(rows))
    for v, ref in enumerate(own_refs):
        ref[...] = own[v : v + 1]


def finish(core, col, wide, other):
    shapes = [(48, 192), (48, DIM), (6, 128), (48, DIM)] + [(1, 48)] * 6
    return pl.pallas_call(
        finish_kernel,
        out_shape=[pltpu.HBM(shape, F32) for shape in shapes],
        in_specs=[SMEM] * 2 + [VMEM] * 2,
        out_specs=[VMEM] * len(shapes),
        compiler_params=params("finish"),
        cost_estimate=cost(1),
        name="finish",
    )(core, col, wide, other)


def joint_kernel(core_ref, last_ref, other_ref, joint_ref, joint_bias_ref):
    last = join(core_ref, last_ref, other_ref)
    chunks = [last[48 * i : 48 * (i + 1)] for i in range(5)]
    heads = [chunks[0][:, 0:64], chunks[0][:, 64:128], chunks[1][:, 0:64]]
    joint_ref[...] = jnp.concatenate([v for h in range(3) for v in (heads[h], chunks[2 + h])], axis=1)
    sums = last[240:248] + last[248:256]
    heads = [sums[0:1, 0:64], sums[0:1, 64:128], sums[1:2, 0:64]]
    joint_bias_ref[...] = jnp.concatenate(
        [jnp.concatenate([heads[h], sums[2 + h : 3 + h, 64:128]], axis=1) for h in range(3)], axis=0
    )


def joint_gradient(core, last, other):
    return pl.pallas_call(
        joint_kernel,
        out_shape=[pltpu.HBM(shape, F32) for shape in ((48, 576), (3, 128))],
        in_specs=[SMEM] + [VMEM] * 2,
        out_specs=[VMEM] * 2,
        compiler_params=params("joint_gradient"),
        cost_estimate=cost(1),
        name="joint_gradient",
    )(core, last, other)


def exchange(blocks, axis):
    return lax.all_to_all(blocks, axis, 0, 0, tiled=True)


def around(v, axis, shift):
    return lax.ppermute(v, axis, [(i, (i + shift) % 4) for i in range(4)])


def swap_cores(v):
    return lax.ppermute(v, "dp", [(0, 1), (1, 0)])


def per_device(
    inputs,
    segments,
    joint_weight,
    joint_bias,
    output_weight,
    output_bias,
    first_norm_gain,
    shift_first,
    up_weight,
    up_bias,
    down_weight,
    down_bias,
    second_norm_gain,
    second_norm_shift,
    cotangent,
):
    core = lax.axis_index("dp")
    col = lax.axis_index(COL)
    row = lax.axis_index("row")
    my_z, my_y = lax.axis_index("z"), lax.axis_index("y")
    core_word = core.reshape(1).astype(jnp.int32)
    row_word = row.reshape(1).astype(jnp.int32)

    def by_col(a):
        return jnp.transpose(a.reshape(48, NCOL, TOK), (1, 0, 2))

    blocks = by_col(inputs)
    blocks, up_weight, down_weight, output_weight = lax.optimization_barrier(
        (blocks, up_weight, down_weight, output_weight)
    )
    x_t = exchange(blocks, COL)
    vectors = jnp.stack(
        [output_bias, first_norm_gain, shift_first, down_bias, second_norm_gain, second_norm_shift], axis=1
    )
    vectors = jnp.pad(jnp.concatenate(split3(vectors), axis=1), ((0, 0), (0, 46)))
    jw = joint_weight.reshape(48, 3, 3, HDIM)
    jw = jnp.concatenate([jw[:, :, 0].reshape(48, 192), vectors, jw[:, :, 1:].reshape(48, 384)], axis=1)
    jw = jnp.broadcast_to(jw[None], (NCOL, 48, JW))
    x_t, jw = lax.optimization_barrier((x_t, jw))
    wj = exchange(jw, COL)
    x4 = lax.all_gather(x_t.reshape(DIM, TOK), "row", axis=0, tiled=False)

    turned = lax.dynamic_slice_in_dim(output_weight, core * 96, 96, 0).T
    my_bias = lax.dynamic_slice_in_dim(up_bias, (core * NCOL + col) * 24, 24, 0)
    my_bias = jnp.pad(jnp.stack(split3(my_bias)), ((0, 45), (0, 8)))
    turned = jnp.concatenate([turned, my_bias], axis=1).reshape(3, 16, 128)
    turned = jnp.transpose(turned, (1, 0, 2)).reshape(16, 384)
    shard = jnp.concatenate(
        [
            lax.dynamic_slice_in_dim(up_weight, core * 384, 384, 1),
            lax.dynamic_slice_in_dim(down_weight, core * 384, 384, 1),
            turned,
        ],
        axis=0,
    )
    shard = lax.optimization_barrier((shard, x_t))[0]
    everything = lax.all_gather(shard, ("dp", "row", "z", "y"), axis=0, tiled=False)
    everything = everything.reshape(2, NROW, NCOL, 112, 384)
    up_b = jnp.sum(everything[:, :, :, 96:99, 96:120].astype(F32), axis=3)
    up_b = jnp.transpose(up_b, (1, 0, 2, 3)).reshape(NROW, DIM)

    bias3 = joint_bias.reshape(3, 2, HDIM)
    bias = jnp.concatenate(
        [
            bias3[:, 0].reshape(192),
            jnp.zeros((64,), F32),
            jnp.concatenate([jnp.zeros((3, HDIM), F32), bias3[:, 1]], axis=1).reshape(384),
        ]
    ).reshape(1, JW)
    seg = segments.reshape(SLOTS, TOK)
    shift = lax.rem(TOK - lax.rem(col, PER_HEAD) * SHARE, TOK).reshape(1).astype(jnp.int32)

    arrived = exchange(project(x4, wj, bias, by_col(cotangent)), COL)
    qa, o, o_blocks = attend(shift, arrived, seg)

    att = exchange(o_blocks, ALL)
    sent, d_blocks, fin, dh1 = tokenwise(row_word, att, x_t, arrived, wj, up_b, everything)

    d_blocks, sent = lax.optimization_barrier((d_blocks, sent))
    grad_o = exchange(d_blocks, ALL)
    got = [around(sent[d], "row", d) for d in range(1, NROW)]
    back_a, doa, turned_qd, acc = attend_back_first(arrived, grad_o, qa, o, fin, seg)
    back_b = attend_back_second(qa, doa, turned_qd, acc, arrived, seg)
    back_a = exchange(back_a, COL)
    back_b, got, sent, back_a = lax.optimization_barrier((back_b, got, sent, back_a))
    mine, other = weight_grads(core_word, sent, got)
    theirs = swap_cores(other)
    back_b, back_a = lax.optimization_barrier((back_b, back_a))
    back_b = exchange(back_b, COL)
    wide = (mine.astype(F32) + theirs.astype(F32)).astype(BF).reshape(4, 4, WROWS // 2, 128)
    near = [lax.dynamic_index_in_dim(wide, lax.rem(my_z + d, 4), 0, keepdims=False) for d in range(4)]
    near = [near[0]] + [around(near[d], "z", d) for d in range(1, 4)]
    wide = near[0].astype(F32) + near[1].astype(F32) + near[2].astype(F32) + near[3].astype(F32)
    wide = wide.astype(BF)

    din, mine_j, other_j, layer_output = project_back(core_word, back_a, back_b, wj, x4)
    theirs_j = swap_cores(other_j)
    din = exchange(din, "row")
    near = [lax.dynamic_index_in_dim(wide, lax.rem(my_y + d, 4), 0, keepdims=False) for d in range(4)]
    din, near = lax.optimization_barrier((din, near))
    near = [near[0]] + [around(near[d], "y", d) for d in range(1, 4)]
    mixed = exchange(last_payload(mine_j, theirs_j, din, dh1), COL)
    wide = near[0].astype(F32) + near[1].astype(F32) + near[2].astype(F32) + near[3].astype(F32)
    grad_out, grad_up, grad_up_bias, grad_down, *own = finish(
        core_word, col.reshape(1).astype(jnp.int32), wide, swap_cores(wide)
    )
    last = jnp.sum(mixed[:, :128].astype(F32), axis=0)
    grad_inputs = jnp.transpose(mixed[:, 128:].astype(F32), (1, 0, 2)).reshape(48, 2048)
    grad_joint, grad_joint_bias = joint_gradient(core_word, last, swap_cores(last))
    own = [v.reshape(48) for v in own]

    return (
        layer_output,
        grad_inputs,
        grad_joint,
        grad_joint_bias.reshape(384),
        grad_out.T,
        own[5],
        own[0],
        own[1],
        grad_up,
        grad_up_bias.reshape(768),
        grad_down,
        own[4],
        own[2],
        own[3],
    )


def solution(mesh):
    sizes = (mesh.shape["dp"], mesh.shape["row"], 4, 4)
    fine = jax.sharding.Mesh(mesh.devices.reshape(sizes), ("dp", "row", "z", "y"))
    grid = P(COL, ("dp", "row"))
    block = P(COL, "row")
    return jax.shard_map(
        per_device,
        mesh=fine,
        in_specs=(
            grid, P("dp", None), block, P("row"), P("row", COL), P(COL), P(COL), P(COL),
            block, P("row"), block, P(COL), P(COL), P(COL), grid,
        ),
        out_specs=(
            grid, grid, block, P("row"), P("row", COL), P(COL), P(COL), P(COL),
            block, P("row"), block, P(COL), P(COL), P(COL),
        ),
        check_vma=False,
    )
```

```python
import math

import jax
import jax.numpy as jnp
from jax import lax
from jax.experimental import pallas as pl
from jax.experimental.pallas import tpu as pltpu
from jax.sharding import PartitionSpec as P

HDIM = 64
EPS = 1e-06
BLOCK_OUT = -1e30
LOG2E = 1.4426950408889634
BF = jnp.bfloat16
F32 = jnp.float32

DIM = 768
FF = 3072
NCOL = 16
NROW = 4
TOK = 128
PER_HEAD = 5
SHARE = 26
SLOTS = NROW * NCOL
ROWS = SLOTS * SHARE
AUG = 144
JW = 640
HALF = 2
FWD_C = 2
BWD_C = 4
Q_AT = NROW * TOK
C_AT = Q_AT + 64
BLOCK = C_AT + 48
MIB = 2**20
COL = ("z", "y")
ALL = ("row", "z", "y")
VMEM = pl.BlockSpec(memory_space=pltpu.VMEM)
SMEM = pl.BlockSpec(memory_space=pltpu.SMEM)
A_AT = 5 * DIM + 48
SENT = A_AT + 192
SAME = 3 * DIM + 48
WROWS = 768


def split3(v):
    hi = v.astype(BF)
    rest = v - hi.astype(F32)
    mid = rest.astype(BF)
    low = (rest - mid.astype(F32)).astype(BF)
    return hi, mid, low


def dot(a, b, ca, cb):
    return lax.dot_general(a, b, (((ca,), (cb,)), ((), ())), preferred_element_type=F32)


LIMITS = {
    "project": 16,
    "attend": 32,
    "attend_back_first": 63.9,
    "attend_back_second": 63.9,
    "tokenwise": 63.9,
    "weight_grads": 63.9,
    "project_back": 63.9,
    "last_payload": 12,
    "finish": 12,
    "joint_gradient": 8,
}


def params(name):
    return pltpu.CompilerParams(vmem_limit_bytes=int(LIMITS[name] * MIB))


def cost(us):
    return pl.CostEstimate(flops=int(us * 1e9), bytes_accessed=int(us * 2e6), transcendentals=0)


Q_BLOCK = pl.BlockSpec((NCOL, 64, 128), lambda i: (0, Q_AT // 64, 0))


def whole(shape):
    return pl.BlockSpec(shape, lambda i: (0,) * len(shape))


def pack(ref, at, lane, scale=None):
    lanes = slice(lane, lane + HDIM)
    rest = jnp.concatenate([ref[at + 16 : at + SHARE, lanes], jnp.zeros((6, HDIM), F32)], axis=0)
    both = jnp.concatenate([ref[at : at + 16, lanes], rest], axis=1)
    return (both if scale is None else both * scale).astype(BF)


def unpack(block, ref, at, lane, rows=SHARE):
    block = block.astype(F32)
    lanes = slice(lane, lane + HDIM)
    ref[at : at + 16, lanes] = block[:, 0:64]
    ref[at + 16 : at + rows, lanes] = block[0 : rows - 16, 64:128]


def project_kernel(x_ref, w_ref, b_ref, cot_ref, out_ref, q_ref):
    w = w_ref[...].reshape(DIM, JW)
    q_ref[...] = jnp.zeros_like(q_ref)
    for r in range(NROW):
        tokens = x_ref[r].astype(F32).T.astype(BF)
        y = dot(tokens, w, 1, 0) + b_ref[...]
        q_ref[r * TOK : (r + 1) * TOK, :] = y[:, 0:256]
        for h in range(3):
            kv = y[:, 256 + 128 * h : 384 + 128 * h].T.astype(BF)
            for j in range(PER_HEAD * h, PER_HEAD * (h + 1) + (1 if h == 2 else 0)):
                out_ref[j, r * TOK : (r + 1) * TOK, :] = kv
    for j in range(NCOL):
        h, k = min(j, 14) // PER_HEAD, min(j, 14) % PER_HEAD
        for r in range(NROW):
            at = r * TOK + SHARE * k
            out_ref[j, Q_AT + 16 * r : Q_AT + 16 * (r + 1), :] = pack(q_ref, at, HDIM * h)
    out_ref[:, C_AT:BLOCK, :] = cot_ref[...]


def project(x4, wj, bias, cot):
    return pl.pallas_call(
        project_kernel,
        out_shape=pltpu.HBM((NCOL, BLOCK, 128), BF),
        in_specs=[VMEM] * 4,
        out_specs=VMEM,
        scratch_shapes=[pltpu.VMEM((640, 256), F32)],
        compiler_params=params("project"),
        cost_estimate=cost(3),
        name="project",
    )(x4, wj, bias, cot)


def key_rows(seg_row):
    row = lax.broadcasted_iota(jnp.int32, (16, seg_row.shape[1]), 0)
    hot = jnp.where(row < 5, jnp.where(row == seg_row, 1.0, 0.0), jnp.where(row < 8, 1.0, 0.0))
    return hot.astype(BF)


def offset_columns(value, base):
    h, m, l = split3(-value)
    lane = lax.broadcasted_iota(jnp.int32, base.shape, 1)
    return jnp.where(
        lane == 5,
        h.astype(F32),
        jnp.where(lane == 6, m.astype(F32), jnp.where(lane == 7, l.astype(F32), base)),
    )


def key_block(kv_ref, seg_ref, begin):
    pairs = [(c, r) for c in range(kv_ref.shape[0]) for r in range(kv_ref.shape[1] // TOK)]
    tiles = [kv_ref[c, r * TOK : (r + 1) * TOK, :] for c, r in pairs]
    at = pl.program_id(0) * kv_ref.shape[0]
    extra = [key_rows(seg_ref[pl.ds((begin + r) * NCOL + at + c, 1), :]) for c, r in pairs]
    return jnp.concatenate(tiles, axis=1), jnp.concatenate(extra, axis=1)


def forward_step(qa_ref, kv_ref, seg_ref, acc_ref, top_ref):
    kvt, extra = key_block(kv_ref, seg_ref, 0)
    kt = jnp.concatenate([kvt[0:64], kvt[0:64], extra], axis=0)
    turned = kvt.astype(F32).T
    lane = lax.broadcasted_iota(jnp.int32, turned.shape, 1)
    va = jnp.where(lane >= 64, turned, jnp.where(lane == 0, 1.0, 0.0)).astype(BF)
    s = dot(qa_ref[...], kt, 1, 0)
    parts = [s[:, i * 128 : (i + 1) * 128] for i in range(s.shape[1] // 128)]
    high = parts[0]
    for part in parts[1:]:
        high = jnp.maximum(high, part)
    top = top_ref[...]
    raised = jnp.maximum(top, jnp.broadcast_to(jnp.max(high, axis=1, keepdims=True), top.shape))
    p = jnp.concatenate([jnp.exp2(part - raised).astype(BF) for part in parts], axis=1)
    fade = jnp.exp2(top - raised)
    top_ref[...] = raised
    acc_ref[...] = acc_ref[...] * fade + dot(p, va, 1, 0)


def attend_kernel(
    shift_ref, q_ref, kv_ref, seg_ref, qa_ref, o_ref, out_ref, q_scr, pen_scr, acc_ref, top_ref
):
    @pl.when(pl.program_id(0) == 0)
    def _():
        columns = pltpu.roll(seg_ref[...].astype(F32), shift_ref[0], 1).T
        lane = lax.broadcasted_iota(jnp.int32, (SHARE, 16), 1)
        seg = lane.astype(F32)
        for r in range(NROW):
            for c in range(NCOL):
                slot = r * NCOL + c
                unpack(q_ref[c, 16 * r : 16 * (r + 1), :], q_scr, SHARE * slot, 0)
                pen_scr[SHARE * slot : SHARE * (slot + 1), :] = jnp.where(
                    (lane < 5) & (seg != columns[0:SHARE, slot : slot + 1]), BLOCK_OUT, 0.0
                )
        scaled = q_scr[...] * (LOG2E / 8.0)
        hi = scaled.astype(BF)
        lo = (scaled - hi.astype(F32)).astype(BF)
        pen = pen_scr[...]
        qa_ref[...] = jnp.concatenate([hi, lo, pen.astype(BF)], axis=1)
        acc_ref[...] = jnp.zeros_like(acc_ref)
        top_ref[...] = jnp.full_like(top_ref, -3e38)

    forward_step(qa_ref, kv_ref, seg_ref, acc_ref, top_ref)

    @pl.when(pl.program_id(0) == pl.num_programs(0) - 1)
    def _():
        acc = acc_ref[...]
        total = acc[:, 0:1]
        o_ref[...] = acc[:, 64:128] / total
        lse = top_ref[:, 0:1] + jnp.log(total) * LOG2E
        qa_ref[:, 128:144] = offset_columns(lse, qa_ref[:, 128:144].astype(F32)).astype(BF)
        for slot in range(SLOTS):
            out_ref[slot] = pack(o_ref, SHARE * slot, 0)


def attend(shift, arrived, seg):
    return pl.pallas_call(
        attend_kernel,
        grid=(NCOL // FWD_C,),
        out_shape=(
            pltpu.HBM((ROWS, AUG), BF),
            pltpu.HBM((ROWS, HDIM), F32),
            pltpu.HBM((SLOTS, 16, 128), BF),
        ),
        in_specs=[
            SMEM,
            Q_BLOCK,
            pl.BlockSpec((FWD_C, Q_AT, 128), lambda i: (i, 0, 0)),
            whole((SLOTS, TOK)),
        ],
        out_specs=[whole((ROWS, AUG)), whole((ROWS, HDIM)), whole((SLOTS, 16, 128))],
        scratch_shapes=[
            pltpu.VMEM((ROWS, HDIM), F32),
            pltpu.VMEM((ROWS, 16), F32),
            pltpu.VMEM((ROWS, 128), F32),
            pltpu.VMEM((ROWS, 128), F32),
        ],
        compiler_params=params("attend"),
        cost_estimate=cost(20),
        name="attend",
    )(shift, arrived, arrived, seg)


def backward_step(qa_ref, doa_ref, turned_ref, kv_ref, seg_ref, begin, acc_ref):
    kvt, extra = key_block(kv_ref, seg_ref, begin)
    kt = jnp.concatenate([kvt[0:64], kvt[0:64], extra], axis=0)
    vt = jnp.concatenate([kvt[64:128], extra], axis=0)
    keys = kvt.astype(F32).T.astype(BF)
    p = jnp.exp2(dot(qa_ref[...], kt, 1, 0))
    dp = dot(doa_ref[...], vt, 1, 0)
    ds = (p * dp).astype(BF)
    acc_ref[...] += dot(ds, keys, 1, 0)
    dk = dot(turned_ref[0:64, :], ds, 1, 0) * 0.125
    dv = dot(turned_ref[64:128, :], p.astype(BF), 1, 0)
    return jnp.concatenate([dk, dv], axis=0).astype(BF)


def store_keys(out_ref, at, both):
    for c in range(BWD_C):
        for r in range(HALF):
            i = c * HALF + r
            out_ref[at + c, r * TOK : (r + 1) * TOK, :] = both[:, i * TOK : (i + 1) * TOK]


def back_first_kernel(
    q_ref, do_ref, qa_ref, o_ref, fin_ref, kv_ref, seg_ref, out_ref, doa_ref, turned_ref, acc_ref, pair_scr
):
    @pl.when(pl.program_id(0) == 0)
    def _():
        for r in range(NROW):
            for c in range(NCOL):
                slot = r * NCOL + c
                unpack(q_ref[c, 16 * r : 16 * (r + 1), :], pair_scr, SHARE * slot, 0)
                unpack(do_ref[slot], pair_scr, SHARE * slot, HDIM)
        pairs = pair_scr[...]
        turned_ref[...] = pairs.T.astype(BF)
        grad = pairs[:, 64:128]
        delta = jnp.sum(grad * o_ref[...], axis=1, keepdims=True)
        ext = offset_columns(delta, jnp.zeros((ROWS, 16), F32))
        doa_ref[...] = jnp.concatenate([grad.astype(BF), ext.astype(BF)], axis=1)
        acc_ref[...] = jnp.zeros_like(acc_ref)

    both = backward_step(qa_ref, doa_ref, turned_ref, kv_ref, seg_ref, 0, acc_ref)
    store_keys(out_ref, 0, both)
    out_ref[:, 256:304, :] = fin_ref[...]


def back_second_kernel(
    qa_ref, doa_ref, turned_ref, acc_in, kv_ref, seg_ref, out_ref, acc_ref
):
    step = pl.program_id(0)

    @pl.when(step == 0)
    def _():
        acc_ref[...] = acc_in[...]

    both = backward_step(qa_ref, doa_ref, turned_ref, kv_ref, seg_ref, HALF, acc_ref)
    store_keys(out_ref, step * BWD_C, both)

    @pl.when(step == pl.num_programs(0) - 1)
    def _():
        for r in range(NROW):
            for c in range(NCOL):
                block = pack(acc_ref, SHARE * (r * NCOL + c), 0, 0.125)
                out_ref[c, 256 + 16 * r : 272 + 16 * r, :] = block


SEG_BACK = whole((SLOTS, TOK))
BACK_STEPS = NCOL // BWD_C


def attend_back_first(arrived, grad, qa, o, fin, seg):
    return pl.pallas_call(
        back_first_kernel,
        grid=(BACK_STEPS,),
        out_shape=(
            pltpu.HBM((NCOL, 304, 128), BF),
            pltpu.HBM((ROWS, 80), BF),
            pltpu.HBM((128, ROWS), BF),
            pltpu.HBM((ROWS, 128), F32),
        ),
        in_specs=[
            Q_BLOCK,
            whole((SLOTS, 16, 128)),
            whole((ROWS, AUG)),
            whole((ROWS, HDIM)),
            pl.BlockSpec((BWD_C, 48, 128), lambda i: (i, 0, 0)),
            pl.BlockSpec((BWD_C, HALF * TOK, 128), lambda i: (i, 0, 0)),
            SEG_BACK,
        ],
        out_specs=[
            pl.BlockSpec((BWD_C, 304, 128), lambda i: (i, 0, 0)),
            whole((ROWS, 80)),
            whole((128, ROWS)),
            whole((ROWS, 128)),
        ],
        scratch_shapes=[pltpu.VMEM((ROWS, 128), F32)],
        compiler_params=params("attend_back_first"),
        cost_estimate=cost(18),
        name="attend_back_first",
    )(arrived, grad, qa, o, fin, arrived, seg)


def attend_back_second(qa, doa, turned, acc, arrived, seg):
    return pl.pallas_call(
        back_second_kernel,
        grid=(BACK_STEPS,),
        out_shape=pltpu.HBM((NCOL, 320, 128), BF),
        in_specs=[
            whole((ROWS, AUG)),
            whole((ROWS, 80)),
            whole((128, ROWS)),
            whole((ROWS, 128)),
            pl.BlockSpec((BWD_C, HALF * TOK, 128), lambda i: (i, 1, 0)),
            SEG_BACK,
        ],
        out_specs=whole((NCOL, 320, 128)),
        scratch_shapes=[pltpu.VMEM((ROWS, 128), F32)],
        compiler_params=params("attend_back_second"),
        cost_estimate=cost(18),
        name="attend_back_second",
    )(qa, doa, turned, acc, arrived, seg)


def heads_of(block):
    return jnp.concatenate(
        [
            jnp.concatenate([block[64 * h : 64 * (h + 1), 64 * k : 64 * (k + 1)] for h in range(3)], axis=1)
            for k in range(2)
        ],
        axis=0,
    )


def room(k):
    return min(SHARE, TOK - SHARE * k)


def feature_mean(v):
    return jnp.sum(v, axis=1, keepdims=True) * (1.0 / DIM)


def tokenwise_kernel(
    row_ref, att_ref, x_ref, cot_ref, vec_ref, upb_ref, all_ref,
    same_ref, sent_ref, datt_ref, fin_ref, dh1_ref,
    up_ref, down_ref, out_ref, slope_ref, att_scr, back_scr, sems,
):
    row = row_ref[0]
    copies = []
    for g in range(3):
        for k in range(2):
            for r in range(NROW):
                copies.append(
                    pltpu.make_async_copy(
                        all_ref.at[k, r, :, 96:112, g * 128 : (g + 1) * 128],
                        out_ref.at[k * NROW + r, :, 16 * g : 16 * (g + 1), :],
                        sems.at[0],
                    )
                )
    n_out = len(copies)
    for r in range(NROW):
        for k in range(2):
            lanes = slice(r * DIM + k * 384, r * DIM + (k + 1) * 384)
            copies.append(
                pltpu.make_async_copy(all_ref.at[k, r, :, 0:48, :], up_ref.at[:, :, lanes], sems.at[1 + r])
            )
    for r in range(NROW):
        for k in range(2):
            lanes = slice(r * DIM + k * 384, r * DIM + (k + 1) * 384)
            copies.append(
                pltpu.make_async_copy(all_ref.at[k, r, :, 48:96, :], down_ref.at[:, :, lanes], sems.at[5 + r])
            )
    for copy in copies:
        copy.start()

    def wait(group):
        chosen = copies[:n_out] if group == 0 else copies[n_out + 2 * (group - 1) : n_out + 2 * group]
        for copy in chosen:
            copy.wait()

    tok = x_ref[...].reshape(DIM, TOK).astype(F32).T
    cot = cot_ref[...].reshape(DIM, TOK).astype(F32).T
    vecs = vec_ref[...].reshape(DIM, TOK).astype(F32).T[64:128]
    out_b, gain_1, shift_1, down_b, gain_2, shift_2 = [
        vecs[i : i + 1] + vecs[6 + i : 7 + i] + vecs[12 + i : 13 + i] for i in range(6)
    ]
    gap = jnp.zeros((TOK, 32), BF)

    for r in range(NROW):
        for j in range(15):
            h, k = j // PER_HEAD, j % PER_HEAD
            unpack(att_ref[r * NCOL + j], att_scr, SHARE * k, 192 * r + HDIM * h, room(k))
    for r in range(NROW):
        target = lax.rem(r + NROW - row, NROW)
        for h in range(3):
            lanes = slice(192 * r + HDIM * h, 192 * r + HDIM * (h + 1))
            both = jnp.concatenate([att_scr[0:64, lanes], att_scr[64:128, lanes]], axis=1)
            at = A_AT - SAME + 64 * h
            sent_ref[target, at : at + 64, :] = both.astype(BF)
    wait(0)
    attn = jnp.zeros((TOK, DIM), F32)
    for r in range(NROW):
        for k in range(2):
            lanes = slice(192 * r + 96 * k, 192 * r + 96 * (k + 1))
            piece = jnp.concatenate([att_scr[:, lanes].astype(BF), gap], axis=1)
            attn = attn + dot(piece, out_ref[k * NROW + r].reshape(DIM, 128), 1, 1)
    h1 = tok + (attn + out_b)
    off = h1 - feature_mean(h1)
    inv1 = lax.rsqrt(feature_mean(off * off) + EPS)
    xhat1 = off * inv1
    n1 = xhat1 * gain_1 + shift_1
    n1_low = n1.astype(BF)

    branch = jnp.zeros((TOK, DIM), F32)
    for r in range(NROW):
        wait(1 + r)
        cols = slice(r * DIM, (r + 1) * DIM)
        pre = dot(n1_low, up_ref[:, :, cols].reshape(DIM, DIM), 1, 0) + upb_ref[r : r + 1, :]
        phi = 0.5 * (1.0 + lax.erf(pre * (1.0 / math.sqrt(2.0))))
        act = (pre * phi).astype(BF)
        slope_ref[:, cols] = phi + pre * jnp.exp(-0.5 * pre * pre) * (1.0 / math.sqrt(2.0 * math.pi))
        for i in range(6):
            at = DIM + i * TOK
            sent_ref[lax.rem(r + NROW - row, NROW), at : at + TOK, :] = act[:, i * TOK : (i + 1) * TOK]
        wait(5 + r)
        branch = branch + dot(act, down_ref[:, :, cols].reshape(DIM, DIM), 1, 1)
    h2 = n1 + (branch + down_b)
    off = h2 - feature_mean(h2)
    inv2 = lax.rsqrt(feature_mean(off * off) + EPS)
    xhat2 = off * inv2
    fin_ref[...] = (xhat2 * gain_2 + shift_2).T.astype(BF).reshape(NCOL, 48, TOK)
    dx = cot * gain_2
    dh2 = inv2 * (dx - feature_mean(dx) - xhat2 * feature_mean(dx * xhat2))
    d_branch = dh2.astype(BF)

    back = jnp.zeros((TOK, DIM), F32)
    for r in range(NROW):
        cols = slice(r * DIM, (r + 1) * DIM)
        d_act = dot(d_branch, down_ref[:, :, cols].reshape(DIM, DIM), 1, 0)
        d_pre = (d_act * slope_ref[:, cols]).astype(BF)
        for i in range(6):
            at = i * TOK
            sent_ref[lax.rem(r + NROW - row, NROW), at : at + TOK, :] = d_pre[:, i * TOK : (i + 1) * TOK]
        back = back + dot(d_pre, up_ref[:, :, cols].reshape(DIM, DIM), 1, 1)
    up1 = dh2 + back
    dx = up1 * gain_1
    dh1 = inv1 * (dx - feature_mean(dx) - xhat1 * feature_mean(dx * xhat1))
    d_attn = dh1.astype(BF)
    back_scr[TOK : TOK + 8, :] = jnp.zeros((8, 192), F32)
    for r in range(NROW):
        pieces = [dot(d_attn, out_ref[k * NROW + r].reshape(DIM, 128), 1, 0)[:, 0:96] for k in range(2)]
        back_scr[0:TOK, :] = jnp.concatenate(pieces, axis=1)
        for j in range(15):
            h, k = j // PER_HEAD, j % PER_HEAD
            datt_ref[r * NCOL + j] = pack(back_scr, SHARE * k, HDIM * h)
        datt_ref[r * NCOL + 15] = jnp.zeros((16, 128), BF)
    turned = dh1.T
    dh1_ref[...] = turned
    shared = [n1.T.astype(BF), dh2.T.astype(BF), turned.astype(BF)]
    sums = [
        jnp.sum(v, axis=0, keepdims=True) for v in (up1 * xhat1, up1, cot * xhat2, cot)
    ]
    rows = []
    for part in range(2):
        for v in sums:
            hi = v.astype(BF).astype(F32)
            piece = hi if part == 0 else v - hi
            rows += [piece[:, i * 128 : (i + 1) * 128] for i in range(6)]
    shared.append(jnp.concatenate(rows, axis=0).astype(BF))
    at = 0
    for v in shared:
        same_ref[at : at + v.shape[0], :] = v
        at += v.shape[0]


def tokenwise(row, att, x_t, arrived, wj, up_bias, everything):
    return pl.pallas_call(
        tokenwise_kernel,
        out_shape=(
            pltpu.HBM((SAME, TOK), BF),
            pltpu.HBM((NROW, SENT - SAME, TOK), BF),
            pltpu.HBM((SLOTS, 16, 128), BF),
            pltpu.HBM((NCOL, 48, TOK), BF),
            pltpu.HBM((DIM, TOK), F32),
        ),
        grid=(1,),
        in_specs=[
            SMEM,
            whole((SLOTS, 16, 128)),
            whole((NCOL, 48, TOK)),
            pl.BlockSpec((NCOL, 48, TOK), lambda i: (0, C_AT // 48, 0)),
            pl.BlockSpec((NCOL, 48, TOK), lambda i: (0, 0, 1)),
            whole((NROW, DIM)),
            pl.BlockSpec(memory_space=pl.ANY),
        ],
        out_specs=[
            whole((SAME, TOK)),
            whole((NROW, SENT - SAME, TOK)),
            whole((SLOTS, 16, 128)),
            whole((NCOL, 48, TOK)),
            whole((DIM, TOK)),
        ],
        scratch_shapes=[
            pltpu.VMEM((NCOL, 48, FF), BF),
            pltpu.VMEM((NCOL, 48, FF), BF),
            pltpu.VMEM((2 * NROW, NCOL, 48, 128), BF),
            pltpu.VMEM((TOK, FF), F32),
            pltpu.VMEM((TOK, DIM), F32),
            pltpu.VMEM((TOK + 8, 192), F32),
            pltpu.SemaphoreType.DMA((9,)),
        ],
        compiler_params=params("tokenwise"),
        cost_estimate=cost(15),
        name="tokenwise",
    )(row, att, x_t, arrived, wj, up_bias, everything)


def weight_grads_kernel(core_ref, *refs):
    got, out_ref = refs[:-1], refs[-1]

    def feats(at):
        return jnp.concatenate([ref[at : at + DIM, :] for ref in got], axis=1)

    def hidden(at, begin, end):
        return jnp.concatenate(
            [
                jnp.concatenate(
                    [ref[at + i * TOK : at + (i + 1) * TOK, :] for i in range(begin, end)], axis=1
                )
                for ref in got
            ],
            axis=0,
        )

    def keep(at, g):
        for i in range(g.shape[1] // 128):
            piece = g[:, i * 128 : (i + 1) * 128].astype(BF).reshape(NCOL, 48, 128)
            out_ref[:, at + 48 * i : at + 48 * (i + 1), :] = piece

    @pl.when(core_ref[0] == 0)
    def _():
        keep(0, dot(feats(0), hidden(3 * DIM + 48, 0, 6), 1, 0))
        keep(288, dot(feats(DIM), hidden(4 * DIM + 48, 0, 2), 1, 0))

    @pl.when(core_ref[0] != 0)
    def _():
        d_branch = feats(DIM)
        d_attn = feats(2 * DIM)
        keep(0, dot(d_branch, hidden(4 * DIM + 48, 2, 6), 1, 0))
        att = [heads_of(ref[A_AT:SENT, :].astype(F32)).astype(BF) for ref in got]
        att = jnp.concatenate(att, axis=0)
        att = jnp.concatenate([att, jnp.zeros((att.shape[0], 64), BF)], axis=1)
        keep(192, dot(d_attn, att, 1, 0))
        d_pre = hidden(3 * DIM + 48, 0, 6)
        ones = jnp.ones((16, d_pre.shape[0]), BF)
        sums = [dot(ones, d_branch, 1, 1)[0:1], dot(ones, d_attn, 1, 1)[0:1], dot(ones, d_pre, 1, 0)[0:1]]
        norm = got[0][3 * DIM : 3 * DIM + 48, :].astype(F32)
        for ref in got[1:]:
            norm = norm + ref[3 * DIM : 3 * DIM + 48, :].astype(F32)
        rows = [norm[0:24] + norm[24:48]]
        for v in sums:
            rows += [v[:, i * 128 : (i + 1) * 128] for i in range(6)]
        rows.append(jnp.zeros((6, 128), F32))
        rows = jnp.concatenate(rows, axis=0)
        hi = rows.astype(BF)
        lo = (rows - hi.astype(F32)).astype(BF)
        misc = jnp.concatenate([hi, lo], axis=0)
        out_ref[:, 288:384, :] = jnp.broadcast_to(misc[None], (NCOL, 96, 128))


def weight_grads(core, got, theirs):
    shape = (NCOL, WROWS // 2, 128)
    return pl.pallas_call(
        weight_grads_kernel,
        grid=(1,),
        out_shape=pltpu.HBM(shape, BF),
        in_specs=[SMEM] + [whole((SENT, TOK))] * 8,
        out_specs=whole(shape),
        compiler_params=params("weight_grads"),
        cost_estimate=cost(1),
        name="weight_grads",
    )(core, *got, *theirs)


def place(core, mine_ref, other_ref, blocks, half_rows):
    for at, block in blocks:
        low = at < half_rows
        local = at if low else at - half_rows
        rows = slice(local, local + block.shape[1])
        keep = core == (0 if low else 1)

        @pl.when(keep)
        def _():
            mine_ref[:, rows, :] = block

        @pl.when(jnp.logical_not(keep))
        def _():
            other_ref[:, rows, :] = block


def project_back_kernel(
    core_ref, first_ref, second_ref, w_ref, x_ref, din_ref, mine_ref, other_ref, layer_ref, scr
):
    core = core_ref[0]
    layer_ref[...] = jnp.concatenate([first_ref[c, 256:304, :] for c in range(NCOL)], axis=1)
    scr[...] = jnp.zeros_like(scr)
    for j in range(15):
        h, k = j // PER_HEAD, j % PER_HEAD
        for r in range(NROW):
            block = second_ref[j, 256 + 16 * r : 272 + 16 * r, :]
            unpack(block, scr, r * TOK + SHARE * k, HDIM * h, room(k))
    dq = scr[...].T.astype(BF)
    w = w_ref[...].reshape(DIM, JW)
    grad = jnp.zeros((DIM, JW), F32)
    total = jnp.zeros((16, JW), F32)
    ones = jnp.ones((16, TOK), BF)
    for r in range(NROW):
        source, at = (first_ref, r) if r < HALF else (second_ref, r - HALF)
        parts = [dq[:, r * TOK : (r + 1) * TOK]]
        for h in range(3):
            acc = source[PER_HEAD * h, at * TOK : (at + 1) * TOK, :].astype(F32)
            for k in range(1, PER_HEAD):
                acc = acc + source[PER_HEAD * h + k, at * TOK : (at + 1) * TOK, :].astype(F32)
            parts.append(acc.astype(BF))
        d_proj = jnp.concatenate(parts, axis=0)
        din_ref[r] = dot(w, d_proj, 1, 0).astype(BF)
        grad = grad + dot(x_ref[r], d_proj, 1, 1)
        total = total + dot(ones, d_proj, 1, 1)
    rows = [total[0:1, i * 128 : (i + 1) * 128] for i in range(5)] + [jnp.zeros((3, 128), F32)]
    rows = jnp.concatenate(rows, axis=0)
    hi = rows.astype(BF)
    lo = (rows - hi.astype(F32)).astype(BF)
    misc = jnp.broadcast_to(jnp.concatenate([hi, lo], axis=0)[None], (NCOL, 16, 128))
    low = grad.astype(BF)
    pieces = [low[:, i * 128 : (i + 1) * 128].reshape(NCOL, 48, 128) for i in range(5)]
    blocks = [(0, pieces[0]), (48, pieces[1]), (96, pieces[2][:, 0:32]), (128, pieces[2][:, 32:48])]
    blocks += [(144, pieces[3]), (192, pieces[4]), (240, misc)]
    place(core, mine_ref, other_ref, blocks, 128)


def project_back(core, first, second, wj, x4):
    kind = pltpu.HBM((NCOL, 128, 128), BF)
    return pl.pallas_call(
        project_back_kernel,
        out_shape=(
            pltpu.HBM((NROW, DIM, TOK), BF),
            kind,
            kind,
            pltpu.HBM((48, NCOL * TOK), BF),
        ),
        in_specs=[SMEM] + [VMEM] * 4,
        out_specs=[VMEM] * 4,
        scratch_shapes=[pltpu.VMEM((512, 256), F32)],
        compiler_params=params("project_back"),
        cost_estimate=cost(5),
        name="project_back",
    )(core, first, second, wj, x4)


def last_kernel(mine_ref, theirs_ref, din_ref, dh1_ref, out_ref):
    out_ref[:, 0:128, :] = (mine_ref[...].astype(F32) + theirs_ref[...].astype(F32)).astype(BF)
    total = dh1_ref[...]
    for r in range(NROW):
        total = total + din_ref[r].astype(F32)
    out_ref[:, 128:176, :] = total.astype(BF).reshape(NCOL, 48, TOK)


def last_payload(mine, theirs, din, dh1):
    return pl.pallas_call(
        last_kernel,
        out_shape=pltpu.HBM((NCOL, 176, 128), BF),
        in_specs=[VMEM] * 4,
        out_specs=VMEM,
        compiler_params=params("last_payload"),
        cost_estimate=cost(1),
        name="last_payload",
    )(mine, theirs, din, dh1)


def join(core_ref, mine, theirs):
    first = core_ref[0] == 0
    a, b = mine[...], theirs[...]
    return jnp.concatenate([jnp.where(first, a, b), jnp.where(first, b, a)], axis=0)


def finish_kernel(
    core_ref, col_ref, wide_ref, other_ref, out_ref, up_ref, up_bias_ref, down_ref, *own_refs
):
    wide = join(core_ref, wide_ref, other_ref)
    for i in range(6):
        lanes = slice(i * 128, (i + 1) * 128)
        up_ref[:, lanes] = wide[48 * i : 48 * (i + 1)]
        down_ref[:, lanes] = wide[288 + 48 * i : 288 + 48 * (i + 1)]
    out_ref[...] = jnp.concatenate([wide[576:624], wide[624:672, 0:64]], axis=1)
    vecs = wide[672:720] + wide[720:768]
    up_bias_ref[...] = vecs[36:42]
    rows = [
        jnp.concatenate([vecs[6 * v + i : 6 * v + i + 1] for i in range(6)], axis=1) for v in range(6)
    ]
    rows = jnp.concatenate(rows + [jnp.zeros((2, DIM), F32)], axis=0)
    feature = lax.broadcasted_iota(jnp.int32, (DIM, 48), 0)
    lane = lax.broadcasted_iota(jnp.int32, (DIM, 48), 1)
    pick = jnp.where(feature == col_ref[0] * 48 + lane, 1.0, 0.0).astype(BF)
    own = sum(dot(part, pick, 1, 0) for part in split3(rows))
    for v, ref in enumerate(own_refs):
        ref[...] = own[v : v + 1]


def finish(core, col, wide, other):
    shapes = [(48, 192), (48, DIM), (6, 128), (48, DIM)] + [(1, 48)] * 6
    return pl.pallas_call(
        finish_kernel,
        out_shape=[pltpu.HBM(shape, F32) for shape in shapes],
        in_specs=[SMEM] * 2 + [VMEM] * 2,
        out_specs=[VMEM] * len(shapes),
        compiler_params=params("finish"),
        cost_estimate=cost(1),
        name="finish",
    )(core, col, wide, other)


def joint_kernel(core_ref, last_ref, other_ref, joint_ref, joint_bias_ref):
    last = join(core_ref, last_ref, other_ref)
    chunks = [last[48 * i : 48 * (i + 1)] for i in range(5)]
    heads = [chunks[0][:, 0:64], chunks[0][:, 64:128], chunks[1][:, 0:64]]
    joint_ref[...] = jnp.concatenate([v for h in range(3) for v in (heads[h], chunks[2 + h])], axis=1)
    sums = last[240:248] + last[248:256]
    heads = [sums[0:1, 0:64], sums[0:1, 64:128], sums[1:2, 0:64]]
    joint_bias_ref[...] = jnp.concatenate(
        [jnp.concatenate([heads[h], sums[2 + h : 3 + h, 64:128]], axis=1) for h in range(3)], axis=0
    )


def joint_gradient(core, last, other):
    return pl.pallas_call(
        joint_kernel,
        out_shape=[pltpu.HBM(shape, F32) for shape in ((48, 576), (3, 128))],
        in_specs=[SMEM] + [VMEM] * 2,
        out_specs=[VMEM] * 2,
        compiler_params=params("joint_gradient"),
        cost_estimate=cost(1),
        name="joint_gradient",
    )(core, last, other)


def exchange(blocks, axis):
    return lax.all_to_all(blocks, axis, 0, 0, tiled=True)


def around(v, axis, shift):
    return lax.ppermute(v, axis, [(i, (i + shift) % 4) for i in range(4)])


def swap_cores(v):
    return lax.ppermute(v, "dp", [(0, 1), (1, 0)])


def per_device(
    inputs,
    segments,
    joint_weight,
    joint_bias,
    output_weight,
    output_bias,
    first_norm_gain,
    shift_first,
    up_weight,
    up_bias,
    down_weight,
    down_bias,
    second_norm_gain,
    second_norm_shift,
    cotangent,
):
    core = lax.axis_index("dp")
    col = lax.axis_index(COL)
    row = lax.axis_index("row")
    my_z, my_y = lax.axis_index("z"), lax.axis_index("y")
    core_word = core.reshape(1).astype(jnp.int32)
    row_word = row.reshape(1).astype(jnp.int32)

    def by_col(a):
        return jnp.transpose(a.reshape(48, NCOL, TOK), (1, 0, 2))

    blocks = by_col(inputs)
    blocks, up_weight, down_weight, output_weight = lax.optimization_barrier(
        (blocks, up_weight, down_weight, output_weight)
    )
    x_t = exchange(blocks, COL)
    vectors = jnp.stack(
        [output_bias, first_norm_gain, shift_first, down_bias, second_norm_gain, second_norm_shift], axis=1
    )
    vectors = jnp.pad(jnp.concatenate(split3(vectors), axis=1), ((0, 0), (0, 46)))
    jw = joint_weight.reshape(48, 3, 3, HDIM)
    jw = jnp.concatenate([jw[:, :, 0].reshape(48, 192), vectors, jw[:, :, 1:].reshape(48, 384)], axis=1)
    jw = jnp.broadcast_to(jw[None], (NCOL, 48, JW))
    x_t, jw = lax.optimization_barrier((x_t, jw))
    wj = exchange(jw, COL)
    x4 = lax.all_gather(x_t.reshape(DIM, TOK), "row", axis=0, tiled=False)

    turned = lax.dynamic_slice_in_dim(output_weight, core * 96, 96, 0).T
    my_bias = lax.dynamic_slice_in_dim(up_bias, (core * NCOL + col) * 24, 24, 0)
    my_bias = jnp.pad(jnp.stack(split3(my_bias)), ((0, 45), (0, 8)))
    turned = jnp.concatenate([turned, my_bias], axis=1).reshape(3, 16, 128)
    turned = jnp.transpose(turned, (1, 0, 2)).reshape(16, 384)
    shard = jnp.concatenate(
        [
            lax.dynamic_slice_in_dim(up_weight, core * 384, 384, 1),
            lax.dynamic_slice_in_dim(down_weight, core * 384, 384, 1),
            turned,
        ],
        axis=0,
    )
    shard = lax.optimization_barrier((shard, x_t))[0]
    everything = lax.all_gather(shard, ("dp", "row", "z", "y"), axis=0, tiled=False)
    everything = everything.reshape(2, NROW, NCOL, 112, 384)
    up_b = jnp.sum(everything[:, :, :, 96:99, 96:120].astype(F32), axis=3)
    up_b = jnp.transpose(up_b, (1, 0, 2, 3)).reshape(NROW, DIM)

    bias3 = joint_bias.reshape(3, 2, HDIM)
    bias = jnp.concatenate(
        [
            bias3[:, 0].reshape(192),
            jnp.zeros((64,), F32),
            jnp.concatenate([jnp.zeros((3, HDIM), F32), bias3[:, 1]], axis=1).reshape(384),
        ]
    ).reshape(1, JW)
    seg = segments.reshape(SLOTS, TOK)
    shift = lax.rem(TOK - lax.rem(col, PER_HEAD) * SHARE, TOK).reshape(1).astype(jnp.int32)

    arrived = exchange(project(x4, wj, bias, by_col(cotangent)), COL)
    qa, o, o_blocks = attend(shift, arrived, seg)

    att = exchange(o_blocks, ALL)
    same, sent, d_blocks, fin, dh1 = tokenwise(row_word, att, x_t, arrived, wj, up_b, everything)

    d_blocks, same, sent = lax.optimization_barrier((d_blocks, same, sent))
    pieces = [jnp.concatenate([same, sent[d]], axis=0) for d in range(NROW)]
    grad_o = exchange(d_blocks, ALL)
    got = [around(pieces[d], "row", d) for d in range(1, NROW)]
    grad_o, own_piece = lax.optimization_barrier((grad_o, pieces[0]))
    back_a, doa, turned_qd, acc = attend_back_first(arrived, grad_o, qa, o, fin, seg)
    back_b = attend_back_second(qa, doa, turned_qd, acc, arrived, seg)
    back_a = exchange(back_a, COL)
    back_b, got, own_piece, back_a = lax.optimization_barrier((back_b, got, own_piece, back_a))
    got = [own_piece, *got]
    theirs = [swap_cores(v) for v in got]
    wide = weight_grads(core_word, got, theirs).reshape(4, 4, WROWS // 2, 128)
    back_b, back_a = lax.optimization_barrier((back_b, back_a))
    back_b = exchange(back_b, COL)
    near = [lax.dynamic_index_in_dim(wide, lax.rem(my_z + d, 4), 0, keepdims=False) for d in range(4)]
    near = [near[0]] + [around(near[d], "z", d) for d in range(1, 4)]
    wide = near[0].astype(F32) + near[1].astype(F32) + near[2].astype(F32) + near[3].astype(F32)
    wide = wide.astype(BF)

    din, mine_j, other_j, layer_output = project_back(core_word, back_a, back_b, wj, x4)
    theirs_j = swap_cores(other_j)
    din = exchange(din, "row")
    near = [lax.dynamic_index_in_dim(wide, lax.rem(my_y + d, 4), 0, keepdims=False) for d in range(4)]
    din, near = lax.optimization_barrier((din, near))
    near = [near[0]] + [around(near[d], "y", d) for d in range(1, 4)]
    mixed = exchange(last_payload(mine_j, theirs_j, din, dh1), COL)
    wide = near[0].astype(F32) + near[1].astype(F32) + near[2].astype(F32) + near[3].astype(F32)
    grad_out, grad_up, grad_up_bias, grad_down, *own = finish(
        core_word, col.reshape(1).astype(jnp.int32), wide, swap_cores(wide)
    )
    last = jnp.sum(mixed[:, :128].astype(F32), axis=0)
    grad_inputs = jnp.transpose(mixed[:, 128:].astype(F32), (1, 0, 2)).reshape(48, 2048)
    grad_joint, grad_joint_bias = joint_gradient(core_word, last, swap_cores(last))
    own = [v.reshape(48) for v in own]

    return (
        layer_output,
        grad_inputs,
        grad_joint,
        grad_joint_bias.reshape(384),
        grad_out.T,
        own[5],
        own[0],
        own[1],
        grad_up,
        grad_up_bias.reshape(768),
        grad_down,
        own[4],
        own[2],
        own[3],
    )


def solution(mesh):
    sizes = (mesh.shape["dp"], mesh.shape["row"], 4, 4)
    fine = jax.sharding.Mesh(mesh.devices.reshape(sizes), ("dp", "row", "z", "y"))
    grid = P(COL, ("dp", "row"))
    block = P(COL, "row")
    return jax.shard_map(
        per_device,
        mesh=fine,
        in_specs=(
            grid, P("dp", None), block, P("row"), P("row", COL), P(COL), P(COL), P(COL),
            block, P("row"), block, P(COL), P(COL), P(COL), grid,
        ),
        out_specs=(
            grid, grid, block, P("row"), P("row", COL), P(COL), P(COL), P(COL),
            block, P("row"), block, P(COL), P(COL), P(COL),
        ),
        check_vma=False,
    )
```

```python
import math

import jax
import jax.numpy as jnp
from jax import lax
from jax.experimental import pallas as pl
from jax.experimental.pallas import tpu as pltpu
from jax.sharding import PartitionSpec as P

HDIM = 64
EPS = 1e-06
BLOCK_OUT = -1e30
LOG2E = 1.4426950408889634
BF = jnp.bfloat16
F32 = jnp.float32

DIM = 768
FF = 3072
NCOL = 16
NROW = 4
TOK = 128
PER_HEAD = 5
SHARE = 26
SLOTS = NROW * NCOL
ROWS = SLOTS * SHARE
AUG = 144
JW = 640
HALF = 2
FWD_C = 2
BWD_C = 2
Q_AT = NROW * TOK
C_AT = Q_AT + 64
BLOCK = C_AT + 48
MIB = 2**20
COL = ("z", "y")
ALL = ("row", "z", "y")
VMEM = pl.BlockSpec(memory_space=pltpu.VMEM)
SMEM = pl.BlockSpec(memory_space=pltpu.SMEM)
A_AT = 5 * DIM + 48
SENT = A_AT + 192
SAME = 3 * DIM + 48
WROWS = 768


def split3(v):
    hi = v.astype(BF)
    rest = v - hi.astype(F32)
    mid = rest.astype(BF)
    low = (rest - mid.astype(F32)).astype(BF)
    return hi, mid, low


def dot(a, b, ca, cb):
    return lax.dot_general(a, b, (((ca,), (cb,)), ((), ())), preferred_element_type=F32)


LIMITS = {
    "project": 16,
    "attend": 32,
    "attend_back_first": 63.9,
    "attend_back_second": 63.9,
    "tokenwise": 63.9,
    "weight_grads": 63.9,
    "project_back": 63.9,
    "last_payload": 12,
    "finish": 12,
    "joint_gradient": 8,
}


def params(name):
    return pltpu.CompilerParams(vmem_limit_bytes=int(LIMITS[name] * MIB))


def cost(us):
    return pl.CostEstimate(flops=int(us * 1e9), bytes_accessed=int(us * 2e6), transcendentals=0)


Q_BLOCK = pl.BlockSpec((NCOL, 64, 128), lambda i: (0, Q_AT // 64, 0))


def whole(shape):
    return pl.BlockSpec(shape, lambda i: (0,) * len(shape))


def pack(ref, at, lane, scale=None):
    lanes = slice(lane, lane + HDIM)
    rest = jnp.concatenate([ref[at + 16 : at + SHARE, lanes], jnp.zeros((6, HDIM), F32)], axis=0)
    both = jnp.concatenate([ref[at : at + 16, lanes], rest], axis=1)
    return (both if scale is None else both * scale).astype(BF)


def unpack(block, ref, at, lane, rows=SHARE):
    block = block.astype(F32)
    lanes = slice(lane, lane + HDIM)
    ref[at : at + 16, lanes] = block[:, 0:64]
    ref[at + 16 : at + rows, lanes] = block[0 : rows - 16, 64:128]


def project_kernel(x_ref, w_ref, b_ref, cot_ref, out_ref, q_ref):
    w = w_ref[...].reshape(DIM, JW)
    q_ref[...] = jnp.zeros_like(q_ref)
    for r in range(NROW):
        tokens = x_ref[r].astype(F32).T.astype(BF)
        y = dot(tokens, w, 1, 0) + b_ref[...]
        q_ref[r * TOK : (r + 1) * TOK, :] = y[:, 0:256]
        for h in range(3):
            kv = y[:, 256 + 128 * h : 384 + 128 * h].T.astype(BF)
            for j in range(PER_HEAD * h, PER_HEAD * (h + 1) + (1 if h == 2 else 0)):
                out_ref[j, r * TOK : (r + 1) * TOK, :] = kv
    for j in range(NCOL):
        h, k = min(j, 14) // PER_HEAD, min(j, 14) % PER_HEAD
        for r in range(NROW):
            at = r * TOK + SHARE * k
            out_ref[j, Q_AT + 16 * r : Q_AT + 16 * (r + 1), :] = pack(q_ref, at, HDIM * h)
    out_ref[:, C_AT:BLOCK, :] = cot_ref[...]


def project(x4, wj, bias, cot):
    return pl.pallas_call(
        project_kernel,
        out_shape=pltpu.HBM((NCOL, BLOCK, 128), BF),
        in_specs=[VMEM] * 4,
        out_specs=VMEM,
        scratch_shapes=[pltpu.VMEM((640, 256), F32)],
        compiler_params=params("project"),
        cost_estimate=cost(3),
        name="project",
    )(x4, wj, bias, cot)


def key_rows(seg_row):
    row = lax.broadcasted_iota(jnp.int32, (16, seg_row.shape[1]), 0)
    hot = jnp.where(row < 5, jnp.where(row == seg_row, 1.0, 0.0), jnp.where(row < 8, 1.0, 0.0))
    return hot.astype(BF)


def offset_columns(value, base):
    h, m, l = split3(-value)
    lane = lax.broadcasted_iota(jnp.int32, base.shape, 1)
    return jnp.where(
        lane == 5,
        h.astype(F32),
        jnp.where(lane == 6, m.astype(F32), jnp.where(lane == 7, l.astype(F32), base)),
    )


def key_block(kv_ref, seg_ref, begin):
    pairs = [(c, r) for c in range(kv_ref.shape[0]) for r in range(kv_ref.shape[1] // TOK)]
    tiles = [kv_ref[c, r * TOK : (r + 1) * TOK, :] for c, r in pairs]
    at = pl.program_id(0) * kv_ref.shape[0]
    extra = [key_rows(seg_ref[pl.ds((begin + r) * NCOL + at + c, 1), :]) for c, r in pairs]
    return jnp.concatenate(tiles, axis=1), jnp.concatenate(extra, axis=1)


def forward_step(qa_ref, kv_ref, seg_ref, acc_ref, top_ref):
    kvt, extra = key_block(kv_ref, seg_ref, 0)
    kt = jnp.concatenate([kvt[0:64], kvt[0:64], extra], axis=0)
    turned = kvt.astype(F32).T
    lane = lax.broadcasted_iota(jnp.int32, turned.shape, 1)
    va = jnp.where(lane >= 64, turned, jnp.where(lane == 0, 1.0, 0.0)).astype(BF)
    s = dot(qa_ref[...], kt, 1, 0)
    parts = [s[:, i * 128 : (i + 1) * 128] for i in range(s.shape[1] // 128)]
    high = parts[0]
    for part in parts[1:]:
        high = jnp.maximum(high, part)
    top = top_ref[...]
    raised = jnp.maximum(top, jnp.broadcast_to(jnp.max(high, axis=1, keepdims=True), top.shape))
    p = jnp.concatenate([jnp.exp2(part - raised).astype(BF) for part in parts], axis=1)
    fade = jnp.exp2(top - raised)
    top_ref[...] = raised
    acc_ref[...] = acc_ref[...] * fade + dot(p, va, 1, 0)


def attend_kernel(
    shift_ref, q_ref, kv_ref, seg_ref, qa_ref, o_ref, out_ref, q_scr, pen_scr, acc_ref, top_ref
):
    @pl.when(pl.program_id(0) == 0)
    def _():
        columns = pltpu.roll(seg_ref[...].astype(F32), shift_ref[0], 1).T
        lane = lax.broadcasted_iota(jnp.int32, (SHARE, 16), 1)
        seg = lane.astype(F32)
        for r in range(NROW):
            for c in range(NCOL):
                slot = r * NCOL + c
                unpack(q_ref[c, 16 * r : 16 * (r + 1), :], q_scr, SHARE * slot, 0)
                pen_scr[SHARE * slot : SHARE * (slot + 1), :] = jnp.where(
                    (lane < 5) & (seg != columns[0:SHARE, slot : slot + 1]), BLOCK_OUT, 0.0
                )
        scaled = q_scr[...] * (LOG2E / 8.0)
        hi = scaled.astype(BF)
        lo = (scaled - hi.astype(F32)).astype(BF)
        pen = pen_scr[...]
        qa_ref[...] = jnp.concatenate([hi, lo, pen.astype(BF)], axis=1)
        acc_ref[...] = jnp.zeros_like(acc_ref)
        top_ref[...] = jnp.full_like(top_ref, -3e38)

    forward_step(qa_ref, kv_ref, seg_ref, acc_ref, top_ref)

    @pl.when(pl.program_id(0) == pl.num_programs(0) - 1)
    def _():
        acc = acc_ref[...]
        total = acc[:, 0:1]
        o_ref[...] = acc[:, 64:128] / total
        lse = top_ref[:, 0:1] + jnp.log(total) * LOG2E
        qa_ref[:, 128:144] = offset_columns(lse, qa_ref[:, 128:144].astype(F32)).astype(BF)
        for slot in range(SLOTS):
            out_ref[slot] = pack(o_ref, SHARE * slot, 0)


def attend(shift, arrived, seg):
    return pl.pallas_call(
        attend_kernel,
        grid=(NCOL // FWD_C,),
        out_shape=(
            pltpu.HBM((ROWS, AUG), BF),
            pltpu.HBM((ROWS, HDIM), F32),
            pltpu.HBM((SLOTS, 16, 128), BF),
        ),
        in_specs=[
            SMEM,
            Q_BLOCK,
            pl.BlockSpec((FWD_C, Q_AT, 128), lambda i: (i, 0, 0)),
            whole((SLOTS, TOK)),
        ],
        out_specs=[whole((ROWS, AUG)), whole((ROWS, HDIM)), whole((SLOTS, 16, 128))],
        scratch_shapes=[
            pltpu.VMEM((ROWS, HDIM), F32),
            pltpu.VMEM((ROWS, 16), F32),
            pltpu.VMEM((ROWS, 128), F32),
            pltpu.VMEM((ROWS, 128), F32),
        ],
        compiler_params=params("attend"),
        cost_estimate=cost(20),
        name="attend",
    )(shift, arrived, arrived, seg)


def backward_step(qa_ref, doa_ref, turned_ref, kv_ref, seg_ref, begin, acc_ref):
    kvt, extra = key_block(kv_ref, seg_ref, begin)
    kt = jnp.concatenate([kvt[0:64], kvt[0:64], extra], axis=0)
    vt = jnp.concatenate([kvt[64:128], extra], axis=0)
    keys = kvt.astype(F32).T.astype(BF)
    p = jnp.exp2(dot(qa_ref[...], kt, 1, 0))
    dp = dot(doa_ref[...], vt, 1, 0)
    ds = (p * dp).astype(BF)
    acc_ref[...] += dot(ds, keys, 1, 0)
    dk = dot(turned_ref[0:64, :], ds, 1, 0) * 0.125
    dv = dot(turned_ref[64:128, :], p.astype(BF), 1, 0)
    return jnp.concatenate([dk, dv], axis=0).astype(BF)


def store_keys(out_ref, at, both):
    for c in range(BWD_C):
        for r in range(HALF):
            i = c * HALF + r
            out_ref[at + c, r * TOK : (r + 1) * TOK, :] = both[:, i * TOK : (i + 1) * TOK]


def back_first_kernel(
    q_ref, do_ref, qa_ref, o_ref, fin_ref, kv_ref, seg_ref, out_ref, doa_ref, turned_ref, acc_ref, pair_scr
):
    @pl.when(pl.program_id(0) == 0)
    def _():
        for r in range(NROW):
            for c in range(NCOL):
                slot = r * NCOL + c
                unpack(q_ref[c, 16 * r : 16 * (r + 1), :], pair_scr, SHARE * slot, 0)
                unpack(do_ref[slot], pair_scr, SHARE * slot, HDIM)
        pairs = pair_scr[...]
        turned_ref[...] = pairs.T.astype(BF)
        grad = pairs[:, 64:128]
        delta = jnp.sum(grad * o_ref[...], axis=1, keepdims=True)
        ext = offset_columns(delta, jnp.zeros((ROWS, 16), F32))
        doa_ref[...] = jnp.concatenate([grad.astype(BF), ext.astype(BF)], axis=1)
        acc_ref[...] = jnp.zeros_like(acc_ref)

    both = backward_step(qa_ref, doa_ref, turned_ref, kv_ref, seg_ref, 0, acc_ref)
    store_keys(out_ref, 0, both)
    out_ref[:, 256:304, :] = fin_ref[...]


def back_second_kernel(
    qa_ref, doa_ref, turned_ref, acc_in, kv_ref, seg_ref, out_ref, acc_ref
):
    step = pl.program_id(0)

    @pl.when(step == 0)
    def _():
        acc_ref[...] = acc_in[...]

    both = backward_step(qa_ref, doa_ref, turned_ref, kv_ref, seg_ref, HALF, acc_ref)
    store_keys(out_ref, step * BWD_C, both)

    @pl.when(step == pl.num_programs(0) - 1)
    def _():
        for r in range(NROW):
            for c in range(NCOL):
                block = pack(acc_ref, SHARE * (r * NCOL + c), 0, 0.125)
                out_ref[c, 256 + 16 * r : 272 + 16 * r, :] = block


SEG_BACK = whole((SLOTS, TOK))
BACK_STEPS = NCOL // BWD_C


def attend_back_first(arrived, grad, qa, o, fin, seg):
    return pl.pallas_call(
        back_first_kernel,
        grid=(BACK_STEPS,),
        out_shape=(
            pltpu.HBM((NCOL, 304, 128), BF),
            pltpu.HBM((ROWS, 80), BF),
            pltpu.HBM((128, ROWS), BF),
            pltpu.HBM((ROWS, 128), F32),
        ),
        in_specs=[
            Q_BLOCK,
            whole((SLOTS, 16, 128)),
            whole((ROWS, AUG)),
            whole((ROWS, HDIM)),
            pl.BlockSpec((BWD_C, 48, 128), lambda i: (i, 0, 0)),
            pl.BlockSpec((BWD_C, HALF * TOK, 128), lambda i: (i, 0, 0)),
            SEG_BACK,
        ],
        out_specs=[
            pl.BlockSpec((BWD_C, 304, 128), lambda i: (i, 0, 0)),
            whole((ROWS, 80)),
            whole((128, ROWS)),
            whole((ROWS, 128)),
        ],
        scratch_shapes=[pltpu.VMEM((ROWS, 128), F32)],
        compiler_params=params("attend_back_first"),
        cost_estimate=cost(18),
        name="attend_back_first",
    )(arrived, grad, qa, o, fin, arrived, seg)


def attend_back_second(qa, doa, turned, acc, arrived, seg):
    return pl.pallas_call(
        back_second_kernel,
        grid=(BACK_STEPS,),
        out_shape=pltpu.HBM((NCOL, 320, 128), BF),
        in_specs=[
            whole((ROWS, AUG)),
            whole((ROWS, 80)),
            whole((128, ROWS)),
            whole((ROWS, 128)),
            pl.BlockSpec((BWD_C, HALF * TOK, 128), lambda i: (i, 1, 0)),
            SEG_BACK,
        ],
        out_specs=whole((NCOL, 320, 128)),
        scratch_shapes=[pltpu.VMEM((ROWS, 128), F32)],
        compiler_params=params("attend_back_second"),
        cost_estimate=cost(18),
        name="attend_back_second",
    )(qa, doa, turned, acc, arrived, seg)


def heads_of(block):
    return jnp.concatenate(
        [
            jnp.concatenate([block[64 * h : 64 * (h + 1), 64 * k : 64 * (k + 1)] for h in range(3)], axis=1)
            for k in range(2)
        ],
        axis=0,
    )


def room(k):
    return min(SHARE, TOK - SHARE * k)


def feature_mean(v):
    return jnp.sum(v, axis=1, keepdims=True) * (1.0 / DIM)


def tokenwise_kernel(
    row_ref, att_ref, x_ref, cot_ref, vec_ref, upb_ref, all_ref,
    same_ref, sent_ref, datt_ref, fin_ref, dh1_ref,
    up_ref, down_ref, out_ref, slope_ref, att_scr, back_scr, sems,
):
    row = row_ref[0]
    copies = []
    for g in range(3):
        for k in range(2):
            for r in range(NROW):
                copies.append(
                    pltpu.make_async_copy(
                        all_ref.at[k, r, :, 96:112, g * 128 : (g + 1) * 128],
                        out_ref.at[k * NROW + r, :, 16 * g : 16 * (g + 1), :],
                        sems.at[0],
                    )
                )
    n_out = len(copies)
    for r in range(NROW):
        for k in range(2):
            lanes = slice(r * DIM + k * 384, r * DIM + (k + 1) * 384)
            copies.append(
                pltpu.make_async_copy(all_ref.at[k, r, :, 0:48, :], up_ref.at[:, :, lanes], sems.at[1 + r])
            )
    for r in range(NROW):
        for k in range(2):
            lanes = slice(r * DIM + k * 384, r * DIM + (k + 1) * 384)
            copies.append(
                pltpu.make_async_copy(all_ref.at[k, r, :, 48:96, :], down_ref.at[:, :, lanes], sems.at[5 + r])
            )
    for copy in copies:
        copy.start()

    def wait(group):
        chosen = copies[:n_out] if group == 0 else copies[n_out + 2 * (group - 1) : n_out + 2 * group]
        for copy in chosen:
            copy.wait()

    tok = x_ref[...].reshape(DIM, TOK).astype(F32).T
    cot = cot_ref[...].reshape(DIM, TOK).astype(F32).T
    vecs = vec_ref[...].reshape(DIM, TOK).astype(F32).T[64:128]
    out_b, gain_1, shift_1, down_b, gain_2, shift_2 = [
        vecs[i : i + 1] + vecs[6 + i : 7 + i] + vecs[12 + i : 13 + i] for i in range(6)
    ]
    gap = jnp.zeros((TOK, 32), BF)

    for r in range(NROW):
        for j in range(15):
            h, k = j // PER_HEAD, j % PER_HEAD
            unpack(att_ref[r * NCOL + j], att_scr, SHARE * k, 192 * r + HDIM * h, room(k))
    for r in range(NROW):
        target = lax.rem(r + NROW - row, NROW)
        for h in range(3):
            lanes = slice(192 * r + HDIM * h, 192 * r + HDIM * (h + 1))
            both = jnp.concatenate([att_scr[0:64, lanes], att_scr[64:128, lanes]], axis=1)
            at = A_AT - SAME + 64 * h
            sent_ref[target, at : at + 64, :] = both.astype(BF)
    wait(0)
    attn = jnp.zeros((TOK, DIM), F32)
    for r in range(NROW):
        for k in range(2):
            lanes = slice(192 * r + 96 * k, 192 * r + 96 * (k + 1))
            piece = jnp.concatenate([att_scr[:, lanes].astype(BF), gap], axis=1)
            attn = attn + dot(piece, out_ref[k * NROW + r].reshape(DIM, 128), 1, 1)
    h1 = tok + (attn + out_b)
    off = h1 - feature_mean(h1)
    inv1 = lax.rsqrt(feature_mean(off * off) + EPS)
    xhat1 = off * inv1
    n1 = xhat1 * gain_1 + shift_1
    n1_low = n1.astype(BF)

    branch = jnp.zeros((TOK, DIM), F32)
    for r in range(NROW):
        wait(1 + r)
        cols = slice(r * DIM, (r + 1) * DIM)
        pre = dot(n1_low, up_ref[:, :, cols].reshape(DIM, DIM), 1, 0) + upb_ref[r : r + 1, :]
        phi = 0.5 * (1.0 + lax.erf(pre * (1.0 / math.sqrt(2.0))))
        act = (pre * phi).astype(BF)
        slope_ref[:, cols] = phi + pre * jnp.exp(-0.5 * pre * pre) * (1.0 / math.sqrt(2.0 * math.pi))
        for i in range(6):
            at = DIM + i * TOK
            sent_ref[lax.rem(r + NROW - row, NROW), at : at + TOK, :] = act[:, i * TOK : (i + 1) * TOK]
        wait(5 + r)
        branch = branch + dot(act, down_ref[:, :, cols].reshape(DIM, DIM), 1, 1)
    h2 = n1 + (branch + down_b)
    off = h2 - feature_mean(h2)
    inv2 = lax.rsqrt(feature_mean(off * off) + EPS)
    xhat2 = off * inv2
    fin_ref[...] = (xhat2 * gain_2 + shift_2).T.astype(BF).reshape(NCOL, 48, TOK)
    dx = cot * gain_2
    dh2 = inv2 * (dx - feature_mean(dx) - xhat2 * feature_mean(dx * xhat2))
    d_branch = dh2.astype(BF)

    back = jnp.zeros((TOK, DIM), F32)
    for r in range(NROW):
        cols = slice(r * DIM, (r + 1) * DIM)
        d_act = dot(d_branch, down_ref[:, :, cols].reshape(DIM, DIM), 1, 0)
        d_pre = (d_act * slope_ref[:, cols]).astype(BF)
        for i in range(6):
            at = i * TOK
            sent_ref[lax.rem(r + NROW - row, NROW), at : at + TOK, :] = d_pre[:, i * TOK : (i + 1) * TOK]
        back = back + dot(d_pre, up_ref[:, :, cols].reshape(DIM, DIM), 1, 1)
    up1 = dh2 + back
    dx = up1 * gain_1
    dh1 = inv1 * (dx - feature_mean(dx) - xhat1 * feature_mean(dx * xhat1))
    d_attn = dh1.astype(BF)
    back_scr[TOK : TOK + 8, :] = jnp.zeros((8, 192), F32)
    for r in range(NROW):
        pieces = [dot(d_attn, out_ref[k * NROW + r].reshape(DIM, 128), 1, 0)[:, 0:96] for k in range(2)]
        back_scr[0:TOK, :] = jnp.concatenate(pieces, axis=1)
        for j in range(15):
            h, k = j // PER_HEAD, j % PER_HEAD
            datt_ref[r * NCOL + j] = pack(back_scr, SHARE * k, HDIM * h)
        datt_ref[r * NCOL + 15] = jnp.zeros((16, 128), BF)
    turned = dh1.T
    dh1_ref[...] = turned
    shared = [n1.T.astype(BF), dh2.T.astype(BF), turned.astype(BF)]
    sums = [
        jnp.sum(v, axis=0, keepdims=True) for v in (up1 * xhat1, up1, cot * xhat2, cot)
    ]
    rows = []
    for part in range(2):
        for v in sums:
            hi = v.astype(BF).astype(F32)
            piece = hi if part == 0 else v - hi
            rows += [piece[:, i * 128 : (i + 1) * 128] for i in range(6)]
    shared.append(jnp.concatenate(rows, axis=0).astype(BF))
    at = 0
    for v in shared:
        same_ref[at : at + v.shape[0], :] = v
        at += v.shape[0]


def tokenwise(row, att, x_t, arrived, wj, up_bias, everything):
    return pl.pallas_call(
        tokenwise_kernel,
        out_shape=(
            pltpu.HBM((SAME, TOK), BF),
            pltpu.HBM((NROW, SENT - SAME, TOK), BF),
            pltpu.HBM((SLOTS, 16, 128), BF),
            pltpu.HBM((NCOL, 48, TOK), BF),
            pltpu.HBM((DIM, TOK), F32),
        ),
        grid=(1,),
        in_specs=[
            SMEM,
            whole((SLOTS, 16, 128)),
            whole((NCOL, 48, TOK)),
            pl.BlockSpec((NCOL, 48, TOK), lambda i: (0, C_AT // 48, 0)),
            pl.BlockSpec((NCOL, 48, TOK), lambda i: (0, 0, 1)),
            whole((NROW, DIM)),
            pl.BlockSpec(memory_space=pl.ANY),
        ],
        out_specs=[
            whole((SAME, TOK)),
            whole((NROW, SENT - SAME, TOK)),
            whole((SLOTS, 16, 128)),
            whole((NCOL, 48, TOK)),
            whole((DIM, TOK)),
        ],
        scratch_shapes=[
            pltpu.VMEM((NCOL, 48, FF), BF),
            pltpu.VMEM((NCOL, 48, FF), BF),
            pltpu.VMEM((2 * NROW, NCOL, 48, 128), BF),
            pltpu.VMEM((TOK, FF), F32),
            pltpu.VMEM((TOK, DIM), F32),
            pltpu.VMEM((TOK + 8, 192), F32),
            pltpu.SemaphoreType.DMA((9,)),
        ],
        compiler_params=params("tokenwise"),
        cost_estimate=cost(15),
        name="tokenwise",
    )(row, att, x_t, arrived, wj, up_bias, everything)


def weight_grads_kernel(core_ref, *refs):
    got, out_ref = refs[:-1], refs[-1]

    def feats(at):
        return jnp.concatenate([ref[at : at + DIM, :] for ref in got], axis=1)

    def hidden(at, begin, end):
        return jnp.concatenate(
            [
                jnp.concatenate(
                    [ref[at + i * TOK : at + (i + 1) * TOK, :] for i in range(begin, end)], axis=1
                )
                for ref in got
            ],
            axis=0,
        )

    def keep(at, g):
        for i in range(g.shape[1] // 128):
            piece = g[:, i * 128 : (i + 1) * 128].astype(BF).reshape(NCOL, 48, 128)
            out_ref[:, at + 48 * i : at + 48 * (i + 1), :] = piece

    @pl.when(core_ref[0] == 0)
    def _():
        keep(0, dot(feats(0), hidden(3 * DIM + 48, 0, 6), 1, 0))
        keep(288, dot(feats(DIM), hidden(4 * DIM + 48, 0, 2), 1, 0))

    @pl.when(core_ref[0] != 0)
    def _():
        d_branch = feats(DIM)
        d_attn = feats(2 * DIM)
        keep(0, dot(d_branch, hidden(4 * DIM + 48, 2, 6), 1, 0))
        att = [heads_of(ref[A_AT:SENT, :].astype(F32)).astype(BF) for ref in got]
        att = jnp.concatenate(att, axis=0)
        att = jnp.concatenate([att, jnp.zeros((att.shape[0], 64), BF)], axis=1)
        keep(192, dot(d_attn, att, 1, 0))
        d_pre = hidden(3 * DIM + 48, 0, 6)
        ones = jnp.ones((16, d_pre.shape[0]), BF)
        sums = [dot(ones, d_branch, 1, 1)[0:1], dot(ones, d_attn, 1, 1)[0:1], dot(ones, d_pre, 1, 0)[0:1]]
        norm = got[0][3 * DIM : 3 * DIM + 48, :].astype(F32)
        for ref in got[1:]:
            norm = norm + ref[3 * DIM : 3 * DIM + 48, :].astype(F32)
        rows = [norm[0:24] + norm[24:48]]
        for v in sums:
            rows += [v[:, i * 128 : (i + 1) * 128] for i in range(6)]
        rows.append(jnp.zeros((6, 128), F32))
        rows = jnp.concatenate(rows, axis=0)
        hi = rows.astype(BF)
        lo = (rows - hi.astype(F32)).astype(BF)
        misc = jnp.concatenate([hi, lo], axis=0)
        out_ref[:, 288:384, :] = jnp.broadcast_to(misc[None], (NCOL, 96, 128))


def weight_grads(core, got, theirs):
    shape = (NCOL, WROWS // 2, 128)
    return pl.pallas_call(
        weight_grads_kernel,
        grid=(1,),
        out_shape=pltpu.HBM(shape, BF),
        in_specs=[SMEM] + [whole((SENT, TOK))] * 8,
        out_specs=whole(shape),
        compiler_params=params("weight_grads"),
        cost_estimate=cost(1),
        name="weight_grads",
    )(core, *got, *theirs)


def place(core, mine_ref, other_ref, blocks, half_rows):
    for at, block in blocks:
        low = at < half_rows
        local = at if low else at - half_rows
        rows = slice(local, local + block.shape[1])
        keep = core == (0 if low else 1)

        @pl.when(keep)
        def _():
            mine_ref[:, rows, :] = block

        @pl.when(jnp.logical_not(keep))
        def _():
            other_ref[:, rows, :] = block


def project_back_kernel(
    core_ref, first_ref, second_ref, w_ref, x_ref, din_ref, mine_ref, other_ref, layer_ref, scr
):
    core = core_ref[0]
    layer_ref[...] = jnp.concatenate([first_ref[c, 256:304, :] for c in range(NCOL)], axis=1)
    scr[...] = jnp.zeros_like(scr)
    for j in range(15):
        h, k = j // PER_HEAD, j % PER_HEAD
        for r in range(NROW):
            block = second_ref[j, 256 + 16 * r : 272 + 16 * r, :]
            unpack(block, scr, r * TOK + SHARE * k, HDIM * h, room(k))
    dq = scr[...].T.astype(BF)
    w = w_ref[...].reshape(DIM, JW)
    grad = jnp.zeros((DIM, JW), F32)
    total = jnp.zeros((16, JW), F32)
    ones = jnp.ones((16, TOK), BF)
    for r in range(NROW):
        source, at = (first_ref, r) if r < HALF else (second_ref, r - HALF)
        parts = [dq[:, r * TOK : (r + 1) * TOK]]
        for h in range(3):
            acc = source[PER_HEAD * h, at * TOK : (at + 1) * TOK, :].astype(F32)
            for k in range(1, PER_HEAD):
                acc = acc + source[PER_HEAD * h + k, at * TOK : (at + 1) * TOK, :].astype(F32)
            parts.append(acc.astype(BF))
        d_proj = jnp.concatenate(parts, axis=0)
        din_ref[r] = dot(w, d_proj, 1, 0).astype(BF)
        grad = grad + dot(x_ref[r], d_proj, 1, 1)
        total = total + dot(ones, d_proj, 1, 1)
    rows = [total[0:1, i * 128 : (i + 1) * 128] for i in range(5)] + [jnp.zeros((3, 128), F32)]
    rows = jnp.concatenate(rows, axis=0)
    hi = rows.astype(BF)
    lo = (rows - hi.astype(F32)).astype(BF)
    misc = jnp.broadcast_to(jnp.concatenate([hi, lo], axis=0)[None], (NCOL, 16, 128))
    low = grad.astype(BF)
    pieces = [low[:, i * 128 : (i + 1) * 128].reshape(NCOL, 48, 128) for i in range(5)]
    blocks = [(0, pieces[0]), (48, pieces[1]), (96, pieces[2][:, 0:32]), (128, pieces[2][:, 32:48])]
    blocks += [(144, pieces[3]), (192, pieces[4]), (240, misc)]
    place(core, mine_ref, other_ref, blocks, 128)


def project_back(core, first, second, wj, x4):
    kind = pltpu.HBM((NCOL, 128, 128), BF)
    return pl.pallas_call(
        project_back_kernel,
        out_shape=(
            pltpu.HBM((NROW, DIM, TOK), BF),
            kind,
            kind,
            pltpu.HBM((48, NCOL * TOK), BF),
        ),
        in_specs=[SMEM] + [VMEM] * 4,
        out_specs=[VMEM] * 4,
        scratch_shapes=[pltpu.VMEM((512, 256), F32)],
        compiler_params=params("project_back"),
        cost_estimate=cost(5),
        name="project_back",
    )(core, first, second, wj, x4)


def last_kernel(mine_ref, theirs_ref, din_ref, dh1_ref, out_ref):
    out_ref[:, 0:128, :] = (mine_ref[...].astype(F32) + theirs_ref[...].astype(F32)).astype(BF)
    total = dh1_ref[...]
    for r in range(NROW):
        total = total + din_ref[r].astype(F32)
    out_ref[:, 128:176, :] = total.astype(BF).reshape(NCOL, 48, TOK)


def last_payload(mine, theirs, din, dh1):
    return pl.pallas_call(
        last_kernel,
        out_shape=pltpu.HBM((NCOL, 176, 128), BF),
        in_specs=[VMEM] * 4,
        out_specs=VMEM,
        compiler_params=params("last_payload"),
        cost_estimate=cost(1),
        name="last_payload",
    )(mine, theirs, din, dh1)


def join(core_ref, mine, theirs):
    first = core_ref[0] == 0
    a, b = mine[...], theirs[...]
    return jnp.concatenate([jnp.where(first, a, b), jnp.where(first, b, a)], axis=0)


def finish_kernel(
    core_ref, col_ref, wide_ref, other_ref, out_ref, up_ref, up_bias_ref, down_ref, *own_refs
):
    wide = join(core_ref, wide_ref, other_ref)
    for i in range(6):
        lanes = slice(i * 128, (i + 1) * 128)
        up_ref[:, lanes] = wide[48 * i : 48 * (i + 1)]
        down_ref[:, lanes] = wide[288 + 48 * i : 288 + 48 * (i + 1)]
    out_ref[...] = jnp.concatenate([wide[576:624], wide[624:672, 0:64]], axis=1)
    vecs = wide[672:720] + wide[720:768]
    up_bias_ref[...] = vecs[36:42]
    rows = [
        jnp.concatenate([vecs[6 * v + i : 6 * v + i + 1] for i in range(6)], axis=1) for v in range(6)
    ]
    rows = jnp.concatenate(rows + [jnp.zeros((2, DIM), F32)], axis=0)
    feature = lax.broadcasted_iota(jnp.int32, (DIM, 48), 0)
    lane = lax.broadcasted_iota(jnp.int32, (DIM, 48), 1)
    pick = jnp.where(feature == col_ref[0] * 48 + lane, 1.0, 0.0).astype(BF)
    own = sum(dot(part, pick, 1, 0) for part in split3(rows))
    for v, ref in enumerate(own_refs):
        ref[...] = own[v : v + 1]


def finish(core, col, wide, other):
    shapes = [(48, 192), (48, DIM), (6, 128), (48, DIM)] + [(1, 48)] * 6
    return pl.pallas_call(
        finish_kernel,
        out_shape=[pltpu.HBM(shape, F32) for shape in shapes],
        in_specs=[SMEM] * 2 + [VMEM] * 2,
        out_specs=[VMEM] * len(shapes),
        compiler_params=params("finish"),
        cost_estimate=cost(1),
        name="finish",
    )(core, col, wide, other)


def joint_kernel(core_ref, last_ref, other_ref, joint_ref, joint_bias_ref):
    last = join(core_ref, last_ref, other_ref)
    chunks = [last[48 * i : 48 * (i + 1)] for i in range(5)]
    heads = [chunks[0][:, 0:64], chunks[0][:, 64:128], chunks[1][:, 0:64]]
    joint_ref[...] = jnp.concatenate([v for h in range(3) for v in (heads[h], chunks[2 + h])], axis=1)
    sums = last[240:248] + last[248:256]
    heads = [sums[0:1, 0:64], sums[0:1, 64:128], sums[1:2, 0:64]]
    joint_bias_ref[...] = jnp.concatenate(
        [jnp.concatenate([heads[h], sums[2 + h : 3 + h, 64:128]], axis=1) for h in range(3)], axis=0
    )


def joint_gradient(core, last, other):
    return pl.pallas_call(
        joint_kernel,
        out_shape=[pltpu.HBM(shape, F32) for shape in ((48, 576), (3, 128))],
        in_specs=[SMEM] + [VMEM] * 2,
        out_specs=[VMEM] * 2,
        compiler_params=params("joint_gradient"),
        cost_estimate=cost(1),
        name="joint_gradient",
    )(core, last, other)


def exchange(blocks, axis):
    return lax.all_to_all(blocks, axis, 0, 0, tiled=True)


def around(v, axis, shift):
    return lax.ppermute(v, axis, [(i, (i + shift) % 4) for i in range(4)])


def swap_cores(v):
    return lax.ppermute(v, "dp", [(0, 1), (1, 0)])


def per_device(
    inputs,
    segments,
    joint_weight,
    joint_bias,
    output_weight,
    output_bias,
    first_norm_gain,
    shift_first,
    up_weight,
    up_bias,
    down_weight,
    down_bias,
    second_norm_gain,
    second_norm_shift,
    cotangent,
):
    core = lax.axis_index("dp")
    col = lax.axis_index(COL)
    row = lax.axis_index("row")
    my_z, my_y = lax.axis_index("z"), lax.axis_index("y")
    core_word = core.reshape(1).astype(jnp.int32)
    row_word = row.reshape(1).astype(jnp.int32)

    def by_col(a):
        return jnp.transpose(a.reshape(48, NCOL, TOK), (1, 0, 2))

    blocks = by_col(inputs)
    blocks, up_weight, down_weight, output_weight = lax.optimization_barrier(
        (blocks, up_weight, down_weight, output_weight)
    )
    x_t = exchange(blocks, COL)
    vectors = jnp.stack(
        [output_bias, first_norm_gain, shift_first, down_bias, second_norm_gain, second_norm_shift], axis=1
    )
    vectors = jnp.pad(jnp.concatenate(split3(vectors), axis=1), ((0, 0), (0, 46)))
    jw = joint_weight.reshape(48, 3, 3, HDIM)
    jw = jnp.concatenate([jw[:, :, 0].reshape(48, 192), vectors, jw[:, :, 1:].reshape(48, 384)], axis=1)
    jw = jnp.broadcast_to(jw[None], (NCOL, 48, JW))
    x_t, jw = lax.optimization_barrier((x_t, jw))
    wj = exchange(jw, COL)
    x4 = lax.all_gather(x_t.reshape(DIM, TOK), "row", axis=0, tiled=False)

    turned = lax.dynamic_slice_in_dim(output_weight, core * 96, 96, 0).T
    my_bias = lax.dynamic_slice_in_dim(up_bias, (core * NCOL + col) * 24, 24, 0)
    my_bias = jnp.pad(jnp.stack(split3(my_bias)), ((0, 45), (0, 8)))
    turned = jnp.concatenate([turned, my_bias], axis=1).reshape(3, 16, 128)
    turned = jnp.transpose(turned, (1, 0, 2)).reshape(16, 384)
    shard = jnp.concatenate(
        [
            lax.dynamic_slice_in_dim(up_weight, core * 384, 384, 1),
            lax.dynamic_slice_in_dim(down_weight, core * 384, 384, 1),
            turned,
        ],
        axis=0,
    )
    shard = lax.optimization_barrier((shard, x_t))[0]
    everything = lax.all_gather(shard, ("dp", "row", "z", "y"), axis=0, tiled=False)
    everything = everything.reshape(2, NROW, NCOL, 112, 384)
    up_b = jnp.sum(everything[:, :, :, 96:99, 96:120].astype(F32), axis=3)
    up_b = jnp.transpose(up_b, (1, 0, 2, 3)).reshape(NROW, DIM)

    bias3 = joint_bias.reshape(3, 2, HDIM)
    bias = jnp.concatenate(
        [
            bias3[:, 0].reshape(192),
            jnp.zeros((64,), F32),
            jnp.concatenate([jnp.zeros((3, HDIM), F32), bias3[:, 1]], axis=1).reshape(384),
        ]
    ).reshape(1, JW)
    seg = segments.reshape(SLOTS, TOK)
    shift = lax.rem(TOK - lax.rem(col, PER_HEAD) * SHARE, TOK).reshape(1).astype(jnp.int32)

    arrived = exchange(project(x4, wj, bias, by_col(cotangent)), COL)
    qa, o, o_blocks = attend(shift, arrived, seg)

    att = exchange(o_blocks, ALL)
    same, sent, d_blocks, fin, dh1 = tokenwise(row_word, att, x_t, arrived, wj, up_b, everything)

    d_blocks, same, sent = lax.optimization_barrier((d_blocks, same, sent))
    pieces = [jnp.concatenate([same, sent[d]], axis=0) for d in range(NROW)]
    grad_o = exchange(d_blocks, ALL)
    got = [around(pieces[d], "row", d) for d in range(1, NROW)]
    grad_o, own_piece = lax.optimization_barrier((grad_o, pieces[0]))
    back_a, doa, turned_qd, acc = attend_back_first(arrived, grad_o, qa, o, fin, seg)
    back_b = attend_back_second(qa, doa, turned_qd, acc, arrived, seg)
    back_a = exchange(back_a, COL)
    back_b, got, own_piece, back_a = lax.optimization_barrier((back_b, got, own_piece, back_a))
    got = [own_piece, *got]
    theirs = [swap_cores(v) for v in got]
    wide = weight_grads(core_word, got, theirs).reshape(4, 4, WROWS // 2, 128)
    back_b, back_a = lax.optimization_barrier((back_b, back_a))
    back_b = exchange(back_b, COL)
    near = [lax.dynamic_index_in_dim(wide, lax.rem(my_z + d, 4), 0, keepdims=False) for d in range(4)]
    near = [near[0]] + [around(near[d], "z", d) for d in range(1, 4)]
    wide = near[0].astype(F32) + near[1].astype(F32) + near[2].astype(F32) + near[3].astype(F32)
    wide = wide.astype(BF)

    din, mine_j, other_j, layer_output = project_back(core_word, back_a, back_b, wj, x4)
    theirs_j = swap_cores(other_j)
    din = exchange(din, "row")
    near = [lax.dynamic_index_in_dim(wide, lax.rem(my_y + d, 4), 0, keepdims=False) for d in range(4)]
    din, near = lax.optimization_barrier((din, near))
    near = [near[0]] + [around(near[d], "y", d) for d in range(1, 4)]
    mixed = exchange(last_payload(mine_j, theirs_j, din, dh1), COL)
    wide = near[0].astype(F32) + near[1].astype(F32) + near[2].astype(F32) + near[3].astype(F32)
    grad_out, grad_up, grad_up_bias, grad_down, *own = finish(
        core_word, col.reshape(1).astype(jnp.int32), wide, swap_cores(wide)
    )
    last = jnp.sum(mixed[:, :128].astype(F32), axis=0)
    grad_inputs = jnp.transpose(mixed[:, 128:].astype(F32), (1, 0, 2)).reshape(48, 2048)
    grad_joint, grad_joint_bias = joint_gradient(core_word, last, swap_cores(last))
    own = [v.reshape(48) for v in own]

    return (
        layer_output,
        grad_inputs,
        grad_joint,
        grad_joint_bias.reshape(384),
        grad_out.T,
        own[5],
        own[0],
        own[1],
        grad_up,
        grad_up_bias.reshape(768),
        grad_down,
        own[4],
        own[2],
        own[3],
    )


def solution(mesh):
    sizes = (mesh.shape["dp"], mesh.shape["row"], 4, 4)
    fine = jax.sharding.Mesh(mesh.devices.reshape(sizes), ("dp", "row", "z", "y"))
    grid = P(COL, ("dp", "row"))
    block = P(COL, "row")
    return jax.shard_map(
        per_device,
        mesh=fine,
        in_specs=(
            grid, P("dp", None), block, P("row"), P("row", COL), P(COL), P(COL), P(COL),
            block, P("row"), block, P(COL), P(COL), P(COL), grid,
        ),
        out_specs=(
            grid, grid, block, P("row"), P("row", COL), P(COL), P(COL), P(COL),
            block, P("row"), block, P(COL), P(COL), P(COL),
        ),
        check_vma=False,
    )
```

```python
import math

import jax
import jax.numpy as jnp
from jax import lax
from jax.experimental import pallas as pl
from jax.experimental.pallas import tpu as pltpu
from jax.sharding import PartitionSpec as P

HDIM = 64
EPS = 1e-06
BLOCK_OUT = -1e30
LOG2E = 1.4426950408889634
BF = jnp.bfloat16
F32 = jnp.float32

DIM = 768
FF = 3072
NCOL = 16
NROW = 4
TOK = 128
PER_HEAD = 5
SHARE = 26
SLOTS = NROW * NCOL
ROWS = SLOTS * SHARE
AUG = 144
JW = 640
HALF = 2
FWD_C = 2
BWD_C = 2
Q_AT = NROW * TOK
C_AT = Q_AT + 64
BLOCK = C_AT + 48
MIB = 2**20
COL = ("z", "y")
ALL = ("row", "z", "y")
VMEM = pl.BlockSpec(memory_space=pltpu.VMEM)
SMEM = pl.BlockSpec(memory_space=pltpu.SMEM)
A_AT = 5 * DIM + 48
SENT = A_AT + 192
SAME = 3 * DIM + 48
WROWS = 768


def split3(v):
    hi = v.astype(BF)
    rest = v - hi.astype(F32)
    mid = rest.astype(BF)
    low = (rest - mid.astype(F32)).astype(BF)
    return hi, mid, low


def dot(a, b, ca, cb):
    return lax.dot_general(a, b, (((ca,), (cb,)), ((), ())), preferred_element_type=F32)


LIMITS = {
    "project": 16,
    "attend": 32,
    "attend_back_first": 63.9,
    "attend_back_second": 63.9,
    "tokenwise": 63.9,
    "weight_grads": 63.9,
    "project_back": 63.9,
    "last_payload": 12,
    "finish": 12,
    "joint_gradient": 8,
}


def params(name):
    return pltpu.CompilerParams(vmem_limit_bytes=int(LIMITS[name] * MIB))


def cost(us):
    return pl.CostEstimate(flops=int(us * 1e9), bytes_accessed=int(us * 2e6), transcendentals=0)


Q_BLOCK = pl.BlockSpec((NCOL, 64, 128), lambda i: (0, Q_AT // 64, 0))


def whole(shape):
    return pl.BlockSpec(shape, lambda i: (0,) * len(shape))


def pack(ref, at, lane, scale=None):
    lanes = slice(lane, lane + HDIM)
    rest = jnp.concatenate([ref[at + 16 : at + SHARE, lanes], jnp.zeros((6, HDIM), F32)], axis=0)
    both = jnp.concatenate([ref[at : at + 16, lanes], rest], axis=1)
    return (both if scale is None else both * scale).astype(BF)


def unpack(block, ref, at, lane, rows=SHARE):
    block = block.astype(F32)
    lanes = slice(lane, lane + HDIM)
    ref[at : at + 16, lanes] = block[:, 0:64]
    ref[at + 16 : at + rows, lanes] = block[0 : rows - 16, 64:128]


def project_kernel(x_ref, w_ref, b_ref, cot_ref, out_ref, q_ref):
    w = w_ref[...].reshape(DIM, JW)
    q_ref[...] = jnp.zeros_like(q_ref)
    for r in range(NROW):
        tokens = x_ref[r].astype(F32).T.astype(BF)
        y = dot(tokens, w, 1, 0) + b_ref[...]
        q_ref[r * TOK : (r + 1) * TOK, :] = y[:, 0:256]
        for h in range(3):
            kv = y[:, 256 + 128 * h : 384 + 128 * h].T.astype(BF)
            for j in range(PER_HEAD * h, PER_HEAD * (h + 1) + (1 if h == 2 else 0)):
                out_ref[j, r * TOK : (r + 1) * TOK, :] = kv
    for j in range(NCOL):
        h, k = min(j, 14) // PER_HEAD, min(j, 14) % PER_HEAD
        for r in range(NROW):
            at = r * TOK + SHARE * k
            out_ref[j, Q_AT + 16 * r : Q_AT + 16 * (r + 1), :] = pack(q_ref, at, HDIM * h)
    out_ref[:, C_AT:BLOCK, :] = cot_ref[...]


def project(x4, wj, bias, cot):
    return pl.pallas_call(
        project_kernel,
        out_shape=pltpu.HBM((NCOL, BLOCK, 128), BF),
        in_specs=[VMEM] * 4,
        out_specs=VMEM,
        scratch_shapes=[pltpu.VMEM((640, 256), F32)],
        compiler_params=params("project"),
        cost_estimate=cost(3),
        name="project",
    )(x4, wj, bias, cot)


def key_rows(seg_row):
    row = lax.broadcasted_iota(jnp.int32, (16, seg_row.shape[1]), 0)
    hot = jnp.where(row < 5, jnp.where(row == seg_row, 1.0, 0.0), jnp.where(row < 8, 1.0, 0.0))
    return hot.astype(BF)


def offset_columns(value, base):
    h, m, l = split3(-value)
    lane = lax.broadcasted_iota(jnp.int32, base.shape, 1)
    return jnp.where(
        lane == 5,
        h.astype(F32),
        jnp.where(lane == 6, m.astype(F32), jnp.where(lane == 7, l.astype(F32), base)),
    )


def key_block(kv_ref, seg_ref, begin):
    pairs = [(c, r) for c in range(kv_ref.shape[0]) for r in range(kv_ref.shape[1] // TOK)]
    tiles = [kv_ref[c, r * TOK : (r + 1) * TOK, :] for c, r in pairs]
    at = pl.program_id(0) * kv_ref.shape[0]
    extra = [key_rows(seg_ref[pl.ds((begin + r) * NCOL + at + c, 1), :]) for c, r in pairs]
    return jnp.concatenate(tiles, axis=1), jnp.concatenate(extra, axis=1)


def forward_step(qa_ref, kv_ref, seg_ref, acc_ref, top_ref):
    kvt, extra = key_block(kv_ref, seg_ref, 0)
    kt = jnp.concatenate([kvt[0:64], kvt[0:64], extra], axis=0)
    turned = kvt.astype(F32).T
    lane = lax.broadcasted_iota(jnp.int32, turned.shape, 1)
    va = jnp.where(lane >= 64, turned, jnp.where(lane == 0, 1.0, 0.0)).astype(BF)
    s = dot(qa_ref[...], kt, 1, 0)
    parts = [s[:, i * 128 : (i + 1) * 128] for i in range(s.shape[1] // 128)]
    high = parts[0]
    for part in parts[1:]:
        high = jnp.maximum(high, part)
    top = top_ref[...]
    raised = jnp.maximum(top, jnp.broadcast_to(jnp.max(high, axis=1, keepdims=True), top.shape))
    p = jnp.concatenate([jnp.exp2(part - raised).astype(BF) for part in parts], axis=1)
    fade = jnp.exp2(top - raised)
    top_ref[...] = raised
    acc_ref[...] = acc_ref[...] * fade + dot(p, va, 1, 0)


def attend_kernel(
    shift_ref, q_ref, kv_ref, seg_ref, qa_ref, o_ref, out_ref, q_scr, pen_scr, acc_ref, top_ref
):
    @pl.when(pl.program_id(0) == 0)
    def _():
        columns = pltpu.roll(seg_ref[...].astype(F32), shift_ref[0], 1).T
        lane = lax.broadcasted_iota(jnp.int32, (SHARE, 16), 1)
        seg = lane.astype(F32)
        for r in range(NROW):
            for c in range(NCOL):
                slot = r * NCOL + c
                unpack(q_ref[c, 16 * r : 16 * (r + 1), :], q_scr, SHARE * slot, 0)
                pen_scr[SHARE * slot : SHARE * (slot + 1), :] = jnp.where(
                    (lane < 5) & (seg != columns[0:SHARE, slot : slot + 1]), BLOCK_OUT, 0.0
                )
        scaled = q_scr[...] * (LOG2E / 8.0)
        hi = scaled.astype(BF)
        lo = (scaled - hi.astype(F32)).astype(BF)
        pen = pen_scr[...]
        qa_ref[...] = jnp.concatenate([hi, lo, pen.astype(BF)], axis=1)
        acc_ref[...] = jnp.zeros_like(acc_ref)
        top_ref[...] = jnp.full_like(top_ref, -3e38)

    forward_step(qa_ref, kv_ref, seg_ref, acc_ref, top_ref)

    @pl.when(pl.program_id(0) == pl.num_programs(0) - 1)
    def _():
        acc = acc_ref[...]
        total = acc[:, 0:1]
        o_ref[...] = acc[:, 64:128] / total
        lse = top_ref[:, 0:1] + jnp.log(total) * LOG2E
        qa_ref[:, 128:144] = offset_columns(lse, qa_ref[:, 128:144].astype(F32)).astype(BF)
        for slot in range(SLOTS):
            out_ref[slot] = pack(o_ref, SHARE * slot, 0)


def attend(shift, arrived, seg):
    return pl.pallas_call(
        attend_kernel,
        grid=(NCOL // FWD_C,),
        out_shape=(
            pltpu.HBM((ROWS, AUG), BF),
            pltpu.HBM((ROWS, HDIM), F32),
            pltpu.HBM((SLOTS, 16, 128), BF),
        ),
        in_specs=[
            SMEM,
            Q_BLOCK,
            pl.BlockSpec((FWD_C, Q_AT, 128), lambda i: (i, 0, 0)),
            whole((SLOTS, TOK)),
        ],
        out_specs=[whole((ROWS, AUG)), whole((ROWS, HDIM)), whole((SLOTS, 16, 128))],
        scratch_shapes=[
            pltpu.VMEM((ROWS, HDIM), F32),
            pltpu.VMEM((ROWS, 16), F32),
            pltpu.VMEM((ROWS, 128), F32),
            pltpu.VMEM((ROWS, 128), F32),
        ],
        compiler_params=params("attend"),
        cost_estimate=cost(20),
        name="attend",
    )(shift, arrived, arrived, seg)


def backward_step(qa_ref, doa_ref, turned_ref, kv_ref, seg_ref, begin, acc_ref):
    kvt, extra = key_block(kv_ref, seg_ref, begin)
    kt = jnp.concatenate([kvt[0:64], kvt[0:64], extra], axis=0)
    vt = jnp.concatenate([kvt[64:128], extra], axis=0)
    keys = kvt.astype(F32).T.astype(BF)
    p = jnp.exp2(dot(qa_ref[...], kt, 1, 0))
    dp = dot(doa_ref[...], vt, 1, 0)
    ds = (p * dp).astype(BF)
    acc_ref[...] += dot(ds, keys, 1, 0)
    dk = dot(turned_ref[0:64, :], ds, 1, 0) * 0.125
    dv = dot(turned_ref[64:128, :], p.astype(BF), 1, 0)
    return jnp.concatenate([dk, dv], axis=0).astype(BF)


def store_keys(out_ref, at, both):
    for c in range(BWD_C):
        for r in range(HALF):
            i = c * HALF + r
            out_ref[at + c, r * TOK : (r + 1) * TOK, :] = both[:, i * TOK : (i + 1) * TOK]


def back_first_kernel(
    q_ref, do_ref, qa_ref, o_ref, fin_ref, kv_ref, seg_ref, out_ref, doa_ref, turned_ref, acc_ref, pair_scr
):
    @pl.when(pl.program_id(0) == 0)
    def _():
        for r in range(NROW):
            for c in range(NCOL):
                slot = r * NCOL + c
                unpack(q_ref[c, 16 * r : 16 * (r + 1), :], pair_scr, SHARE * slot, 0)
                unpack(do_ref[slot], pair_scr, SHARE * slot, HDIM)
        pairs = pair_scr[...]
        turned_ref[...] = pairs.T.astype(BF)
        grad = pairs[:, 64:128]
        delta = jnp.sum(grad * o_ref[...], axis=1, keepdims=True)
        ext = offset_columns(delta, jnp.zeros((ROWS, 16), F32))
        doa_ref[...] = jnp.concatenate([grad.astype(BF), ext.astype(BF)], axis=1)
        acc_ref[...] = jnp.zeros_like(acc_ref)

    both = backward_step(qa_ref, doa_ref, turned_ref, kv_ref, seg_ref, 0, acc_ref)
    store_keys(out_ref, 0, both)
    out_ref[:, 256:304, :] = fin_ref[...]


def back_second_kernel(
    qa_ref, doa_ref, turned_ref, acc_in, kv_ref, seg_ref, out_ref, acc_ref
):
    step = pl.program_id(0)

    @pl.when(step == 0)
    def _():
        acc_ref[...] = acc_in[...]

    both = backward_step(qa_ref, doa_ref, turned_ref, kv_ref, seg_ref, HALF, acc_ref)
    store_keys(out_ref, step * BWD_C, both)

    @pl.when(step == pl.num_programs(0) - 1)
    def _():
        for r in range(NROW):
            for c in range(NCOL):
                block = pack(acc_ref, SHARE * (r * NCOL + c), 0, 0.125)
                out_ref[c, 256 + 16 * r : 272 + 16 * r, :] = block


SEG_BACK = whole((SLOTS, TOK))
BACK_STEPS = NCOL // BWD_C


def attend_back_first(arrived, grad, qa, o, fin, seg):
    return pl.pallas_call(
        back_first_kernel,
        grid=(BACK_STEPS,),
        out_shape=(
            pltpu.HBM((NCOL, 304, 128), BF),
            pltpu.HBM((ROWS, 80), BF),
            pltpu.HBM((128, ROWS), BF),
            pltpu.HBM((ROWS, 128), F32),
        ),
        in_specs=[
            Q_BLOCK,
            whole((SLOTS, 16, 128)),
            whole((ROWS, AUG)),
            whole((ROWS, HDIM)),
            pl.BlockSpec((BWD_C, 48, 128), lambda i: (i, 0, 0)),
            pl.BlockSpec((BWD_C, HALF * TOK, 128), lambda i: (i, 0, 0)),
            SEG_BACK,
        ],
        out_specs=[
            pl.BlockSpec((BWD_C, 304, 128), lambda i: (i, 0, 0)),
            whole((ROWS, 80)),
            whole((128, ROWS)),
            whole((ROWS, 128)),
        ],
        scratch_shapes=[pltpu.VMEM((ROWS, 128), F32)],
        compiler_params=params("attend_back_first"),
        cost_estimate=cost(18),
        name="attend_back_first",
    )(arrived, grad, qa, o, fin, arrived, seg)


def attend_back_second(qa, doa, turned, acc, arrived, seg):
    return pl.pallas_call(
        back_second_kernel,
        grid=(BACK_STEPS,),
        out_shape=pltpu.HBM((NCOL, 320, 128), BF),
        in_specs=[
            whole((ROWS, AUG)),
            whole((ROWS, 80)),
            whole((128, ROWS)),
            whole((ROWS, 128)),
            pl.BlockSpec((BWD_C, HALF * TOK, 128), lambda i: (i, 1, 0)),
            SEG_BACK,
        ],
        out_specs=whole((NCOL, 320, 128)),
        scratch_shapes=[pltpu.VMEM((ROWS, 128), F32)],
        compiler_params=params("attend_back_second"),
        cost_estimate=cost(18),
        name="attend_back_second",
    )(qa, doa, turned, acc, arrived, seg)


def heads_of(block):
    return jnp.concatenate(
        [
            jnp.concatenate([block[64 * h : 64 * (h + 1), 64 * k : 64 * (k + 1)] for h in range(3)], axis=1)
            for k in range(2)
        ],
        axis=0,
    )


def room(k):
    return min(SHARE, TOK - SHARE * k)


def feature_mean(v):
    return jnp.sum(v, axis=1, keepdims=True) * (1.0 / DIM)


def tokenwise_kernel(
    row_ref, att_ref, x_ref, cot_ref, vec_ref, upb_ref, all_ref,
    same_ref, sent_ref, datt_ref, fin_ref, dh1_ref,
    up_ref, down_ref, out_ref, slope_ref, att_scr, back_scr, sems,
):
    row = row_ref[0]
    copies = []
    for g in range(3):
        for k in range(2):
            for r in range(NROW):
                copies.append(
                    pltpu.make_async_copy(
                        all_ref.at[k, r, :, 96:112, g * 128 : (g + 1) * 128],
                        out_ref.at[k * NROW + r, :, 16 * g : 16 * (g + 1), :],
                        sems.at[0],
                    )
                )
    n_out = len(copies)
    for r in range(NROW):
        for k in range(2):
            lanes = slice(r * DIM + k * 384, r * DIM + (k + 1) * 384)
            copies.append(
                pltpu.make_async_copy(all_ref.at[k, r, :, 0:48, :], up_ref.at[:, :, lanes], sems.at[1 + r])
            )
    for r in range(NROW):
        for k in range(2):
            lanes = slice(r * DIM + k * 384, r * DIM + (k + 1) * 384)
            copies.append(
                pltpu.make_async_copy(all_ref.at[k, r, :, 48:96, :], down_ref.at[:, :, lanes], sems.at[5 + r])
            )
    for copy in copies:
        copy.start()

    def wait(group):
        chosen = copies[:n_out] if group == 0 else copies[n_out + 2 * (group - 1) : n_out + 2 * group]
        for copy in chosen:
            copy.wait()

    tok = x_ref[...].reshape(DIM, TOK).astype(F32).T
    cot = cot_ref[...].reshape(DIM, TOK).astype(F32).T
    vecs = vec_ref[...].reshape(DIM, TOK).astype(F32).T[64:128]
    out_b, gain_1, shift_1, down_b, gain_2, shift_2 = [
        vecs[i : i + 1] + vecs[6 + i : 7 + i] + vecs[12 + i : 13 + i] for i in range(6)
    ]
    gap = jnp.zeros((TOK, 32), BF)

    for r in range(NROW):
        for j in range(15):
            h, k = j // PER_HEAD, j % PER_HEAD
            unpack(att_ref[r * NCOL + j], att_scr, SHARE * k, 192 * r + HDIM * h, room(k))
    for r in range(NROW):
        target = lax.rem(r + NROW - row, NROW)
        for h in range(3):
            lanes = slice(192 * r + HDIM * h, 192 * r + HDIM * (h + 1))
            both = jnp.concatenate([att_scr[0:64, lanes], att_scr[64:128, lanes]], axis=1)
            at = A_AT - SAME + 64 * h
            sent_ref[target, at : at + 64, :] = both.astype(BF)
    wait(0)
    attn = jnp.zeros((TOK, DIM), F32)
    for r in range(NROW):
        for k in range(2):
            lanes = slice(192 * r + 96 * k, 192 * r + 96 * (k + 1))
            piece = jnp.concatenate([att_scr[:, lanes].astype(BF), gap], axis=1)
            attn = attn + dot(piece, out_ref[k * NROW + r].reshape(DIM, 128), 1, 1)
    h1 = tok + (attn + out_b)
    off = h1 - feature_mean(h1)
    inv1 = lax.rsqrt(feature_mean(off * off) + EPS)
    xhat1 = off * inv1
    n1 = xhat1 * gain_1 + shift_1
    n1_low = n1.astype(BF)

    branch = jnp.zeros((TOK, DIM), F32)
    for r in range(NROW):
        wait(1 + r)
        cols = slice(r * DIM, (r + 1) * DIM)
        pre = dot(n1_low, up_ref[:, :, cols].reshape(DIM, DIM), 1, 0) + upb_ref[r : r + 1, :]
        phi = 0.5 * (1.0 + lax.erf(pre * (1.0 / math.sqrt(2.0))))
        act = (pre * phi).astype(BF)
        slope_ref[:, cols] = phi + pre * jnp.exp(-0.5 * pre * pre) * (1.0 / math.sqrt(2.0 * math.pi))
        for i in range(6):
            at = DIM + i * TOK
            sent_ref[lax.rem(r + NROW - row, NROW), at : at + TOK, :] = act[:, i * TOK : (i + 1) * TOK]
        wait(5 + r)
        branch = branch + dot(act, down_ref[:, :, cols].reshape(DIM, DIM), 1, 1)
    h2 = n1 + (branch + down_b)
    off = h2 - feature_mean(h2)
    inv2 = lax.rsqrt(feature_mean(off * off) + EPS)
    xhat2 = off * inv2
    fin_ref[...] = (xhat2 * gain_2 + shift_2).T.astype(BF).reshape(NCOL, 48, TOK)
    dx = cot * gain_2
    dh2 = inv2 * (dx - feature_mean(dx) - xhat2 * feature_mean(dx * xhat2))
    d_branch = dh2.astype(BF)

    back = jnp.zeros((TOK, DIM), F32)
    for r in range(NROW):
        cols = slice(r * DIM, (r + 1) * DIM)
        d_act = dot(d_branch, down_ref[:, :, cols].reshape(DIM, DIM), 1, 0)
        d_pre = (d_act * slope_ref[:, cols]).astype(BF)
        for i in range(6):
            at = i * TOK
            sent_ref[lax.rem(r + NROW - row, NROW), at : at + TOK, :] = d_pre[:, i * TOK : (i + 1) * TOK]
        back = back + dot(d_pre, up_ref[:, :, cols].reshape(DIM, DIM), 1, 1)
    up1 = dh2 + back
    dx = up1 * gain_1
    dh1 = inv1 * (dx - feature_mean(dx) - xhat1 * feature_mean(dx * xhat1))
    d_attn = dh1.astype(BF)
    back_scr[TOK : TOK + 8, :] = jnp.zeros((8, 192), F32)
    for r in range(NROW):
        pieces = [dot(d_attn, out_ref[k * NROW + r].reshape(DIM, 128), 1, 0)[:, 0:96] for k in range(2)]
        back_scr[0:TOK, :] = jnp.concatenate(pieces, axis=1)
        for j in range(15):
            h, k = j // PER_HEAD, j % PER_HEAD
            datt_ref[r * NCOL + j] = pack(back_scr, SHARE * k, HDIM * h)
        datt_ref[r * NCOL + 15] = jnp.zeros((16, 128), BF)
    turned = dh1.T
    dh1_ref[...] = turned
    shared = [n1.T.astype(BF), dh2.T.astype(BF), turned.astype(BF)]
    sums = [
        jnp.sum(v, axis=0, keepdims=True) for v in (up1 * xhat1, up1, cot * xhat2, cot)
    ]
    rows = []
    for part in range(2):
        for v in sums:
            hi = v.astype(BF).astype(F32)
            piece = hi if part == 0 else v - hi
            rows += [piece[:, i * 128 : (i + 1) * 128] for i in range(6)]
    shared.append(jnp.concatenate(rows, axis=0).astype(BF))
    at = 0
    for v in shared:
        same_ref[at : at + v.shape[0], :] = v
        at += v.shape[0]


def tokenwise(row, att, x_t, arrived, wj, up_bias, everything):
    return pl.pallas_call(
        tokenwise_kernel,
        out_shape=(
            pltpu.HBM((SAME, TOK), BF),
            pltpu.HBM((NROW, SENT - SAME, TOK), BF),
            pltpu.HBM((SLOTS, 16, 128), BF),
            pltpu.HBM((NCOL, 48, TOK), BF),
            pltpu.HBM((DIM, TOK), F32),
        ),
        grid=(1,),
        in_specs=[
            SMEM,
            whole((SLOTS, 16, 128)),
            whole((NCOL, 48, TOK)),
            pl.BlockSpec((NCOL, 48, TOK), lambda i: (0, C_AT // 48, 0)),
            pl.BlockSpec((NCOL, 48, TOK), lambda i: (0, 0, 1)),
            whole((NROW, DIM)),
            pl.BlockSpec(memory_space=pl.ANY),
        ],
        out_specs=[
            whole((SAME, TOK)),
            whole((NROW, SENT - SAME, TOK)),
            whole((SLOTS, 16, 128)),
            whole((NCOL, 48, TOK)),
            whole((DIM, TOK)),
        ],
        scratch_shapes=[
            pltpu.VMEM((NCOL, 48, FF), BF),
            pltpu.VMEM((NCOL, 48, FF), BF),
            pltpu.VMEM((2 * NROW, NCOL, 48, 128), BF),
            pltpu.VMEM((TOK, FF), F32),
            pltpu.VMEM((TOK, DIM), F32),
            pltpu.VMEM((TOK + 8, 192), F32),
            pltpu.SemaphoreType.DMA((9,)),
        ],
        compiler_params=params("tokenwise"),
        cost_estimate=cost(15),
        name="tokenwise",
    )(row, att, x_t, arrived, wj, up_bias, everything)


def weight_grads_kernel(core_ref, *refs):
    got, out_ref = refs[:-1], refs[-1]

    def feats(at):
        return jnp.concatenate([ref[at : at + DIM, :] for ref in got], axis=1)

    def hidden(at, begin, end):
        return jnp.concatenate(
            [
                jnp.concatenate(
                    [ref[at + i * TOK : at + (i + 1) * TOK, :] for i in range(begin, end)], axis=1
                )
                for ref in got
            ],
            axis=0,
        )

    def keep(at, g):
        for i in range(g.shape[1] // 128):
            piece = g[:, i * 128 : (i + 1) * 128].astype(BF).reshape(NCOL, 48, 128)
            out_ref[:, at + 48 * i : at + 48 * (i + 1), :] = piece

    @pl.when(core_ref[0] == 0)
    def _():
        keep(0, dot(feats(0), hidden(3 * DIM + 48, 0, 6), 1, 0))
        keep(288, dot(feats(DIM), hidden(4 * DIM + 48, 0, 2), 1, 0))

    @pl.when(core_ref[0] != 0)
    def _():
        d_branch = feats(DIM)
        d_attn = feats(2 * DIM)
        keep(0, dot(d_branch, hidden(4 * DIM + 48, 2, 6), 1, 0))
        att = [heads_of(ref[A_AT:SENT, :].astype(F32)).astype(BF) for ref in got]
        att = jnp.concatenate(att, axis=0)
        att = jnp.concatenate([att, jnp.zeros((att.shape[0], 64), BF)], axis=1)
        keep(192, dot(d_attn, att, 1, 0))
        d_pre = hidden(3 * DIM + 48, 0, 6)
        ones = jnp.ones((16, d_pre.shape[0]), BF)
        sums = [dot(ones, d_branch, 1, 1)[0:1], dot(ones, d_attn, 1, 1)[0:1], dot(ones, d_pre, 1, 0)[0:1]]
        norm = got[0][3 * DIM : 3 * DIM + 48, :].astype(F32)
        for ref in got[1:]:
            norm = norm + ref[3 * DIM : 3 * DIM + 48, :].astype(F32)
        rows = [norm[0:24] + norm[24:48]]
        for v in sums:
            rows += [v[:, i * 128 : (i + 1) * 128] for i in range(6)]
        rows.append(jnp.zeros((6, 128), F32))
        rows = jnp.concatenate(rows, axis=0)
        hi = rows.astype(BF)
        lo = (rows - hi.astype(F32)).astype(BF)
        misc = jnp.concatenate([hi, lo], axis=0)
        out_ref[:, 288:384, :] = jnp.broadcast_to(misc[None], (NCOL, 96, 128))


def weight_grads(core, got, theirs):
    shape = (NCOL, WROWS // 2, 128)
    return pl.pallas_call(
        weight_grads_kernel,
        grid=(1,),
        out_shape=pltpu.HBM(shape, BF),
        in_specs=[SMEM] + [whole((SENT, TOK))] * 8,
        out_specs=whole(shape),
        compiler_params=params("weight_grads"),
        cost_estimate=cost(1),
        name="weight_grads",
    )(core, *got, *theirs)


def place(core, mine_ref, other_ref, blocks, half_rows):
    for at, block in blocks:
        low = at < half_rows
        local = at if low else at - half_rows
        rows = slice(local, local + block.shape[1])
        keep = core == (0 if low else 1)

        @pl.when(keep)
        def _():
            mine_ref[:, rows, :] = block

        @pl.when(jnp.logical_not(keep))
        def _():
            other_ref[:, rows, :] = block


def project_back_kernel(
    core_ref, first_ref, second_ref, w_ref, x_ref, din_ref, mine_ref, other_ref, layer_ref, scr
):
    core = core_ref[0]
    layer_ref[...] = jnp.concatenate([first_ref[c, 256:304, :] for c in range(NCOL)], axis=1)
    scr[...] = jnp.zeros_like(scr)
    for j in range(15):
        h, k = j // PER_HEAD, j % PER_HEAD
        for r in range(NROW):
            block = second_ref[j, 256 + 16 * r : 272 + 16 * r, :]
            unpack(block, scr, r * TOK + SHARE * k, HDIM * h, room(k))
    dq = scr[...].T.astype(BF)
    w = w_ref[...].reshape(DIM, JW)
    grad = jnp.zeros((DIM, JW), F32)
    total = jnp.zeros((16, JW), F32)
    ones = jnp.ones((16, TOK), BF)
    for r in range(NROW):
        source, at = (first_ref, r) if r < HALF else (second_ref, r - HALF)
        parts = [dq[:, r * TOK : (r + 1) * TOK]]
        for h in range(3):
            acc = source[PER_HEAD * h, at * TOK : (at + 1) * TOK, :].astype(F32)
            for k in range(1, PER_HEAD):
                acc = acc + source[PER_HEAD * h + k, at * TOK : (at + 1) * TOK, :].astype(F32)
            parts.append(acc.astype(BF))
        d_proj = jnp.concatenate(parts, axis=0)
        din_ref[r] = dot(w, d_proj, 1, 0).astype(BF)
        grad = grad + dot(x_ref[r], d_proj, 1, 1)
        total = total + dot(ones, d_proj, 1, 1)
    rows = [total[0:1, i * 128 : (i + 1) * 128] for i in range(5)] + [jnp.zeros((3, 128), F32)]
    rows = jnp.concatenate(rows, axis=0)
    hi = rows.astype(BF)
    lo = (rows - hi.astype(F32)).astype(BF)
    misc = jnp.broadcast_to(jnp.concatenate([hi, lo], axis=0)[None], (NCOL, 16, 128))
    low = grad.astype(BF)
    pieces = [low[:, i * 128 : (i + 1) * 128].reshape(NCOL, 48, 128) for i in range(5)]
    blocks = [(0, pieces[0]), (48, pieces[1]), (96, pieces[2][:, 0:32]), (128, pieces[2][:, 32:48])]
    blocks += [(144, pieces[3]), (192, pieces[4]), (240, misc)]
    place(core, mine_ref, other_ref, blocks, 128)


def project_back(core, first, second, wj, x4):
    kind = pltpu.HBM((NCOL, 128, 128), BF)
    return pl.pallas_call(
        project_back_kernel,
        out_shape=(
            pltpu.HBM((NROW, DIM, TOK), BF),
            kind,
            kind,
            pltpu.HBM((48, NCOL * TOK), BF),
        ),
        in_specs=[SMEM] + [VMEM] * 4,
        out_specs=[VMEM] * 4,
        scratch_shapes=[pltpu.VMEM((512, 256), F32)],
        compiler_params=params("project_back"),
        cost_estimate=cost(5),
        name="project_back",
    )(core, first, second, wj, x4)


def last_kernel(mine_ref, theirs_ref, din_ref, dh1_ref, out_ref):
    out_ref[:, 0:128, :] = (mine_ref[...].astype(F32) + theirs_ref[...].astype(F32)).astype(BF)
    total = dh1_ref[...]
    for r in range(NROW):
        total = total + din_ref[r].astype(F32)
    out_ref[:, 128:176, :] = total.astype(BF).reshape(NCOL, 48, TOK)


def last_payload(mine, theirs, din, dh1):
    return pl.pallas_call(
        last_kernel,
        out_shape=pltpu.HBM((NCOL, 176, 128), BF),
        in_specs=[VMEM] * 4,
        out_specs=VMEM,
        compiler_params=params("last_payload"),
        cost_estimate=cost(1),
        name="last_payload",
    )(mine, theirs, din, dh1)


def join(core_ref, mine, theirs):
    first = core_ref[0] == 0
    a, b = mine[...], theirs[...]
    return jnp.concatenate([jnp.where(first, a, b), jnp.where(first, b, a)], axis=0)


def finish_kernel(
    core_ref, col_ref, wide_ref, other_ref, out_ref, up_ref, up_bias_ref, down_ref, *own_refs
):
    wide = join(core_ref, wide_ref, other_ref)
    for i in range(6):
        lanes = slice(i * 128, (i + 1) * 128)
        up_ref[:, lanes] = wide[48 * i : 48 * (i + 1)]
        down_ref[:, lanes] = wide[288 + 48 * i : 288 + 48 * (i + 1)]
    out_ref[...] = jnp.concatenate([wide[576:624], wide[624:672, 0:64]], axis=1)
    vecs = wide[672:720] + wide[720:768]
    up_bias_ref[...] = vecs[36:42]
    rows = [
        jnp.concatenate([vecs[6 * v + i : 6 * v + i + 1] for i in range(6)], axis=1) for v in range(6)
    ]
    rows = jnp.concatenate(rows + [jnp.zeros((2, DIM), F32)], axis=0)
    feature = lax.broadcasted_iota(jnp.int32, (DIM, 48), 0)
    lane = lax.broadcasted_iota(jnp.int32, (DIM, 48), 1)
    pick = jnp.where(feature == col_ref[0] * 48 + lane, 1.0, 0.0).astype(BF)
    own = sum(dot(part, pick, 1, 0) for part in split3(rows))
    for v, ref in enumerate(own_refs):
        ref[...] = own[v : v + 1]


def finish(core, col, wide, other):
    shapes = [(48, 192), (48, DIM), (6, 128), (48, DIM)] + [(1, 48)] * 6
    return pl.pallas_call(
        finish_kernel,
        out_shape=[pltpu.HBM(shape, F32) for shape in shapes],
        in_specs=[SMEM] * 2 + [VMEM] * 2,
        out_specs=[VMEM] * len(shapes),
        compiler_params=params("finish"),
        cost_estimate=cost(1),
        name="finish",
    )(core, col, wide, other)


def joint_kernel(core_ref, last_ref, other_ref, joint_ref, joint_bias_ref):
    last = join(core_ref, last_ref, other_ref)
    chunks = [last[48 * i : 48 * (i + 1)] for i in range(5)]
    heads = [chunks[0][:, 0:64], chunks[0][:, 64:128], chunks[1][:, 0:64]]
    joint_ref[...] = jnp.concatenate([v for h in range(3) for v in (heads[h], chunks[2 + h])], axis=1)
    sums = last[240:248] + last[248:256]
    heads = [sums[0:1, 0:64], sums[0:1, 64:128], sums[1:2, 0:64]]
    joint_bias_ref[...] = jnp.concatenate(
        [jnp.concatenate([heads[h], sums[2 + h : 3 + h, 64:128]], axis=1) for h in range(3)], axis=0
    )


def joint_gradient(core, last, other):
    return pl.pallas_call(
        joint_kernel,
        out_shape=[pltpu.HBM(shape, F32) for shape in ((48, 576), (3, 128))],
        in_specs=[SMEM] + [VMEM] * 2,
        out_specs=[VMEM] * 2,
        compiler_params=params("joint_gradient"),
        cost_estimate=cost(1),
        name="joint_gradient",
    )(core, last, other)


def exchange(blocks, axis):
    return lax.all_to_all(blocks, axis, 0, 0, tiled=True)


def around(v, axis, shift):
    return lax.ppermute(v, axis, [(i, (i + shift) % 4) for i in range(4)])


def swap_cores(v):
    return lax.ppermute(v, "dp", [(0, 1), (1, 0)])


def per_device(
    inputs,
    segments,
    joint_weight,
    joint_bias,
    output_weight,
    output_bias,
    first_norm_gain,
    shift_first,
    up_weight,
    up_bias,
    down_weight,
    down_bias,
    second_norm_gain,
    second_norm_shift,
    cotangent,
):
    core = lax.axis_index("dp")
    col = lax.axis_index(COL)
    row = lax.axis_index("row")
    my_z, my_y = lax.axis_index("z"), lax.axis_index("y")
    core_word = core.reshape(1).astype(jnp.int32)
    row_word = row.reshape(1).astype(jnp.int32)

    def by_col(a):
        return jnp.transpose(a.reshape(48, NCOL, TOK), (1, 0, 2))

    blocks = by_col(inputs)
    blocks, up_weight, down_weight, output_weight = lax.optimization_barrier(
        (blocks, up_weight, down_weight, output_weight)
    )
    x_t = exchange(blocks, COL)
    vectors = jnp.stack(
        [output_bias, first_norm_gain, shift_first, down_bias, second_norm_gain, second_norm_shift], axis=1
    )
    vectors = jnp.pad(jnp.concatenate(split3(vectors), axis=1), ((0, 0), (0, 46)))
    jw = joint_weight.reshape(48, 3, 3, HDIM)
    jw = jnp.concatenate([jw[:, :, 0].reshape(48, 192), vectors, jw[:, :, 1:].reshape(48, 384)], axis=1)
    jw = jnp.broadcast_to(jw[None], (NCOL, 48, JW))
    x_t, jw = lax.optimization_barrier((x_t, jw))
    wj = exchange(jw, COL)
    x4 = lax.all_gather(x_t.reshape(DIM, TOK), "row", axis=0, tiled=False)

    turned = lax.dynamic_slice_in_dim(output_weight, core * 96, 96, 0).T
    my_bias = lax.dynamic_slice_in_dim(up_bias, (core * NCOL + col) * 24, 24, 0)
    my_bias = jnp.pad(jnp.stack(split3(my_bias)), ((0, 45), (0, 8)))
    turned = jnp.concatenate([turned, my_bias], axis=1).reshape(3, 16, 128)
    turned = jnp.transpose(turned, (1, 0, 2)).reshape(16, 384)
    shard = jnp.concatenate(
        [
            lax.dynamic_slice_in_dim(up_weight, core * 384, 384, 1),
            lax.dynamic_slice_in_dim(down_weight, core * 384, 384, 1),
            turned,
        ],
        axis=0,
    )
    shard = lax.optimization_barrier((shard, x_t))[0]
    everything = lax.all_gather(shard, ("dp", "row", "z", "y"), axis=0, tiled=False)
    everything = everything.reshape(2, NROW, NCOL, 112, 384)
    up_b = jnp.sum(everything[:, :, :, 96:99, 96:120].astype(F32), axis=3)
    up_b = jnp.transpose(up_b, (1, 0, 2, 3)).reshape(NROW, DIM)

    bias3 = joint_bias.reshape(3, 2, HDIM)
    bias = jnp.concatenate(
        [
            bias3[:, 0].reshape(192),
            jnp.zeros((64,), F32),
            jnp.concatenate([jnp.zeros((3, HDIM), F32), bias3[:, 1]], axis=1).reshape(384),
        ]
    ).reshape(1, JW)
    seg = segments.reshape(SLOTS, TOK)
    shift = lax.rem(TOK - lax.rem(col, PER_HEAD) * SHARE, TOK).reshape(1).astype(jnp.int32)

    arrived = exchange(project(x4, wj, bias, by_col(cotangent)), COL)
    qa, o, o_blocks = attend(shift, arrived, seg)

    att = exchange(o_blocks, ALL)
    same, sent, d_blocks, fin, dh1 = tokenwise(row_word, att, x_t, arrived, wj, up_b, everything)

    d_blocks, same, sent = lax.optimization_barrier((d_blocks, same, sent))
    zero = jnp.minimum(row, 0)
    pieces = [
        jnp.concatenate([same, lax.dynamic_index_in_dim(sent, zero + d, 0, keepdims=False)], axis=0)
        for d in range(NROW)
    ]
    grad_o = exchange(d_blocks, ALL)
    got = [around(pieces[d], "row", d) for d in range(1, NROW)]
    grad_o, own_piece = lax.optimization_barrier((grad_o, pieces[0]))
    back_a, doa, turned_qd, acc = attend_back_first(arrived, grad_o, qa, o, fin, seg)
    back_b = attend_back_second(qa, doa, turned_qd, acc, arrived, seg)
    back_a = exchange(back_a, COL)
    back_b, got, own_piece, back_a = lax.optimization_barrier((back_b, got, own_piece, back_a))
    got = [own_piece, *got]
    theirs = [swap_cores(v) for v in got]
    wide = weight_grads(core_word, got, theirs).reshape(4, 4, WROWS // 2, 128)
    back_b, back_a = lax.optimization_barrier((back_b, back_a))
    back_b = exchange(back_b, COL)
    near = [lax.dynamic_index_in_dim(wide, lax.rem(my_z + d, 4), 0, keepdims=False) for d in range(4)]
    near = [near[0]] + [around(near[d], "z", d) for d in range(1, 4)]
    wide = near[0].astype(F32) + near[1].astype(F32) + near[2].astype(F32) + near[3].astype(F32)
    wide = wide.astype(BF)

    din, mine_j, other_j, layer_output = project_back(core_word, back_a, back_b, wj, x4)
    theirs_j = swap_cores(other_j)
    din = exchange(din, "row")
    near = [lax.dynamic_index_in_dim(wide, lax.rem(my_y + d, 4), 0, keepdims=False) for d in range(4)]
    din, near = lax.optimization_barrier((din, near))
    near = [near[0]] + [around(near[d], "y", d) for d in range(1, 4)]
    mixed = exchange(last_payload(mine_j, theirs_j, din, dh1), COL)
    wide = near[0].astype(F32) + near[1].astype(F32) + near[2].astype(F32) + near[3].astype(F32)
    grad_out, grad_up, grad_up_bias, grad_down, *own = finish(
        core_word, col.reshape(1).astype(jnp.int32), wide, swap_cores(wide)
    )
    last = jnp.sum(mixed[:, :128].astype(F32), axis=0)
    grad_inputs = jnp.transpose(mixed[:, 128:].astype(F32), (1, 0, 2)).reshape(48, 2048)
    grad_joint, grad_joint_bias = joint_gradient(core_word, last, swap_cores(last))
    own = [v.reshape(48) for v in own]

    return (
        layer_output,
        grad_inputs,
        grad_joint,
        grad_joint_bias.reshape(384),
        grad_out.T,
        own[5],
        own[0],
        own[1],
        grad_up,
        grad_up_bias.reshape(768),
        grad_down,
        own[4],
        own[2],
        own[3],
    )


def solution(mesh):
    sizes = (mesh.shape["dp"], mesh.shape["row"], 4, 4)
    fine = jax.sharding.Mesh(mesh.devices.reshape(sizes), ("dp", "row", "z", "y"))
    grid = P(COL, ("dp", "row"))
    block = P(COL, "row")
    return jax.shard_map(
        per_device,
        mesh=fine,
        in_specs=(
            grid, P("dp", None), block, P("row"), P("row", COL), P(COL), P(COL), P(COL),
            block, P("row"), block, P(COL), P(COL), P(COL), grid,
        ),
        out_specs=(
            grid, grid, block, P("row"), P("row", COL), P(COL), P(COL), P(COL),
            block, P("row"), block, P(COL), P(COL), P(COL),
        ),
        check_vma=False,
    )
```

```python
import math

import jax
import jax.numpy as jnp
from jax import lax
from jax.experimental import pallas as pl
from jax.experimental.pallas import tpu as pltpu
from jax.sharding import PartitionSpec as P

HDIM = 64
EPS = 1e-06
BLOCK_OUT = -1e30
LOG2E = 1.4426950408889634
BF = jnp.bfloat16
F32 = jnp.float32

DIM = 768
FF = 3072
NCOL = 16
NROW = 4
TOK = 128
PER_HEAD = 5
SHARE = 26
SLOTS = NROW * NCOL
ROWS = SLOTS * SHARE
AUG = 144
JW = 640
HALF = 2
FWD_C = 2
BWD_C = 1
Q_AT = NROW * TOK
C_AT = Q_AT + 64
BLOCK = C_AT + 48
MIB = 2**20
COL = ("z", "y")
ALL = ("row", "z", "y")
VMEM = pl.BlockSpec(memory_space=pltpu.VMEM)
SMEM = pl.BlockSpec(memory_space=pltpu.SMEM)
A_AT = 5 * DIM + 48
SENT = A_AT + 192
SAME = 3 * DIM + 48
WROWS = 768


def split3(v):
    hi = v.astype(BF)
    rest = v - hi.astype(F32)
    mid = rest.astype(BF)
    low = (rest - mid.astype(F32)).astype(BF)
    return hi, mid, low


def dot(a, b, ca, cb):
    return lax.dot_general(a, b, (((ca,), (cb,)), ((), ())), preferred_element_type=F32)


LIMITS = {
    "project": 16,
    "attend": 32,
    "attend_back_first": 63.9,
    "attend_back_second": 63.9,
    "tokenwise": 63.9,
    "weight_grads": 63.9,
    "project_back": 63.9,
    "last_payload": 12,
    "finish": 12,
    "joint_gradient": 8,
}


def params(name):
    return pltpu.CompilerParams(vmem_limit_bytes=int(LIMITS[name] * MIB))


def cost(us):
    return pl.CostEstimate(flops=int(us * 1e9), bytes_accessed=int(us * 2e6), transcendentals=0)


Q_BLOCK = pl.BlockSpec((NCOL, 64, 128), lambda i: (0, Q_AT // 64, 0))


def whole(shape):
    return pl.BlockSpec(shape, lambda i: (0,) * len(shape))


def pack(ref, at, lane, scale=None):
    lanes = slice(lane, lane + HDIM)
    rest = jnp.concatenate([ref[at + 16 : at + SHARE, lanes], jnp.zeros((6, HDIM), F32)], axis=0)
    both = jnp.concatenate([ref[at : at + 16, lanes], rest], axis=1)
    return (both if scale is None else both * scale).astype(BF)


def unpack(block, ref, at, lane, rows=SHARE):
    block = block.astype(F32)
    lanes = slice(lane, lane + HDIM)
    ref[at : at + 16, lanes] = block[:, 0:64]
    ref[at + 16 : at + rows, lanes] = block[0 : rows - 16, 64:128]


def project_kernel(x_ref, w_ref, b_ref, cot_ref, out_ref, q_ref):
    w = w_ref[...].reshape(DIM, JW)
    q_ref[...] = jnp.zeros_like(q_ref)
    for r in range(NROW):
        tokens = x_ref[r].astype(F32).T.astype(BF)
        y = dot(tokens, w, 1, 0) + b_ref[...]
        q_ref[r * TOK : (r + 1) * TOK, :] = y[:, 0:256]
        for h in range(3):
            kv = y[:, 256 + 128 * h : 384 + 128 * h].T.astype(BF)
            for j in range(PER_HEAD * h, PER_HEAD * (h + 1) + (1 if h == 2 else 0)):
                out_ref[j, r * TOK : (r + 1) * TOK, :] = kv
    for j in range(NCOL):
        h, k = min(j, 14) // PER_HEAD, min(j, 14) % PER_HEAD
        for r in range(NROW):
            at = r * TOK + SHARE * k
            out_ref[j, Q_AT + 16 * r : Q_AT + 16 * (r + 1), :] = pack(q_ref, at, HDIM * h)
    out_ref[:, C_AT:BLOCK, :] = cot_ref[...]


def project(x4, wj, bias, cot):
    return pl.pallas_call(
        project_kernel,
        out_shape=pltpu.HBM((NCOL, BLOCK, 128), BF),
        in_specs=[VMEM] * 4,
        out_specs=VMEM,
        scratch_shapes=[pltpu.VMEM((640, 256), F32)],
        compiler_params=params("project"),
        cost_estimate=cost(3),
        name="project",
    )(x4, wj, bias, cot)


def key_rows(seg_row):
    row = lax.broadcasted_iota(jnp.int32, (16, seg_row.shape[1]), 0)
    hot = jnp.where(row < 5, jnp.where(row == seg_row, 1.0, 0.0), jnp.where(row < 8, 1.0, 0.0))
    return hot.astype(BF)


def offset_columns(value, base):
    h, m, l = split3(-value)
    lane = lax.broadcasted_iota(jnp.int32, base.shape, 1)
    return jnp.where(
        lane == 5,
        h.astype(F32),
        jnp.where(lane == 6, m.astype(F32), jnp.where(lane == 7, l.astype(F32), base)),
    )


def key_block(kv_ref, seg_ref, begin):
    pairs = [(c, r) for c in range(kv_ref.shape[0]) for r in range(kv_ref.shape[1] // TOK)]
    tiles = [kv_ref[c, r * TOK : (r + 1) * TOK, :] for c, r in pairs]
    at = pl.program_id(0) * kv_ref.shape[0]
    extra = [key_rows(seg_ref[pl.ds((begin + r) * NCOL + at + c, 1), :]) for c, r in pairs]
    return jnp.concatenate(tiles, axis=1), jnp.concatenate(extra, axis=1)


def forward_step(qa_ref, kv_ref, seg_ref, acc_ref, top_ref):
    kvt, extra = key_block(kv_ref, seg_ref, 0)
    kt = jnp.concatenate([kvt[0:64], kvt[0:64], extra], axis=0)
    turned = kvt.astype(F32).T
    lane = lax.broadcasted_iota(jnp.int32, turned.shape, 1)
    va = jnp.where(lane >= 64, turned, jnp.where(lane == 0, 1.0, 0.0)).astype(BF)
    s = dot(qa_ref[...], kt, 1, 0)
    parts = [s[:, i * 128 : (i + 1) * 128] for i in range(s.shape[1] // 128)]
    high = parts[0]
    for part in parts[1:]:
        high = jnp.maximum(high, part)
    top = top_ref[...]
    raised = jnp.maximum(top, jnp.broadcast_to(jnp.max(high, axis=1, keepdims=True), top.shape))
    p = jnp.concatenate([jnp.exp2(part - raised).astype(BF) for part in parts], axis=1)
    fade = jnp.exp2(top - raised)
    top_ref[...] = raised
    acc_ref[...] = acc_ref[...] * fade + dot(p, va, 1, 0)


def attend_kernel(
    shift_ref, q_ref, kv_ref, seg_ref, qa_ref, o_ref, out_ref, q_scr, pen_scr, acc_ref, top_ref
):
    @pl.when(pl.program_id(0) == 0)
    def _():
        columns = pltpu.roll(seg_ref[...].astype(F32), shift_ref[0], 1).T
        lane = lax.broadcasted_iota(jnp.int32, (SHARE, 16), 1)
        seg = lane.astype(F32)
        for r in range(NROW):
            for c in range(NCOL):
                slot = r * NCOL + c
                unpack(q_ref[c, 16 * r : 16 * (r + 1), :], q_scr, SHARE * slot, 0)
                pen_scr[SHARE * slot : SHARE * (slot + 1), :] = jnp.where(
                    (lane < 5) & (seg != columns[0:SHARE, slot : slot + 1]), BLOCK_OUT, 0.0
                )
        scaled = q_scr[...] * (LOG2E / 8.0)
        hi = scaled.astype(BF)
        lo = (scaled - hi.astype(F32)).astype(BF)
        pen = pen_scr[...]
        qa_ref[...] = jnp.concatenate([hi, lo, pen.astype(BF)], axis=1)
        acc_ref[...] = jnp.zeros_like(acc_ref)
        top_ref[...] = jnp.full_like(top_ref, -3e38)

    forward_step(qa_ref, kv_ref, seg_ref, acc_ref, top_ref)

    @pl.when(pl.program_id(0) == pl.num_programs(0) - 1)
    def _():
        acc = acc_ref[...]
        total = acc[:, 0:1]
        o_ref[...] = acc[:, 64:128] / total
        lse = top_ref[:, 0:1] + jnp.log(total) * LOG2E
        qa_ref[:, 128:144] = offset_columns(lse, qa_ref[:, 128:144].astype(F32)).astype(BF)
        for slot in range(SLOTS):
            out_ref[slot] = pack(o_ref, SHARE * slot, 0)


def attend(shift, arrived, seg):
    return pl.pallas_call(
        attend_kernel,
        grid=(NCOL // FWD_C,),
        out_shape=(
            pltpu.HBM((ROWS, AUG), BF),
            pltpu.HBM((ROWS, HDIM), F32),
            pltpu.HBM((SLOTS, 16, 128), BF),
        ),
        in_specs=[
            SMEM,
            Q_BLOCK,
            pl.BlockSpec((FWD_C, Q_AT, 128), lambda i: (i, 0, 0)),
            whole((SLOTS, TOK)),
        ],
        out_specs=[whole((ROWS, AUG)), whole((ROWS, HDIM)), whole((SLOTS, 16, 128))],
        scratch_shapes=[
            pltpu.VMEM((ROWS, HDIM), F32),
            pltpu.VMEM((ROWS, 16), F32),
            pltpu.VMEM((ROWS, 128), F32),
            pltpu.VMEM((ROWS, 128), F32),
        ],
        compiler_params=params("attend"),
        cost_estimate=cost(20),
        name="attend",
    )(shift, arrived, arrived, seg)


def backward_step(qa_ref, doa_ref, turned_ref, kv_ref, seg_ref, begin, acc_ref):
    kvt, extra = key_block(kv_ref, seg_ref, begin)
    kt = jnp.concatenate([kvt[0:64], kvt[0:64], extra], axis=0)
    vt = jnp.concatenate([kvt[64:128], extra], axis=0)
    keys = kvt.astype(F32).T.astype(BF)
    p = jnp.exp2(dot(qa_ref[...], kt, 1, 0))
    dp = dot(doa_ref[...], vt, 1, 0)
    ds = (p * dp).astype(BF)
    acc_ref[...] += dot(ds, keys, 1, 0)
    dk = dot(turned_ref[0:64, :], ds, 1, 0) * 0.125
    dv = dot(turned_ref[64:128, :], p.astype(BF), 1, 0)
    return jnp.concatenate([dk, dv], axis=0).astype(BF)


def store_keys(out_ref, at, both):
    for c in range(BWD_C):
        for r in range(HALF):
            i = c * HALF + r
            out_ref[at + c, r * TOK : (r + 1) * TOK, :] = both[:, i * TOK : (i + 1) * TOK]


def back_first_kernel(
    q_ref, do_ref, qa_ref, o_ref, fin_ref, kv_ref, seg_ref, out_ref, doa_ref, turned_ref, acc_ref, pair_scr
):
    @pl.when(pl.program_id(0) == 0)
    def _():
        for r in range(NROW):
            for c in range(NCOL):
                slot = r * NCOL + c
                unpack(q_ref[c, 16 * r : 16 * (r + 1), :], pair_scr, SHARE * slot, 0)
                unpack(do_ref[slot], pair_scr, SHARE * slot, HDIM)
        pairs = pair_scr[...]
        turned_ref[...] = pairs.T.astype(BF)
        grad = pairs[:, 64:128]
        delta = jnp.sum(grad * o_ref[...], axis=1, keepdims=True)
        ext = offset_columns(delta, jnp.zeros((ROWS, 16), F32))
        doa_ref[...] = jnp.concatenate([grad.astype(BF), ext.astype(BF)], axis=1)
        acc_ref[...] = jnp.zeros_like(acc_ref)

    both = backward_step(qa_ref, doa_ref, turned_ref, kv_ref, seg_ref, 0, acc_ref)
    store_keys(out_ref, 0, both)
    out_ref[:, 256:304, :] = fin_ref[...]


def back_second_kernel(
    qa_ref, doa_ref, turned_ref, acc_in, kv_ref, seg_ref, out_ref, acc_ref
):
    step = pl.program_id(0)

    @pl.when(step == 0)
    def _():
        acc_ref[...] = acc_in[...]

    both = backward_step(qa_ref, doa_ref, turned_ref, kv_ref, seg_ref, HALF, acc_ref)
    store_keys(out_ref, step * BWD_C, both)

    @pl.when(step == pl.num_programs(0) - 1)
    def _():
        for r in range(NROW):
            for c in range(NCOL):
                block = pack(acc_ref, SHARE * (r * NCOL + c), 0, 0.125)
                out_ref[c, 256 + 16 * r : 272 + 16 * r, :] = block


SEG_BACK = whole((SLOTS, TOK))
BACK_STEPS = NCOL // BWD_C


def attend_back_first(arrived, grad, qa, o, fin, seg):
    return pl.pallas_call(
        back_first_kernel,
        grid=(BACK_STEPS,),
        out_shape=(
            pltpu.HBM((NCOL, 304, 128), BF),
            pltpu.HBM((ROWS, 80), BF),
            pltpu.HBM((128, ROWS), BF),
            pltpu.HBM((ROWS, 128), F32),
        ),
        in_specs=[
            Q_BLOCK,
            whole((SLOTS, 16, 128)),
            whole((ROWS, AUG)),
            whole((ROWS, HDIM)),
            pl.BlockSpec((BWD_C, 48, 128), lambda i: (i, 0, 0)),
            pl.BlockSpec((BWD_C, HALF * TOK, 128), lambda i: (i, 0, 0)),
            SEG_BACK,
        ],
        out_specs=[
            pl.BlockSpec((BWD_C, 304, 128), lambda i: (i, 0, 0)),
            whole((ROWS, 80)),
            whole((128, ROWS)),
            whole((ROWS, 128)),
        ],
        scratch_shapes=[pltpu.VMEM((ROWS, 128), F32)],
        compiler_params=params("attend_back_first"),
        cost_estimate=cost(18),
        name="attend_back_first",
    )(arrived, grad, qa, o, fin, arrived, seg)


def attend_back_second(qa, doa, turned, acc, arrived, seg):
    return pl.pallas_call(
        back_second_kernel,
        grid=(BACK_STEPS,),
        out_shape=pltpu.HBM((NCOL, 320, 128), BF),
        in_specs=[
            whole((ROWS, AUG)),
            whole((ROWS, 80)),
            whole((128, ROWS)),
            whole((ROWS, 128)),
            pl.BlockSpec((BWD_C, HALF * TOK, 128), lambda i: (i, 1, 0)),
            SEG_BACK,
        ],
        out_specs=whole((NCOL, 320, 128)),
        scratch_shapes=[pltpu.VMEM((ROWS, 128), F32)],
        compiler_params=params("attend_back_second"),
        cost_estimate=cost(18),
        name="attend_back_second",
    )(qa, doa, turned, acc, arrived, seg)


def heads_of(block):
    return jnp.concatenate(
        [
            jnp.concatenate([block[64 * h : 64 * (h + 1), 64 * k : 64 * (k + 1)] for h in range(3)], axis=1)
            for k in range(2)
        ],
        axis=0,
    )


def room(k):
    return min(SHARE, TOK - SHARE * k)


def feature_mean(v):
    return jnp.sum(v, axis=1, keepdims=True) * (1.0 / DIM)


def tokenwise_kernel(
    row_ref, att_ref, x_ref, cot_ref, vec_ref, upb_ref, all_ref,
    same_ref, sent_ref, datt_ref, fin_ref, dh1_ref,
    up_ref, down_ref, out_ref, slope_ref, att_scr, back_scr, sems,
):
    row = row_ref[0]
    copies = []
    for g in range(3):
        for k in range(2):
            for r in range(NROW):
                copies.append(
                    pltpu.make_async_copy(
                        all_ref.at[k, r, :, 96:112, g * 128 : (g + 1) * 128],
                        out_ref.at[k * NROW + r, :, 16 * g : 16 * (g + 1), :],
                        sems.at[0],
                    )
                )
    n_out = len(copies)
    for r in range(NROW):
        for k in range(2):
            lanes = slice(r * DIM + k * 384, r * DIM + (k + 1) * 384)
            copies.append(
                pltpu.make_async_copy(all_ref.at[k, r, :, 0:48, :], up_ref.at[:, :, lanes], sems.at[1 + r])
            )
    for r in range(NROW):
        for k in range(2):
            lanes = slice(r * DIM + k * 384, r * DIM + (k + 1) * 384)
            copies.append(
                pltpu.make_async_copy(all_ref.at[k, r, :, 48:96, :], down_ref.at[:, :, lanes], sems.at[5 + r])
            )
    for copy in copies:
        copy.start()

    def wait(group):
        chosen = copies[:n_out] if group == 0 else copies[n_out + 2 * (group - 1) : n_out + 2 * group]
        for copy in chosen:
            copy.wait()

    tok = x_ref[...].reshape(DIM, TOK).astype(F32).T
    cot = cot_ref[...].reshape(DIM, TOK).astype(F32).T
    vecs = vec_ref[...].reshape(DIM, TOK).astype(F32).T[64:128]
    out_b, gain_1, shift_1, down_b, gain_2, shift_2 = [
        vecs[i : i + 1] + vecs[6 + i : 7 + i] + vecs[12 + i : 13 + i] for i in range(6)
    ]
    gap = jnp.zeros((TOK, 32), BF)

    for r in range(NROW):
        for j in range(15):
            h, k = j // PER_HEAD, j % PER_HEAD
            unpack(att_ref[r * NCOL + j], att_scr, SHARE * k, 192 * r + HDIM * h, room(k))
    for r in range(NROW):
        target = lax.rem(r + NROW - row, NROW)
        for h in range(3):
            lanes = slice(192 * r + HDIM * h, 192 * r + HDIM * (h + 1))
            both = jnp.concatenate([att_scr[0:64, lanes], att_scr[64:128, lanes]], axis=1)
            at = A_AT - SAME + 64 * h
            sent_ref[target, at : at + 64, :] = both.astype(BF)
    wait(0)
    attn = jnp.zeros((TOK, DIM), F32)
    for r in range(NROW):
        for k in range(2):
            lanes = slice(192 * r + 96 * k, 192 * r + 96 * (k + 1))
            piece = jnp.concatenate([att_scr[:, lanes].astype(BF), gap], axis=1)
            attn = attn + dot(piece, out_ref[k * NROW + r].reshape(DIM, 128), 1, 1)
    h1 = tok + (attn + out_b)
    off = h1 - feature_mean(h1)
    inv1 = lax.rsqrt(feature_mean(off * off) + EPS)
    xhat1 = off * inv1
    n1 = xhat1 * gain_1 + shift_1
    n1_low = n1.astype(BF)

    branch = jnp.zeros((TOK, DIM), F32)
    for r in range(NROW):
        wait(1 + r)
        cols = slice(r * DIM, (r + 1) * DIM)
        pre = dot(n1_low, up_ref[:, :, cols].reshape(DIM, DIM), 1, 0) + upb_ref[r : r + 1, :]
        phi = 0.5 * (1.0 + lax.erf(pre * (1.0 / math.sqrt(2.0))))
        act = (pre * phi).astype(BF)
        slope_ref[:, cols] = phi + pre * jnp.exp(-0.5 * pre * pre) * (1.0 / math.sqrt(2.0 * math.pi))
        for i in range(6):
            at = DIM + i * TOK
            sent_ref[lax.rem(r + NROW - row, NROW), at : at + TOK, :] = act[:, i * TOK : (i + 1) * TOK]
        wait(5 + r)
        branch = branch + dot(act, down_ref[:, :, cols].reshape(DIM, DIM), 1, 1)
    h2 = n1 + (branch + down_b)
    off = h2 - feature_mean(h2)
    inv2 = lax.rsqrt(feature_mean(off * off) + EPS)
    xhat2 = off * inv2
    fin_ref[...] = (xhat2 * gain_2 + shift_2).T.astype(BF).reshape(NCOL, 48, TOK)
    dx = cot * gain_2
    dh2 = inv2 * (dx - feature_mean(dx) - xhat2 * feature_mean(dx * xhat2))
    d_branch = dh2.astype(BF)

    back = jnp.zeros((TOK, DIM), F32)
    for r in range(NROW):
        cols = slice(r * DIM, (r + 1) * DIM)
        d_act = dot(d_branch, down_ref[:, :, cols].reshape(DIM, DIM), 1, 0)
        d_pre = (d_act * slope_ref[:, cols]).astype(BF)
        for i in range(6):
            at = i * TOK
            sent_ref[lax.rem(r + NROW - row, NROW), at : at + TOK, :] = d_pre[:, i * TOK : (i + 1) * TOK]
        back = back + dot(d_pre, up_ref[:, :, cols].reshape(DIM, DIM), 1, 1)
    up1 = dh2 + back
    dx = up1 * gain_1
    dh1 = inv1 * (dx - feature_mean(dx) - xhat1 * feature_mean(dx * xhat1))
    d_attn = dh1.astype(BF)
    back_scr[TOK : TOK + 8, :] = jnp.zeros((8, 192), F32)
    for r in range(NROW):
        pieces = [dot(d_attn, out_ref[k * NROW + r].reshape(DIM, 128), 1, 0)[:, 0:96] for k in range(2)]
        back_scr[0:TOK, :] = jnp.concatenate(pieces, axis=1)
        for j in range(15):
            h, k = j // PER_HEAD, j % PER_HEAD
            datt_ref[r * NCOL + j] = pack(back_scr, SHARE * k, HDIM * h)
        datt_ref[r * NCOL + 15] = jnp.zeros((16, 128), BF)
    turned = dh1.T
    dh1_ref[...] = turned
    shared = [n1.T.astype(BF), dh2.T.astype(BF), turned.astype(BF)]
    sums = [
        jnp.sum(v, axis=0, keepdims=True) for v in (up1 * xhat1, up1, cot * xhat2, cot)
    ]
    rows = []
    for part in range(2):
        for v in sums:
            hi = v.astype(BF).astype(F32)
            piece = hi if part == 0 else v - hi
            rows += [piece[:, i * 128 : (i + 1) * 128] for i in range(6)]
    shared.append(jnp.concatenate(rows, axis=0).astype(BF))
    at = 0
    for v in shared:
        same_ref[at : at + v.shape[0], :] = v
        at += v.shape[0]


def tokenwise(row, att, x_t, arrived, wj, up_bias, everything):
    return pl.pallas_call(
        tokenwise_kernel,
        out_shape=(
            pltpu.HBM((SAME, TOK), BF),
            pltpu.HBM((NROW, SENT - SAME, TOK), BF),
            pltpu.HBM((SLOTS, 16, 128), BF),
            pltpu.HBM((NCOL, 48, TOK), BF),
            pltpu.HBM((DIM, TOK), F32),
        ),
        grid=(1,),
        in_specs=[
            SMEM,
            whole((SLOTS, 16, 128)),
            whole((NCOL, 48, TOK)),
            pl.BlockSpec((NCOL, 48, TOK), lambda i: (0, C_AT // 48, 0)),
            pl.BlockSpec((NCOL, 48, TOK), lambda i: (0, 0, 1)),
            whole((NROW, DIM)),
            pl.BlockSpec(memory_space=pl.ANY),
        ],
        out_specs=[
            whole((SAME, TOK)),
            whole((NROW, SENT - SAME, TOK)),
            whole((SLOTS, 16, 128)),
            whole((NCOL, 48, TOK)),
            whole((DIM, TOK)),
        ],
        scratch_shapes=[
            pltpu.VMEM((NCOL, 48, FF), BF),
            pltpu.VMEM((NCOL, 48, FF), BF),
            pltpu.VMEM((2 * NROW, NCOL, 48, 128), BF),
            pltpu.VMEM((TOK, FF), F32),
            pltpu.VMEM((TOK, DIM), F32),
            pltpu.VMEM((TOK + 8, 192), F32),
            pltpu.SemaphoreType.DMA((9,)),
        ],
        compiler_params=params("tokenwise"),
        cost_estimate=cost(15),
        name="tokenwise",
    )(row, att, x_t, arrived, wj, up_bias, everything)


def weight_grads_kernel(core_ref, *refs):
    got, out_ref = refs[:-1], refs[-1]

    def feats(at):
        return jnp.concatenate([ref[at : at + DIM, :] for ref in got], axis=1)

    def hidden(at, begin, end):
        return jnp.concatenate(
            [
                jnp.concatenate(
                    [ref[at + i * TOK : at + (i + 1) * TOK, :] for i in range(begin, end)], axis=1
                )
                for ref in got
            ],
            axis=0,
        )

    def keep(at, g):
        for i in range(g.shape[1] // 128):
            piece = g[:, i * 128 : (i + 1) * 128].astype(BF).reshape(NCOL, 48, 128)
            out_ref[:, at + 48 * i : at + 48 * (i + 1), :] = piece

    @pl.when(core_ref[0] == 0)
    def _():
        keep(0, dot(feats(0), hidden(3 * DIM + 48, 0, 6), 1, 0))
        keep(288, dot(feats(DIM), hidden(4 * DIM + 48, 0, 2), 1, 0))

    @pl.when(core_ref[0] != 0)
    def _():
        d_branch = feats(DIM)
        d_attn = feats(2 * DIM)
        keep(0, dot(d_branch, hidden(4 * DIM + 48, 2, 6), 1, 0))
        att = [heads_of(ref[A_AT:SENT, :].astype(F32)).astype(BF) for ref in got]
        att = jnp.concatenate(att, axis=0)
        att = jnp.concatenate([att, jnp.zeros((att.shape[0], 64), BF)], axis=1)
        keep(192, dot(d_attn, att, 1, 0))
        d_pre = hidden(3 * DIM + 48, 0, 6)
        ones = jnp.ones((16, d_pre.shape[0]), BF)
        sums = [dot(ones, d_branch, 1, 1)[0:1], dot(ones, d_attn, 1, 1)[0:1], dot(ones, d_pre, 1, 0)[0:1]]
        norm = got[0][3 * DIM : 3 * DIM + 48, :].astype(F32)
        for ref in got[1:]:
            norm = norm + ref[3 * DIM : 3 * DIM + 48, :].astype(F32)
        rows = [norm[0:24] + norm[24:48]]
        for v in sums:
            rows += [v[:, i * 128 : (i + 1) * 128] for i in range(6)]
        rows.append(jnp.zeros((6, 128), F32))
        rows = jnp.concatenate(rows, axis=0)
        hi = rows.astype(BF)
        lo = (rows - hi.astype(F32)).astype(BF)
        misc = jnp.concatenate([hi, lo], axis=0)
        out_ref[:, 288:384, :] = jnp.broadcast_to(misc[None], (NCOL, 96, 128))


def weight_grads(core, got, theirs):
    shape = (NCOL, WROWS // 2, 128)
    return pl.pallas_call(
        weight_grads_kernel,
        grid=(1,),
        out_shape=pltpu.HBM(shape, BF),
        in_specs=[SMEM] + [whole((SENT, TOK))] * 8,
        out_specs=whole(shape),
        compiler_params=params("weight_grads"),
        cost_estimate=cost(1),
        name="weight_grads",
    )(core, *got, *theirs)


def place(core, mine_ref, other_ref, blocks, half_rows):
    for at, block in blocks:
        low = at < half_rows
        local = at if low else at - half_rows
        rows = slice(local, local + block.shape[1])
        keep = core == (0 if low else 1)

        @pl.when(keep)
        def _():
            mine_ref[:, rows, :] = block

        @pl.when(jnp.logical_not(keep))
        def _():
            other_ref[:, rows, :] = block


def project_back_kernel(
    core_ref, first_ref, second_ref, w_ref, x_ref, din_ref, mine_ref, other_ref, layer_ref, scr
):
    core = core_ref[0]
    layer_ref[...] = jnp.concatenate([first_ref[c, 256:304, :] for c in range(NCOL)], axis=1)
    scr[...] = jnp.zeros_like(scr)
    for j in range(15):
        h, k = j // PER_HEAD, j % PER_HEAD
        for r in range(NROW):
            block = second_ref[j, 256 + 16 * r : 272 + 16 * r, :]
            unpack(block, scr, r * TOK + SHARE * k, HDIM * h, room(k))
    dq = scr[...].T.astype(BF)
    w = w_ref[...].reshape(DIM, JW)
    grad = jnp.zeros((DIM, JW), F32)
    total = jnp.zeros((16, JW), F32)
    ones = jnp.ones((16, TOK), BF)
    for r in range(NROW):
        source, at = (first_ref, r) if r < HALF else (second_ref, r - HALF)
        parts = [dq[:, r * TOK : (r + 1) * TOK]]
        for h in range(3):
            acc = source[PER_HEAD * h, at * TOK : (at + 1) * TOK, :].astype(F32)
            for k in range(1, PER_HEAD):
                acc = acc + source[PER_HEAD * h + k, at * TOK : (at + 1) * TOK, :].astype(F32)
            parts.append(acc.astype(BF))
        d_proj = jnp.concatenate(parts, axis=0)
        din_ref[r] = dot(w, d_proj, 1, 0).astype(BF)
        grad = grad + dot(x_ref[r], d_proj, 1, 1)
        total = total + dot(ones, d_proj, 1, 1)
    rows = [total[0:1, i * 128 : (i + 1) * 128] for i in range(5)] + [jnp.zeros((3, 128), F32)]
    rows = jnp.concatenate(rows, axis=0)
    hi = rows.astype(BF)
    lo = (rows - hi.astype(F32)).astype(BF)
    misc = jnp.broadcast_to(jnp.concatenate([hi, lo], axis=0)[None], (NCOL, 16, 128))
    low = grad.astype(BF)
    pieces = [low[:, i * 128 : (i + 1) * 128].reshape(NCOL, 48, 128) for i in range(5)]
    blocks = [(0, pieces[0]), (48, pieces[1]), (96, pieces[2][:, 0:32]), (128, pieces[2][:, 32:48])]
    blocks += [(144, pieces[3]), (192, pieces[4]), (240, misc)]
    place(core, mine_ref, other_ref, blocks, 128)


def project_back(core, first, second, wj, x4):
    kind = pltpu.HBM((NCOL, 128, 128), BF)
    return pl.pallas_call(
        project_back_kernel,
        out_shape=(
            pltpu.HBM((NROW, DIM, TOK), BF),
            kind,
            kind,
            pltpu.HBM((48, NCOL * TOK), BF),
        ),
        in_specs=[SMEM] + [VMEM] * 4,
        out_specs=[VMEM] * 4,
        scratch_shapes=[pltpu.VMEM((512, 256), F32)],
        compiler_params=params("project_back"),
        cost_estimate=cost(5),
        name="project_back",
    )(core, first, second, wj, x4)


def last_kernel(mine_ref, theirs_ref, din_ref, dh1_ref, out_ref):
    out_ref[:, 0:128, :] = (mine_ref[...].astype(F32) + theirs_ref[...].astype(F32)).astype(BF)
    total = dh1_ref[...]
    for r in range(NROW):
        total = total + din_ref[r].astype(F32)
    out_ref[:, 128:176, :] = total.astype(BF).reshape(NCOL, 48, TOK)


def last_payload(mine, theirs, din, dh1):
    return pl.pallas_call(
        last_kernel,
        out_shape=pltpu.HBM((NCOL, 176, 128), BF),
        in_specs=[VMEM] * 4,
        out_specs=VMEM,
        compiler_params=params("last_payload"),
        cost_estimate=cost(1),
        name="last_payload",
    )(mine, theirs, din, dh1)


def join(core_ref, mine, theirs):
    first = core_ref[0] == 0
    a, b = mine[...], theirs[...]
    return jnp.concatenate([jnp.where(first, a, b), jnp.where(first, b, a)], axis=0)


def finish_kernel(
    core_ref, col_ref, wide_ref, other_ref, out_ref, up_ref, up_bias_ref, down_ref, *own_refs
):
    wide = join(core_ref, wide_ref, other_ref)
    for i in range(6):
        lanes = slice(i * 128, (i + 1) * 128)
        up_ref[:, lanes] = wide[48 * i : 48 * (i + 1)]
        down_ref[:, lanes] = wide[288 + 48 * i : 288 + 48 * (i + 1)]
    out_ref[...] = jnp.concatenate([wide[576:624], wide[624:672, 0:64]], axis=1)
    vecs = wide[672:720] + wide[720:768]
    up_bias_ref[...] = vecs[36:42]
    rows = [
        jnp.concatenate([vecs[6 * v + i : 6 * v + i + 1] for i in range(6)], axis=1) for v in range(6)
    ]
    rows = jnp.concatenate(rows + [jnp.zeros((2, DIM), F32)], axis=0)
    feature = lax.broadcasted_iota(jnp.int32, (DIM, 48), 0)
    lane = lax.broadcasted_iota(jnp.int32, (DIM, 48), 1)
    pick = jnp.where(feature == col_ref[0] * 48 + lane, 1.0, 0.0).astype(BF)
    own = sum(dot(part, pick, 1, 0) for part in split3(rows))
    for v, ref in enumerate(own_refs):
        ref[...] = own[v : v + 1]


def finish(core, col, wide, other):
    shapes = [(48, 192), (48, DIM), (6, 128), (48, DIM)] + [(1, 48)] * 6
    return pl.pallas_call(
        finish_kernel,
        out_shape=[pltpu.HBM(shape, F32) for shape in shapes],
        in_specs=[SMEM] * 2 + [VMEM] * 2,
        out_specs=[VMEM] * len(shapes),
        compiler_params=params("finish"),
        cost_estimate=cost(1),
        name="finish",
    )(core, col, wide, other)


def joint_kernel(core_ref, last_ref, other_ref, joint_ref, joint_bias_ref):
    last = join(core_ref, last_ref, other_ref)
    chunks = [last[48 * i : 48 * (i + 1)] for i in range(5)]
    heads = [chunks[0][:, 0:64], chunks[0][:, 64:128], chunks[1][:, 0:64]]
    joint_ref[...] = jnp.concatenate([v for h in range(3) for v in (heads[h], chunks[2 + h])], axis=1)
    sums = last[240:248] + last[248:256]
    heads = [sums[0:1, 0:64], sums[0:1, 64:128], sums[1:2, 0:64]]
    joint_bias_ref[...] = jnp.concatenate(
        [jnp.concatenate([heads[h], sums[2 + h : 3 + h, 64:128]], axis=1) for h in range(3)], axis=0
    )


def joint_gradient(core, last, other):
    return pl.pallas_call(
        joint_kernel,
        out_shape=[pltpu.HBM(shape, F32) for shape in ((48, 576), (3, 128))],
        in_specs=[SMEM] + [VMEM] * 2,
        out_specs=[VMEM] * 2,
        compiler_params=params("joint_gradient"),
        cost_estimate=cost(1),
        name="joint_gradient",
    )(core, last, other)


def exchange(blocks, axis):
    return lax.all_to_all(blocks, axis, 0, 0, tiled=True)


def around(v, axis, shift):
    return lax.ppermute(v, axis, [(i, (i + shift) % 4) for i in range(4)])


def swap_cores(v):
    return lax.ppermute(v, "dp", [(0, 1), (1, 0)])


def per_device(
    inputs,
    segments,
    joint_weight,
    joint_bias,
    output_weight,
    output_bias,
    first_norm_gain,
    shift_first,
    up_weight,
    up_bias,
    down_weight,
    down_bias,
    second_norm_gain,
    second_norm_shift,
    cotangent,
):
    core = lax.axis_index("dp")
    col = lax.axis_index(COL)
    row = lax.axis_index("row")
    my_z, my_y = lax.axis_index("z"), lax.axis_index("y")
    core_word = core.reshape(1).astype(jnp.int32)
    row_word = row.reshape(1).astype(jnp.int32)

    def by_col(a):
        return jnp.transpose(a.reshape(48, NCOL, TOK), (1, 0, 2))

    blocks = by_col(inputs)
    blocks, up_weight, down_weight, output_weight = lax.optimization_barrier(
        (blocks, up_weight, down_weight, output_weight)
    )
    x_t = exchange(blocks, COL)
    vectors = jnp.stack(
        [output_bias, first_norm_gain, shift_first, down_bias, second_norm_gain, second_norm_shift], axis=1
    )
    vectors = jnp.pad(jnp.concatenate(split3(vectors), axis=1), ((0, 0), (0, 46)))
    jw = joint_weight.reshape(48, 3, 3, HDIM)
    jw = jnp.concatenate([jw[:, :, 0].reshape(48, 192), vectors, jw[:, :, 1:].reshape(48, 384)], axis=1)
    jw = jnp.broadcast_to(jw[None], (NCOL, 48, JW))
    x_t, jw = lax.optimization_barrier((x_t, jw))
    wj = exchange(jw, COL)
    x4 = lax.all_gather(x_t.reshape(DIM, TOK), "row", axis=0, tiled=False)

    turned = lax.dynamic_slice_in_dim(output_weight, core * 96, 96, 0).T
    my_bias = lax.dynamic_slice_in_dim(up_bias, (core * NCOL + col) * 24, 24, 0)
    my_bias = jnp.pad(jnp.stack(split3(my_bias)), ((0, 45), (0, 8)))
    turned = jnp.concatenate([turned, my_bias], axis=1).reshape(3, 16, 128)
    turned = jnp.transpose(turned, (1, 0, 2)).reshape(16, 384)
    shard = jnp.concatenate(
        [
            lax.dynamic_slice_in_dim(up_weight, core * 384, 384, 1),
            lax.dynamic_slice_in_dim(down_weight, core * 384, 384, 1),
            turned,
        ],
        axis=0,
    )
    shard = lax.optimization_barrier((shard, x_t))[0]
    everything = lax.all_gather(shard, ("dp", "row", "z", "y"), axis=0, tiled=False)
    everything = everything.reshape(2, NROW, NCOL, 112, 384)
    up_b = jnp.sum(everything[:, :, :, 96:99, 96:120].astype(F32), axis=3)
    up_b = jnp.transpose(up_b, (1, 0, 2, 3)).reshape(NROW, DIM)

    bias3 = joint_bias.reshape(3, 2, HDIM)
    bias = jnp.concatenate(
        [
            bias3[:, 0].reshape(192),
            jnp.zeros((64,), F32),
            jnp.concatenate([jnp.zeros((3, HDIM), F32), bias3[:, 1]], axis=1).reshape(384),
        ]
    ).reshape(1, JW)
    seg = segments.reshape(SLOTS, TOK)
    shift = lax.rem(TOK - lax.rem(col, PER_HEAD) * SHARE, TOK).reshape(1).astype(jnp.int32)

    arrived = exchange(project(x4, wj, bias, by_col(cotangent)), COL)
    qa, o, o_blocks = attend(shift, arrived, seg)

    att = exchange(o_blocks, ALL)
    same, sent, d_blocks, fin, dh1 = tokenwise(row_word, att, x_t, arrived, wj, up_b, everything)

    d_blocks, same, sent = lax.optimization_barrier((d_blocks, same, sent))
    zero = jnp.minimum(row, 0)
    pieces = [
        jnp.concatenate([same, lax.dynamic_index_in_dim(sent, zero + d, 0, keepdims=False)], axis=0)
        for d in range(NROW)
    ]
    grad_o = exchange(d_blocks, ALL)
    got = [around(pieces[d], "row", d) for d in range(1, NROW)]
    grad_o, own_piece = lax.optimization_barrier((grad_o, pieces[0]))
    back_a, doa, turned_qd, acc = attend_back_first(arrived, grad_o, qa, o, fin, seg)
    back_b = attend_back_second(qa, doa, turned_qd, acc, arrived, seg)
    back_a = exchange(back_a, COL)
    back_b, got, own_piece, back_a = lax.optimization_barrier((back_b, got, own_piece, back_a))
    got = [own_piece, *got]
    theirs = [swap_cores(v) for v in got]
    wide = weight_grads(core_word, got, theirs).reshape(4, 4, WROWS // 2, 128)
    back_b, back_a = lax.optimization_barrier((back_b, back_a))
    back_b = exchange(back_b, COL)
    near = [lax.dynamic_index_in_dim(wide, lax.rem(my_z + d, 4), 0, keepdims=False) for d in range(4)]
    near = [near[0]] + [around(near[d], "z", d) for d in range(1, 4)]
    wide = near[0].astype(F32) + near[1].astype(F32) + near[2].astype(F32) + near[3].astype(F32)
    wide = wide.astype(BF)

    din, mine_j, other_j, layer_output = project_back(core_word, back_a, back_b, wj, x4)
    theirs_j = swap_cores(other_j)
    din = exchange(din, "row")
    near = [lax.dynamic_index_in_dim(wide, lax.rem(my_y + d, 4), 0, keepdims=False) for d in range(4)]
    din, near = lax.optimization_barrier((din, near))
    near = [near[0]] + [around(near[d], "y", d) for d in range(1, 4)]
    mixed = exchange(last_payload(mine_j, theirs_j, din, dh1), COL)
    wide = near[0].astype(F32) + near[1].astype(F32) + near[2].astype(F32) + near[3].astype(F32)
    grad_out, grad_up, grad_up_bias, grad_down, *own = finish(
        core_word, col.reshape(1).astype(jnp.int32), wide, swap_cores(wide)
    )
    last = jnp.sum(mixed[:, :128].astype(F32), axis=0)
    grad_inputs = jnp.transpose(mixed[:, 128:].astype(F32), (1, 0, 2)).reshape(48, 2048)
    grad_joint, grad_joint_bias = joint_gradient(core_word, last, swap_cores(last))
    own = [v.reshape(48) for v in own]

    return (
        layer_output,
        grad_inputs,
        grad_joint,
        grad_joint_bias.reshape(384),
        grad_out.T,
        own[5],
        own[0],
        own[1],
        grad_up,
        grad_up_bias.reshape(768),
        grad_down,
        own[4],
        own[2],
        own[3],
    )


def solution(mesh):
    sizes = (mesh.shape["dp"], mesh.shape["row"], 4, 4)
    fine = jax.sharding.Mesh(mesh.devices.reshape(sizes), ("dp", "row", "z", "y"))
    grid = P(COL, ("dp", "row"))
    block = P(COL, "row")
    return jax.shard_map(
        per_device,
        mesh=fine,
        in_specs=(
            grid, P("dp", None), block, P("row"), P("row", COL), P(COL), P(COL), P(COL),
            block, P("row"), block, P(COL), P(COL), P(COL), grid,
        ),
        out_specs=(
            grid, grid, block, P("row"), P("row", COL), P(COL), P(COL), P(COL),
            block, P("row"), block, P(COL), P(COL), P(COL),
        ),
        check_vma=False,
    )
```
